32 devices in a mesh: section: 2 (over core), rows: 16 (over z, y, x).
Axes of the slice: x: 2, y: 2, z: 4, core: 2. Of those that a mesh axis runs over, the one named last changes fastest.
Arguments:
- byte_ids: int32 [32, 1024], P('rows'), may hold values from 0 to 259
- hash_ids: int32 [32, 1024, 3], P('rows'), may hold values from 0 to 131071, as said below
- patch_lengths: int32 [32, 256], P('rows'), may hold values from 1 to 16, 1024 in all within a row
- row_lengths: int32 [32], P('rows'), may hold values from 128 to 256
- byte_table: bfloat16 [260, 1024], P(None, 'section'), may hold values from -3 to 3
- hash_tables: bfloat16 [3, 131072, 1024], P(None, 'rows', 'section'), may hold values from -3 to 3
- norm_gains: bfloat16 [2, 2, 1024], P('section'), may hold values from 0.5 to 1.5
- w_qkv: bfloat16 [2, 1024, 3072], P('section'), may hold values from -0.1875 to 0.1875
- w_out: bfloat16 [2, 1024, 1024], P('section'), may hold values from -0.75 to 0.75
- w_gate_up: bfloat16 [2, 1024, 5632], P('section'), may hold values from -0.1875 to 0.1875
- w_down: bfloat16 [2, 2816, 1024], P('section'), may hold values from -0.109375 to 0.109375
- cotangent: bfloat16 [2, 32, 256, 1024], P('section', 'rows'), may hold values from -6 to 6
Outputs:
- section_out: bfloat16 [2, 32, 256, 1024], P('section', 'rows')
- byte_table_grad: float32 [260, 1024], P(None, 'section')
- hash_grad: float32 [3, 131072, 1024], P(None, 'rows', 'section')
- gains_grad: float32 [2, 2, 1024], P('section', None, 'rows')
- qkv_grad: float32 [2, 1024, 3072], P('section', 'rows')
- out_grad: float32 [2, 1024, 1024], P('section', 'rows')
- gate_up_grad: float32 [2, 1024, 5632], P('section', 'rows')
- down_grad: float32 [2, 2816, 1024], P('section', None, 'rows')
The draws below stay inside these ranges and needn't reach their ends.
Inputs may be any that keep to these rules, and one draw needn't show every extreme that they name: `hash_ids`: within the 2 sequences of one index of rows, the ids of each table fall in every run of 8192 rows starting at a multiple of 8192 exactly 128 times. `patch_lengths`: each sequence's patch lengths sum to 1024.
All inputs are finite; a program needn't handle non-finite values.
Results may differ from the reference program's by a relative error of at most 0.035.
Values may be sent and summed in bfloat16 or wider, within the bound.
A program may use at most 640 MiB of HBM per device.

```python
import math
import jax
import jax.numpy as jnp
import numpy as np
from jax import lax

D = 1024
HEADS = 16
HEAD = 64
FF = 2816
VOCAB = 260
NGRAMS = 3
HASH_DEV = 8192
L = 1024
MOST = 16
M = 2
P_SIZE = 256
SEQS = 32
HASH_ROWS = 131072


def draw_hash_ids(key, part):
    positions = M * L
    devices = HASH_ROWS // HASH_DEV
    owner_keys = jax.random.split(jax.random.fold_in(key, 11), devices * NGRAMS)
    owner_base = jnp.arange(positions, dtype=jnp.int32) % devices
    owners = jax.vmap(lambda single: jax.random.permutation(single, owner_base))(owner_keys)
    offsets = jax.random.randint(jax.random.fold_in(key, 12), (devices * NGRAMS, positions), 0, HASH_DEV, dtype=jnp.int32)
    first_top = jnp.argmax(owners == devices - 1, axis=1)
    first_low = jnp.argmax(owners == 0, axis=1)
    line_index = jnp.arange(devices * NGRAMS)
    offsets = offsets.at[line_index, first_top].set(HASH_DEV - 1)
    offsets = offsets.at[line_index, first_low].set(0)
    table_ids = (owners * HASH_DEV + offsets).astype(jnp.int32)
    table_ids = table_ids.reshape(devices, NGRAMS, positions).transpose(0, 2, 1)
    return table_ids.reshape(devices * M, L, NGRAMS)


def plant(result, key, least, top_value):
    longest = result.shape.index(max(result.shape))
    spots = []
    for shift in (0, 1):
        where = [jax.random.randint(jax.random.fold_in(key, axis), (), 0, length) for axis, length in enumerate(result.shape)]
        where[longest] = (where[longest] + shift) % result.shape[longest]
        spots.append(tuple(where))
    return result.at[spots[0]].set(least).at[spots[1]].set(top_value)


def levels(stream_key, extent, cuts, least, high):
    level, own = 1.0, jax.random.fold_in(stream_key, 6)
    for position, parts in cuts:
        steps = jnp.exp(jax.random.uniform(jax.random.fold_in(own, position), (parts,), jnp.float32, least / len(cuts), high / len(cuts)))
        level = level * jnp.repeat(steps, extent[position] // parts).reshape([-1 if axis == position else 1 for axis in range(len(extent))])
    return level


def length_profile(amount, total, reach, skew):
    portions = [(1 << 20) // math.isqrt(grade ** skew) + 1 for grade in range(2, amount + 1)]
    surplus, counts = total - reach - (amount - 1), [1] * (amount - 1)
    while surplus > 0:
        free = [i for i in range(amount - 1) if counts[i] < reach]
        mass, budget = sum([portions[i] for i in free]), surplus
        for i in free:
            addition = min(reach - counts[i], max(1, budget * portions[i] // mass), surplus)
            counts[i] = counts[i] + addition
            surplus = surplus - addition
    return np.array([reach] + counts)


def ragged(own_key, count, total, bound, slope):
    if count == 2:
        one = jax.random.randint(own_key, (), max(1, total - bound), min(bound, total - 1) + 1)
        return jnp.stack([one, total - one])
    sizes = jnp.asarray(length_profile(count, total, bound, slope), jnp.int32)
    couples = (count - 1) // 2
    source_of, taker = sizes[1:1 + 2 * couples:2], sizes[2:2 + 2 * couples:2]
    room = jnp.minimum(source_of - 1, bound - taker)
    moved = jax.random.randint(jax.random.fold_in(own_key, 1), (couples,), 0, 1 << 20) % (room + 1)
    sizes = sizes.at[1:1 + 2 * couples:2].set(source_of - moved).at[2:2 + 2 * couples:2].set(taker + moved)
    return sizes[jax.random.permutation(jax.random.fold_in(own_key, 2), count)]


def normal_values(key, dims, scale, bound, shards=(), kind=jnp.bfloat16):
    array = scale * jax.random.normal(key, dims, jnp.float32)
    if shards:
        array = array * levels(key, dims, shards, -0.22, 0.18)
    return jnp.clip(array, -bound, bound).astype(kind)


def setup_inputs(seed: int = 0) -> dict:
    key_of = jax.random.split(jax.random.key(seed), 13)
    byte_ids = plant(jax.random.randint(key_of[0], (SEQS, L), 0, VOCAB), jax.random.fold_in(key_of[0], 1), 0, VOCAB - 1).astype(jnp.int32)
    hash_ids = draw_hash_ids(jax.random.fold_in(key_of[12], 71), 0)
    patch_lengths = jax.vmap(lambda own: ragged(own, P_SIZE, L, MOST, 1))(jax.random.split(key_of[2], SEQS)).reshape((SEQS, P_SIZE)).astype(jnp.int32)
    row_lengths = plant(jax.random.randint(key_of[3], (SEQS,), P_SIZE // 2, P_SIZE + 1), jax.random.fold_in(key_of[3], 1), P_SIZE // 2, P_SIZE).astype(jnp.int32)
    byte_table = normal_values(key_of[4], (VOCAB, D), 0.5, 3.0, ((1, 2),))
    hash_tables = normal_values(key_of[5], (NGRAMS, HASH_ROWS, D), 0.5, 3.0, ((1, 16), (2, 2)))
    norm_gains = jnp.clip(1.0 + 0.1 * jax.random.normal(key_of[6], (2, 2, D), jnp.float32), 0.5, 1.5).astype(jnp.bfloat16)
    w_qkv = normal_values(key_of[7], (2, D, 3 * D), D ** -0.5, 0.1875, ((0, 2),))
    w_out = normal_values(key_of[8], (2, D, D), HEAD ** -0.5, 0.75, ((0, 2),))
    w_gate_up = normal_values(key_of[9], (2, D, 2 * FF), D ** -0.5, 0.1875, ((0, 2),))
    w_down = normal_values(key_of[10], (2, FF, D), FF ** -0.5, 0.109375, ((0, 2),))
    cotangent = normal_values(key_of[11], (2, SEQS, P_SIZE, D), 1.0, 6.0, ((0, 2), (1, 16)))
    return dict(byte_ids=byte_ids, hash_ids=hash_ids, patch_lengths=patch_lengths, row_lengths=row_lengths, byte_table=byte_table, hash_tables=hash_tables, norm_gains=norm_gains, w_qkv=w_qkv, w_out=w_out, w_gate_up=w_gate_up, w_down=w_down, cotangent=cotangent)


epsilon = 1e-05
highest = lax.Precision.HIGHEST

@jax.custom_vjp
def low(v):
    return lax.optimization_barrier(v.astype(jnp.bfloat16)).astype(jnp.float32)

@jax.custom_vjp
def low_back(v):
    return v

def low_keep(v):
    return (low(v), None)

def low_pass(kept, grad):
    return (grad,)

def back_keep(v):
    return (v, None)

def back_low(kept, grad):
    return (low(grad),)
low.defvjp(low_keep, low_pass)
low_back.defvjp(back_keep, back_low)

def product(left_side, right_side):
    return jnp.dot(left_side, right_side, precision=highest, preferred_element_type=jnp.float32)

def rms_scale(inputs, norm_gain):
    return inputs * lax.rsqrt(lax.optimization_barrier(jnp.mean(inputs * inputs, axis=-1, keepdims=True)) + epsilon) * norm_gain

def softmax_rows(scores):
    shifted = jnp.exp(scores - lax.optimization_barrier(jnp.max(scores, axis=-1, keepdims=True)))
    return shifted / lax.optimization_barrier(jnp.sum(shifted, axis=-1, keepdims=True))

def slot_layout(lengths):
    starts = (jnp.cumsum(lengths) - lengths).astype(jnp.int32)
    offsets = jnp.arange(MOST, dtype=jnp.int32)
    slot_index = jnp.minimum(starts[:, None] + offsets[None, :], L - 1).astype(jnp.int32)
    members = offsets[None, :] < lengths[:, None]
    return (slot_index, members)

def feed_forward(hidden_in, norm_gain, w_gate_up, w_down):
    normed = low(rms_scale(hidden_in, norm_gain))
    joined = low_back(product(normed, w_gate_up))
    inner_rows = low(jax.nn.silu(joined[:, :FF]) * joined[:, FF:])
    return hidden_in + low_back(product(inner_rows, w_down))

def encoder_block(layer_weights, byte_rows, lengths, patch_valid):
    norm_gains, w_qkv, w_out, w_gate_up, w_down = layer_weights
    slot_index, members = slot_layout(lengths)
    slot_rows = byte_rows[slot_index]
    pooled = lax.optimization_barrier(jnp.sum(jnp.where(members[:, :, None], slot_rows, 0.0), axis=1)) / lengths[:, None].astype(jnp.float32)
    normed = low(rms_scale(pooled, norm_gains[0]))
    queries = low_back(low(product(normed, w_qkv[:, :D]))).reshape(P_SIZE, HEADS, HEAD)
    pairs = low_back(low(product(byte_rows, w_qkv[:, D:])))
    pair_slots = pairs[slot_index].reshape(P_SIZE, MOST, 2, HEADS, HEAD)
    scores = low_back(jnp.einsum('phd,pkhd->phk', queries, pair_slots[:, :, 0], precision=highest) * 0.125)
    scores = jnp.where(members[:, None, :], scores, -jnp.inf)
    attention = low(softmax_rows(scores))
    attended = jnp.einsum('phk,pkhd->phd', attention, pair_slots[:, :, 1], precision=highest).reshape(P_SIZE, D)
    attended = low_back(low(attended))
    middle = pooled + low_back(product(attended, w_out))
    return jnp.where(patch_valid[:, None], feed_forward(middle, norm_gains[1], w_gate_up, w_down), pooled)

def global_block(layer_weights, inputs, patch_valid):
    norm_gains, w_qkv, w_out, w_gate_up, w_down = layer_weights
    normed = low(rms_scale(inputs, norm_gains[0]))
    mixed_rows = low_back(low(product(normed, w_qkv))).reshape(P_SIZE, 3, HEADS, HEAD)
    scores = low_back(jnp.einsum('qhd,khd->hqk', mixed_rows[:, 0], mixed_rows[:, 1], precision=highest) * 0.125)
    positions = jnp.arange(P_SIZE, dtype=jnp.int32)
    causal = positions[:, None] >= positions[None, :]
    scores = jnp.where(causal[None], scores, -jnp.inf)
    attention = low(softmax_rows(scores))
    attended = jnp.einsum('hqk,khd->qhd', attention, mixed_rows[:, 2], precision=highest).reshape(P_SIZE, D)
    attended = low_back(low(attended))
    middle = inputs + low_back(product(attended, w_out))
    return jnp.where(patch_valid[:, None], feed_forward(middle, norm_gains[1], w_gate_up, w_down), inputs)

def reference(byte_ids, hash_ids, patch_lengths, row_lengths, byte_table, hash_tables, norm_gains, w_qkv, w_out, w_gate_up, w_down, cotangent):
    params = tuple((weight_array.astype(jnp.float32) for weight_array in (byte_table, hash_tables, norm_gains, w_qkv, w_out, w_gate_up, w_down)))

    def forward(table_bytes, table_hash, gains_all, qkv_all, out_all, gate_up_all, down_all):
        summed = table_bytes[byte_ids]
        for table_index in range(NGRAMS):
            summed = summed + table_hash[table_index][hash_ids[:, :, table_index]]
        byte_rows = low_back(low(summed))
        first_layer = (gains_all[0], qkv_all[0], out_all[0], gate_up_all[0], down_all[0])
        second_layer = (gains_all[1], qkv_all[1], out_all[1], gate_up_all[1], down_all[1])

        def one_sequence(sequence_items):
            rows_in, lengths, row_length = sequence_items
            patch_valid = jnp.arange(P_SIZE, dtype=jnp.int32) < row_length
            encoded = low(encoder_block(first_layer, rows_in, lengths, patch_valid))
            final_rows = global_block(second_layer, low_back(encoded), patch_valid)
            return (encoded, final_rows)
        encoded, final_rows = lax.map(jax.checkpoint(one_sequence), (byte_rows, patch_lengths, row_lengths))
        return jnp.stack([encoded, final_rows])
    outputs, pullback = jax.vjp(forward, *params)
    gradients = pullback(cotangent.astype(jnp.float32))
    return (outputs.astype(jnp.bfloat16), gradients[0], gradients[1], gradients[2], gradients[3], gradients[4], gradients[5], gradients[6])
```

```python
import functools

import jax
import jax.numpy as jnp
from jax import lax
from jax.experimental import pallas as pl
from jax.experimental.pallas import tpu as pltpu
from jax.sharding import PartitionSpec as P

D = 1024
HEADS = 16
HEAD = 64
FF = 2816
L = 1024
MOST = 16
M = 2
P_SIZE = 256
GROUP = 512
VMEM_BYTES = 48 * 1024 * 1024

epsilon = 1e-05
f32 = jnp.float32
bf16 = jnp.bfloat16


def dot(left, right):
    return jnp.dot(left, right, preferred_element_type=f32)


def dot_nt(left, right):
    return lax.dot_general(left, right, (((1,), (1,)), ((), ())), preferred_element_type=f32)


def dot_tn(left, right):
    return lax.dot_general(left, right, (((0,), (0,)), ((), ())), preferred_element_type=f32)


def params(*semantics):
    return pltpu.CompilerParams(vmem_limit_bytes=VMEM_BYTES, dimension_semantics=semantics)


def combine_kernel(slots_ref, ids_ref, rows_ref, table_ref, out_ref):
    tile = out_ref.shape[0]
    first = pl.program_id(0) * tile
    places = first + lax.broadcasted_iota(jnp.int32, (tile, slots_ref.shape[1]), 0)
    chosen = (places == slots_ref[...]).astype(f32).astype(bf16)
    words = lax.broadcasted_iota(jnp.int32, (tile, table_ref.shape[0]), 1)
    word = (words == ids_ref[...]).astype(f32).astype(bf16)
    total = dot(chosen, rows_ref[...]) + dot(word, table_ref[...])
    out_ref[...] = total.astype(bf16)


def combine(slots, ids, rows, table):
    count, width = rows.shape
    positions = ids.shape[0]
    tile = 256
    return pl.pallas_call(
        combine_kernel,
        grid=(positions // tile,),
        in_specs=[
            pl.BlockSpec((1, count), lambda i: (0, 0)),
            pl.BlockSpec((tile, 1), lambda i: (i, 0)),
            pl.BlockSpec((count, width), lambda i: (0, 0)),
            pl.BlockSpec(table.shape, lambda i: (0, 0)),
        ],
        out_specs=pl.BlockSpec((tile, width), lambda i: (i, 0)),
        out_shape=jax.ShapeDtypeStruct((positions, width), bf16),
        compiler_params=params("arbitrary"),
        cost_estimate=pl.CostEstimate(
            flops=2 * positions * count * width, bytes_accessed=12 * count * width // 4, transcendentals=0
        ),
        name="combine_rows",
    )(slots, ids, rows, table)


def spread_kernel(slots_ref, grads_ref, out_ref):
    positions = grads_ref.shape[0]
    places = lax.broadcasted_iota(jnp.int32, (out_ref.shape[0], positions), 1)
    chosen = (places == slots_ref[...]).astype(f32).astype(bf16)
    out_ref[...] = dot(chosen, grads_ref[...]).astype(bf16)


def spread(slots, grads):
    count = slots.shape[0]
    positions, width = grads.shape
    tile = 256
    return pl.pallas_call(
        spread_kernel,
        grid=(count // tile,),
        in_specs=[
            pl.BlockSpec((tile, 1), lambda i: (i, 0)),
            pl.BlockSpec((positions, width), lambda i: (0, 0)),
        ],
        out_specs=pl.BlockSpec((tile, width), lambda i: (i, 0)),
        out_shape=jax.ShapeDtypeStruct((count, width), bf16),
        compiler_params=params("arbitrary"),
        cost_estimate=pl.CostEstimate(
            flops=2 * positions * count * width, bytes_accessed=3 * count * width, transcendentals=0
        ),
        name="spread_grads",
    )(slots, grads)


def head_marks(heads, width):
    feature = lax.shift_right_logical(lax.broadcasted_iota(jnp.int32, (heads, width), 1), 6)
    return (feature == lax.broadcasted_iota(jnp.int32, (heads, width), 0)).astype(f32).astype(bf16)


def patch_marks(patch_row_ref, patch_col_ref):
    by_patch = (
        lax.broadcasted_iota(jnp.int32, (P_SIZE, L), 0) == patch_row_ref[...]
    ).astype(f32).astype(bf16)
    by_byte = (
        lax.broadcasted_iota(jnp.int32, (L, P_SIZE), 1) == patch_col_ref[...]
    ).astype(f32).astype(bf16)
    return by_patch, by_byte


def per_head(marks, products):
    high = products.astype(bf16)
    low = (products - high.astype(f32)).astype(bf16)
    return dot_nt(marks, high) + dot_nt(marks, low)


def neighbours(patches, heads):
    wide = jnp.broadcast_to(patches, (heads, L))
    back = [(d, pltpu.roll(wide, d, 1) == wide) for d in (1, 2, 4, 8)]
    ahead = [(L - d, pltpu.roll(wide, L - d, 1) == wide) for d in (1, 2, 4, 8)]
    return back, ahead


def scan_max(values, steps):
    for distance, same in steps:
        values = jnp.where(same, jnp.maximum(values, pltpu.roll(values, distance, 1)), values)
    return values


def scan_sum(values, steps):
    for distance, same in steps:
        values = jnp.where(same, values + pltpu.roll(values, distance, 1), values)
    return values


def patch_attention_kernel(
    patch_row_ref, patch_col_ref, query_ref, key_ref, value_ref, attention_ref, attended_ref
):
    heads, width = attention_ref.shape[0], query_ref.shape[1]
    marks = head_marks(heads, width)
    by_patch, by_byte = patch_marks(patch_row_ref, patch_col_ref)
    queries = dot(by_byte, query_ref[...])
    scores = per_head(marks, queries * key_ref[...].astype(f32)) * 0.125
    back, ahead = neighbours(patch_row_ref[...], heads)
    top = scan_max(scan_max(scores, back), ahead)
    shifted = jnp.exp(scores - top)
    total = scan_sum(shifted, back) + scan_sum(shifted, ahead) - shifted
    attention = shifted / total
    attention_ref[...] = attention
    weights = dot_tn(attention.astype(bf16), marks)
    weighted = (weights * value_ref[...].astype(f32)).astype(bf16)
    attended_ref[...] = dot(by_patch, weighted).astype(bf16)


def patch_attention(patch_row, patch_col, queries, key_value):
    groups = D // GROUP
    return pl.pallas_call(
        patch_attention_kernel,
        grid=(groups,),
        in_specs=[
            pl.BlockSpec((1, L), lambda i: (0, 0)),
            pl.BlockSpec((L, 1), lambda i: (0, 0)),
            pl.BlockSpec((P_SIZE, GROUP), lambda i: (0, i)),
            pl.BlockSpec((L, GROUP), lambda i: (0, i)),
            pl.BlockSpec((L, GROUP), lambda i: (0, i + groups)),
        ],
        out_specs=[
            pl.BlockSpec((HEADS // groups, L), lambda i: (i, 0)),
            pl.BlockSpec((P_SIZE, GROUP), lambda i: (0, i)),
        ],
        out_shape=[
            jax.ShapeDtypeStruct((HEADS, L), f32),
            jax.ShapeDtypeStruct((P_SIZE, D), bf16),
        ],
        compiler_params=params("arbitrary"),
        cost_estimate=pl.CostEstimate(flops=4 * 10**9, bytes_accessed=6 * 10**6, transcendentals=16384),
        name="patch_attention",
    )(patch_row, patch_col, queries, key_value, key_value)


def patch_attention_back_kernel(
    patch_row_ref,
    patch_col_ref,
    query_ref,
    key_ref,
    value_ref,
    attention_ref,
    grad_ref,
    grad_query_ref,
    grad_key_ref,
    grad_value_ref,
):
    heads, width = attention_ref.shape[0], query_ref.shape[1]
    marks = head_marks(heads, width)
    by_patch, by_byte = patch_marks(patch_row_ref, patch_col_ref)
    grads = dot(by_byte, grad_ref[...])
    attention = attention_ref[...]
    grad_attention = per_head(marks, grads * value_ref[...].astype(f32))
    weights = dot_tn(attention.astype(bf16), marks)
    grad_value_ref[...] = (weights * grads).astype(bf16)
    back, ahead = neighbours(patch_row_ref[...], heads)
    terms = attention * grad_attention
    total = scan_sum(terms, back) + scan_sum(terms, ahead) - terms
    grad_scores = (attention * (grad_attention - total)).astype(bf16)
    spread_scores = dot_tn(grad_scores, marks) * 0.125
    grad_key_ref[...] = (spread_scores * dot(by_byte, query_ref[...])).astype(bf16)
    weighted = (spread_scores * key_ref[...].astype(f32)).astype(bf16)
    grad_query_ref[...] = dot(by_patch, weighted).astype(bf16)


def patch_attention_back(patch_row, patch_col, queries, key_value, attention, grad_attended):
    groups = D // GROUP
    byte_block = pl.BlockSpec((L, GROUP), lambda i: (0, i))
    patch_block = pl.BlockSpec((P_SIZE, GROUP), lambda i: (0, i))
    return pl.pallas_call(
        patch_attention_back_kernel,
        grid=(groups,),
        in_specs=[
            pl.BlockSpec((1, L), lambda i: (0, 0)),
            pl.BlockSpec((L, 1), lambda i: (0, 0)),
            patch_block,
            byte_block,
            pl.BlockSpec((L, GROUP), lambda i: (0, i + groups)),
            pl.BlockSpec((HEADS // groups, L), lambda i: (i, 0)),
            patch_block,
        ],
        out_specs=[patch_block, byte_block, byte_block],
        out_shape=[
            jax.ShapeDtypeStruct((P_SIZE, D), bf16),
            jax.ShapeDtypeStruct((L, D), bf16),
            jax.ShapeDtypeStruct((L, D), bf16),
        ],
        compiler_params=params("arbitrary"),
        cost_estimate=pl.CostEstimate(flops=6 * 10**9, bytes_accessed=10 * 10**6, transcendentals=0),
        name="patch_attention_back",
    )(patch_row, patch_col, queries, key_value, key_value, attention, grad_attended)


def causal_softmax(queries, keys):
    scores = dot_nt(queries, keys) * 0.125
    size = scores.shape[0]
    allowed = lax.broadcasted_iota(jnp.int32, (size, size), 0) >= lax.broadcasted_iota(
        jnp.int32, (size, size), 1
    )
    scores = jnp.where(allowed, scores, -jnp.inf)
    shifted = jnp.exp(scores - jnp.max(scores, axis=-1, keepdims=True))
    return shifted / jnp.sum(shifted, axis=-1, keepdims=True)


def pair_masks(shape):
    lane = lax.broadcasted_iota(jnp.int32, shape, 1)
    return [lane < HEAD, lane >= HEAD]


def causal_kernel(query_ref, key_ref, value_ref, out_ref):
    queries, keys, values = query_ref[...], key_ref[...], value_ref[...]
    masks = pair_masks(queries.shape)
    parts = []
    for mask in masks:
        attention = causal_softmax(jnp.where(mask, queries, 0), keys).astype(bf16)
        parts.append(dot(attention, values))
    out_ref[...] = jnp.where(masks[0], parts[0], parts[1]).astype(bf16)


def causal_attention(mixed):
    pairs = HEADS // 2
    return pl.pallas_call(
        causal_kernel,
        grid=(pairs,),
        in_specs=[
            pl.BlockSpec((P_SIZE, 2 * HEAD), lambda i: (0, i)),
            pl.BlockSpec((P_SIZE, 2 * HEAD), lambda i: (0, i + pairs)),
            pl.BlockSpec((P_SIZE, 2 * HEAD), lambda i: (0, i + 2 * pairs)),
        ],
        out_specs=pl.BlockSpec((P_SIZE, 2 * HEAD), lambda i: (0, i)),
        out_shape=jax.ShapeDtypeStruct((P_SIZE, D), bf16),
        compiler_params=params("arbitrary"),
        cost_estimate=pl.CostEstimate(flops=2 * 10**9, bytes_accessed=2 * 10**6, transcendentals=10**6),
        name="causal_attention",
    )(mixed, mixed, mixed)


def causal_back_kernel(query_ref, key_ref, value_ref, grad_ref, gq_ref, gk_ref, gv_ref):
    queries, keys, values, grads = query_ref[...], key_ref[...], value_ref[...], grad_ref[...]
    masks = pair_masks(queries.shape)
    results = []
    for mask in masks:
        attention = causal_softmax(jnp.where(mask, queries, 0), keys)
        grad_attention = dot_nt(jnp.where(mask, grads, 0), values)
        total = jnp.sum(attention * grad_attention, axis=-1, keepdims=True)
        grad_scores = (attention * (grad_attention - total)).astype(bf16)
        results.append(
            (
                dot(grad_scores, keys) * 0.125,
                dot_tn(grad_scores, queries) * 0.125,
                dot_tn(attention.astype(bf16), grads),
            )
        )
    for ref, first, second in zip((gq_ref, gk_ref, gv_ref), results[0], results[1]):
        ref[...] = jnp.where(masks[0], first, second).astype(bf16)


def causal_attention_back(mixed, grad_attended):
    pairs = HEADS // 2
    block = pl.BlockSpec((P_SIZE, 2 * HEAD), lambda i: (0, i))
    return pl.pallas_call(
        causal_back_kernel,
        grid=(pairs,),
        in_specs=[
            block,
            pl.BlockSpec((P_SIZE, 2 * HEAD), lambda i: (0, i + pairs)),
            pl.BlockSpec((P_SIZE, 2 * HEAD), lambda i: (0, i + 2 * pairs)),
            block,
        ],
        out_specs=[block] * 3,
        out_shape=[jax.ShapeDtypeStruct((P_SIZE, D), bf16)] * 3,
        compiler_params=params("arbitrary"),
        cost_estimate=pl.CostEstimate(flops=4 * 10**9, bytes_accessed=4 * 10**6, transcendentals=10**6),
        name="causal_attention_back",
    )(mixed, mixed, mixed, grad_attended)


def normalize(inputs, gain):
    inverse = lax.rsqrt(jnp.mean(inputs * inputs, axis=-1, keepdims=True) + epsilon)
    return (inputs * inverse * gain).astype(bf16), inverse


def normalize_back(inputs, gain, inverse, grad_normed):
    scaled = inputs * inverse
    grad_gain = jnp.sum(grad_normed * scaled, axis=0)
    grad_scaled = grad_normed * gain
    grad_inputs = inverse * (
        grad_scaled - scaled * jnp.mean(grad_scaled * scaled, axis=-1, keepdims=True)
    )
    return grad_inputs, grad_gain


def feed_forward(hidden, gain, w_gate_up, w_down):
    normed, inverse = normalize(hidden, gain)
    joined = dot(normed, w_gate_up)
    inner = (jax.nn.silu(joined[:, :FF]) * joined[:, FF:]).astype(bf16)
    return hidden + dot(inner, w_down), (normed, inverse, joined, inner)


def feed_back(hidden, gain, w_gate_up, w_down, kept, grad_out):
    normed, inverse, joined, inner = kept
    gate, up = joined[:, :FF], joined[:, FF:]
    sigmoid = jax.nn.sigmoid(gate)
    grad_branch = grad_out.astype(bf16)
    grad_inner = dot_nt(grad_branch, w_down)
    grad_gate = grad_inner * up * sigmoid * (1.0 + gate * (1.0 - sigmoid))
    grad_up = grad_inner * gate * sigmoid
    grad_joined = jnp.concatenate([grad_gate, grad_up], axis=1).astype(bf16)
    grad_normed = dot_nt(grad_joined, w_gate_up)
    grad_in, grad_gain = normalize_back(hidden, gain, inverse, grad_normed)
    return grad_out + grad_in, grad_gain, grad_joined, grad_branch


def factors(count):
    sides = [1, 1, 1]
    prime = 2
    while count > 1:
        while count % prime == 0:
            sides[sides.index(min(sides))] *= prime
            count //= prime
        prime += 1
    return sides


def sum_along(block, sides, kept, which):
    stride = 1
    for side in sides[which + 1 :]:
        stride *= side
    size = sides[which]
    if size == 1:
        return block
    total = sides[0] * sides[1] * sides[2]
    place = (lax.axis_index("rows") // stride) % size
    axis = kept.index(which)

    def part(index):
        return lax.dynamic_index_in_dim(block, index, axis, keepdims=False)

    result = part(place).astype(f32)
    for step in range(1, size):
        route = []
        for device in range(total):
            own = (device // stride) % size
            route.append((device, device + ((own + step) % size - own) * stride))
        arrived = lax.ppermute(part((place + step) % size), "rows", route)
        result = result + arrived.astype(f32)
    return result.astype(bf16)


def scatter_sum(block, order):
    devices = lax.axis_size("rows")
    sides = factors(devices)
    kept = [0, 1, 2]
    block = block.reshape(*sides, block.shape[0] // devices, block.shape[1])
    for which in order:
        if sides[which] == 1:
            block = block.reshape([s for d, s in enumerate(block.shape) if d != kept.index(which)])
        else:
            block = sum_along(block, sides, kept, which)
        kept.remove(which)
    return block


def swap(array):
    return lax.ppermute(array, "section", [(0, 1), (1, 0)])


def on_device(
    byte_ids,
    hash_ids,
    patch_lengths,
    row_lengths,
    byte_table,
    hash_tables,
    norm_gains,
    w_qkv,
    w_out,
    w_gate_up,
    w_down,
    cotangent,
):
    section = lax.axis_index("section")
    first_core = section == 0
    devices = lax.axis_size("rows")
    count_tables, shard_rows, half_width = hash_tables.shape
    positions = M * L

    def both(array):
        return lax.all_gather(array, "section", axis=0, tiled=True)

    flat_ids = hash_ids.reshape(positions, count_tables).T
    owners = flat_ids // shard_rows
    local_rows = flat_ids % shard_rows + jnp.arange(count_tables, dtype=jnp.int32)[:, None] * shard_rows
    order_key = owners * positions + jnp.arange(positions, dtype=jnp.int32)[None, :]
    order_key, grouped = lax.sort((order_key, local_rows), dimension=1, num_keys=1)

    def by_owner(array):
        return array.reshape(count_tables, devices, -1).transpose(1, 0, 2).reshape(devices, -1)

    slots = by_owner(order_key % positions).reshape(-1)
    requested = lax.all_to_all(by_owner(grouped), "rows", split_axis=0, concat_axis=0, tiled=True)
    flat_tables = hash_tables.reshape(count_tables * shard_rows, half_width)
    found_rows = jnp.take(flat_tables, requested, axis=0)
    returned = lax.all_to_all(found_rows, "rows", split_axis=0, concat_axis=0, tiled=True)

    gains = both(norm_gains).astype(f32)
    qkv_both, out_both = both(w_qkv), both(w_out)
    gate_up_both, down_both = both(w_gate_up), both(w_down)

    lengths = lax.dynamic_index_in_dim(patch_lengths, section, 0, keepdims=False)
    row_length = lax.dynamic_index_in_dim(row_lengths, section, 0, keepdims=False)
    starts = jnp.cumsum(lengths) - lengths
    byte_positions = jnp.arange(L, dtype=jnp.int32)
    byte_patch = jnp.sum((starts[:, None] <= byte_positions[None, :]).astype(jnp.int32), axis=0) - 1
    patch_row, patch_col = byte_patch[None, :], byte_patch[:, None]
    patches = jnp.arange(P_SIZE, dtype=jnp.int32)
    member = (patches[:, None] == patch_row).astype(bf16)
    member_byte = (patches[None, :] == patch_col).astype(bf16)
    counts = lengths.astype(f32)[:, None]
    valid = (patches < row_length)[:, None]

    own_cotangent = lax.dynamic_index_in_dim(cotangent[0], section, 0, keepdims=False)
    sent_cotangent = swap(lax.dynamic_index_in_dim(cotangent[0], 1 - section, 0, keepdims=False))
    cotangent_one = jnp.where(first_core, own_cotangent, sent_cotangent).astype(f32)
    cotangent_two = jnp.where(first_core, sent_cotangent, own_cotangent).astype(f32)

    flat_bytes = byte_ids.reshape(positions)
    table_rows = byte_table.shape[0]
    padded = jnp.pad(byte_table, ((0, -table_rows % 128), (0, 0)))
    own_half = combine(
        slots[None, :], flat_bytes[:, None], returned.reshape(-1, half_width), padded
    ).reshape(M, L, half_width)
    kept_half = lax.dynamic_index_in_dim(own_half, section, 0, keepdims=False)
    sent_half = swap(lax.dynamic_index_in_dim(own_half, 1 - section, 0, keepdims=False))
    byte_rows = jnp.concatenate(
        [jnp.where(first_core, kept_half, sent_half), jnp.where(first_core, sent_half, kept_half)], axis=1
    )

    pooled = dot(member, byte_rows) / counts
    normed_one, inverse_one = normalize(pooled, gains[0, 0])
    queries_one = dot(normed_one, qkv_both[0, :, :D]).astype(bf16)
    byte_pairs = dot(byte_rows, qkv_both[0, :, D:]).astype(bf16)
    attention_one, attended_one = patch_attention(patch_row, patch_col, queries_one, byte_pairs)
    middle_one = pooled + dot(attended_one, out_both[0])
    result_one, kept_one = feed_forward(middle_one, gains[0, 1], gate_up_both[0], down_both[0])
    encoded = jnp.where(valid, result_one, pooled).astype(bf16)

    inputs_two = encoded.astype(f32)
    normed_two, inverse_two = normalize(inputs_two, gains[1, 0])
    mixed = dot(normed_two, qkv_both[1]).astype(bf16)
    attended_two = causal_attention(mixed)
    middle_two = inputs_two + dot(attended_two, out_both[1])
    result_two, kept_two = feed_forward(middle_two, gains[1, 1], gate_up_both[1], down_both[1])
    final = jnp.where(valid, result_two, inputs_two).astype(bf16)
    sent_out = swap(jnp.where(first_core, final, encoded))
    kept_out = jnp.where(first_core, encoded, final)
    section_out = jnp.where(
        first_core, jnp.stack([kept_out, sent_out]), jnp.stack([sent_out, kept_out])
    )[None]

    def share(left, right):
        width = right.shape[1] // 2
        mine = lax.dynamic_slice_in_dim(right, section * width, width, axis=1)
        theirs = lax.dynamic_slice_in_dim(right, (1 - section) * width, width, axis=1)
        lefts = jnp.concatenate([left, swap(left)], axis=0)
        rights = jnp.concatenate([mine, swap(theirs)], axis=0)
        return dot_tn(lefts, rights).astype(bf16)

    grad_kept = jnp.where(valid, cotangent_two, 0.0)
    grad_middle, gain_two_second, grad_joined, grad_branch = feed_back(
        middle_two, gains[1, 1], gate_up_both[1], down_both[1], kept_two, grad_kept
    )
    gate_up_two = scatter_sum(share(kept_two[0], grad_joined), (2, 1, 0))
    down_two = scatter_sum(share(grad_branch, kept_two[3]), (1, 2, 0))
    grad_low = grad_middle.astype(bf16)
    grad_attended = dot_nt(grad_low, out_both[1]).astype(bf16)
    grad_mixed = jnp.concatenate(causal_attention_back(mixed, grad_attended), axis=1)
    rest_two = scatter_sum(
        jnp.concatenate([share(normed_two, grad_mixed), share(attended_two, grad_low)], axis=1), (1, 2, 0)
    )
    grad_normed = dot_nt(grad_mixed, qkv_both[1])
    grad_in, gain_two_first = normalize_back(inputs_two, gains[1, 0], inverse_two, grad_normed)
    grad_encoded = jnp.where(valid, 0.0, cotangent_two) + grad_middle + grad_in

    grad_out = cotangent_one + grad_encoded.astype(bf16).astype(f32)
    grad_kept = jnp.where(valid, grad_out, 0.0)
    grad_middle, gain_one_second, grad_joined, grad_branch = feed_back(
        middle_one, gains[0, 1], gate_up_both[0], down_both[0], kept_one, grad_kept
    )
    gate_up_one = scatter_sum(share(kept_one[0], grad_joined), (2, 1, 0))
    down_one = scatter_sum(share(grad_branch, kept_one[3]), (1, 2, 0))
    grad_low = grad_middle.astype(bf16)
    grad_attended = dot_nt(grad_low, out_both[0]).astype(bf16)
    grad_queries, grad_keys, grad_values = patch_attention_back(
        patch_row, patch_col, queries_one, byte_pairs, attention_one, grad_attended
    )
    grad_pairs = jnp.concatenate([grad_keys, grad_values], axis=1)
    grad_normed = dot_nt(grad_queries, qkv_both[0, :, :D])
    grad_in, gain_one_first = normalize_back(pooled, gains[0, 0], inverse_one, grad_normed)
    grad_pooled = jnp.where(valid, 0.0, grad_out) + grad_middle + grad_in
    grad_bytes = dot(member_byte, (grad_pooled / counts).astype(bf16))
    grad_bytes = (grad_bytes + dot_nt(grad_pairs, qkv_both[0, :, D:])).astype(bf16)

    grad_halves = grad_bytes.reshape(L, 2, half_width)
    kept_grad = lax.dynamic_index_in_dim(grad_halves, section, 1, keepdims=False)
    sent_grad = swap(lax.dynamic_index_in_dim(grad_halves, 1 - section, 1, keepdims=False))
    own_grad = jnp.where(
        first_core,
        jnp.concatenate([kept_grad, sent_grad], axis=0),
        jnp.concatenate([sent_grad, kept_grad], axis=0),
    )
    slot_grads = spread(slots[:, None], own_grad).reshape(devices, -1, half_width)
    arrived = lax.all_to_all(slot_grads, "rows", split_axis=0, concat_axis=0, tiled=True)
    hash_grad = jax.ops.segment_sum(
        arrived.reshape(-1, half_width).astype(f32),
        requested.reshape(-1),
        num_segments=count_tables * shard_rows,
    ).reshape(count_tables, shard_rows, half_width)
    words = (flat_bytes[:, None] == jnp.arange(table_rows, dtype=jnp.int32)[None, :]).astype(bf16)
    byte_table_grad = lax.psum(dot_tn(words, own_grad), "rows")

    rest_one = scatter_sum(
        jnp.concatenate(
            [share(normed_one, grad_queries), share(byte_rows, grad_pairs), share(attended_one, grad_low)],
            axis=1,
        ),
        (1, 2, 0),
    )

    sums_one = jnp.concatenate([gate_up_one, down_one, rest_one], axis=1)
    sums_two = jnp.concatenate([gate_up_two, down_two, rest_two], axis=1)
    kept_sums = jnp.where(first_core, sums_one, sums_two)
    sent_sums = swap(jnp.where(first_core, sums_two, sums_one))
    lower = jnp.where(first_core, kept_sums, sent_sums).astype(f32)
    upper = jnp.where(first_core, sent_sums, kept_sums).astype(f32)
    half_ff = FF // 2
    gate_up_grad = jnp.concatenate([lower[:, :FF], upper[:, :FF]], axis=1)
    down_grad = jnp.concatenate([lower[:, FF : FF + half_ff], upper[:, FF : FF + half_ff]], axis=1).T
    low_rest, high_rest = lower[:, FF + half_ff :], upper[:, FF + half_ff :]
    half = D // 2
    out_grad = jnp.concatenate([low_rest[:, -half:], high_rest[:, -half:]], axis=1)
    pieces_one = [low_rest[:, :half], high_rest[:, :half], low_rest[:, half : 3 * half], high_rest[:, half : 3 * half]]
    pieces_two = [low_rest[:, : 3 * half], high_rest[:, : 3 * half]]
    qkv_grad = jnp.where(
        first_core, jnp.concatenate(pieces_one, axis=1), jnp.concatenate(pieces_two, axis=1)
    )

    gain_sums = jnp.stack([gain_one_first, gain_one_second, gain_two_first, gain_two_second])
    gain_sums = lax.psum_scatter(gain_sums, "rows", scatter_dimension=1, tiled=True)
    gain_sums = (gain_sums + swap(gain_sums)).reshape(2, 2, -1)
    gains_grad = lax.dynamic_index_in_dim(gain_sums, section, 0, keepdims=True)

    return (
        section_out,
        byte_table_grad,
        hash_grad,
        gains_grad,
        qkv_grad[None],
        out_grad[None],
        gate_up_grad[None],
        down_grad[None],
    )


def solution(mesh):
    return jax.shard_map(
        on_device,
        mesh=mesh,
        in_specs=(
            P("rows", None),
            P("rows", None, None),
            P("rows", None),
            P("rows"),
            P(None, "section"),
            P(None, "rows", "section"),
            P("section", None, None),
            P("section", None, None),
            P("section", None, None),
            P("section", None, None),
            P("section", None, None),
            P("section", "rows", None, None),
        ),
        out_specs=(
            P("section", "rows", None, None),
            P(None, "section"),
            P(None, "rows", "section"),
            P("section", None, "rows"),
            P("section", "rows", None),
            P("section", "rows", None),
            P("section", "rows", None),
            P("section", None, "rows"),
        ),
        check_vma=False,
    )
```

```python
import functools

import jax
import jax.numpy as jnp
from jax import lax
from jax.experimental import pallas as pl
from jax.experimental.pallas import tpu as pltpu
from jax.sharding import PartitionSpec as P

D = 1024
HEADS = 16
HEAD = 64
FF = 2816
L = 1024
MOST = 16
M = 2
P_SIZE = 256
GROUP = 512
VMEM_BYTES = 48 * 1024 * 1024

epsilon = 1e-05
A, B = (2, 1, 0), (1, 2, 0)
f32 = jnp.float32
bf16 = jnp.bfloat16


def dot(left, right):
    return jnp.dot(left, right, preferred_element_type=f32)


def dot_nt(left, right):
    return lax.dot_general(left, right, (((1,), (1,)), ((), ())), preferred_element_type=f32)


def dot_tn(left, right):
    return lax.dot_general(left, right, (((0,), (0,)), ((), ())), preferred_element_type=f32)


def params(*semantics):
    return pltpu.CompilerParams(vmem_limit_bytes=VMEM_BYTES, dimension_semantics=semantics)


def combine_kernel(slots_ref, ids_ref, rows_ref, table_ref, out_ref):
    tile = out_ref.shape[0]
    first = pl.program_id(0) * tile
    places = first + lax.broadcasted_iota(jnp.int32, (tile, slots_ref.shape[1]), 0)
    chosen = (places == slots_ref[...]).astype(f32).astype(bf16)
    words = lax.broadcasted_iota(jnp.int32, (tile, table_ref.shape[0]), 1)
    word = (words == ids_ref[...]).astype(f32).astype(bf16)
    total = dot(chosen, rows_ref[...]) + dot(word, table_ref[...])
    out_ref[...] = total.astype(bf16)


def combine(slots, ids, rows, table):
    count, width = rows.shape
    positions = ids.shape[0]
    tile = 256
    return pl.pallas_call(
        combine_kernel,
        grid=(positions // tile,),
        in_specs=[
            pl.BlockSpec((1, count), lambda i: (0, 0)),
            pl.BlockSpec((tile, 1), lambda i: (i, 0)),
            pl.BlockSpec((count, width), lambda i: (0, 0)),
            pl.BlockSpec(table.shape, lambda i: (0, 0)),
        ],
        out_specs=pl.BlockSpec((tile, width), lambda i: (i, 0)),
        out_shape=jax.ShapeDtypeStruct((positions, width), bf16),
        compiler_params=params("arbitrary"),
        cost_estimate=pl.CostEstimate(
            flops=2 * positions * count * width, bytes_accessed=12 * count * width // 4, transcendentals=0
        ),
        name="combine_rows",
    )(slots, ids, rows, table)


def spread_kernel(slots_ref, grads_ref, out_ref):
    positions = grads_ref.shape[0]
    places = lax.broadcasted_iota(jnp.int32, (out_ref.shape[0], positions), 1)
    chosen = (places == slots_ref[...]).astype(f32).astype(bf16)
    out_ref[...] = dot(chosen, grads_ref[...]).astype(bf16)


def spread(slots, grads):
    count = slots.shape[0]
    positions, width = grads.shape
    tile = 256
    return pl.pallas_call(
        spread_kernel,
        grid=(count // tile,),
        in_specs=[
            pl.BlockSpec((tile, 1), lambda i: (i, 0)),
            pl.BlockSpec((positions, width), lambda i: (0, 0)),
        ],
        out_specs=pl.BlockSpec((tile, width), lambda i: (i, 0)),
        out_shape=jax.ShapeDtypeStruct((count, width), bf16),
        compiler_params=params("arbitrary"),
        cost_estimate=pl.CostEstimate(
            flops=2 * positions * count * width, bytes_accessed=3 * count * width, transcendentals=0
        ),
        name="spread_grads",
    )(slots, grads)


def head_marks(heads, width):
    feature = lax.shift_right_logical(lax.broadcasted_iota(jnp.int32, (heads, width), 1), 6)
    return (feature == lax.broadcasted_iota(jnp.int32, (heads, width), 0)).astype(f32).astype(bf16)


def patch_marks(patch_row_ref, patch_col_ref):
    by_patch = (
        lax.broadcasted_iota(jnp.int32, (P_SIZE, L), 0) == patch_row_ref[...]
    ).astype(f32).astype(bf16)
    by_byte = (
        lax.broadcasted_iota(jnp.int32, (L, P_SIZE), 1) == patch_col_ref[...]
    ).astype(f32).astype(bf16)
    return by_patch, by_byte


def per_head(marks, products):
    high = products.astype(bf16)
    low = (products - high.astype(f32)).astype(bf16)
    return dot_nt(marks, high) + dot_nt(marks, low)


def neighbours(patches, heads):
    wide = jnp.broadcast_to(patches, (heads, L))
    back = [(d, pltpu.roll(wide, d, 1) == wide) for d in (1, 2, 4, 8)]
    ahead = [(L - d, pltpu.roll(wide, L - d, 1) == wide) for d in (1, 2, 4, 8)]
    return back, ahead


def scan_max(values, steps):
    for distance, same in steps:
        values = jnp.where(same, jnp.maximum(values, pltpu.roll(values, distance, 1)), values)
    return values


def scan_sum(values, steps):
    for distance, same in steps:
        values = jnp.where(same, values + pltpu.roll(values, distance, 1), values)
    return values


def patch_attention_kernel(
    patch_row_ref, patch_col_ref, query_ref, key_ref, value_ref, attention_ref, attended_ref
):
    heads, width = attention_ref.shape[0], query_ref.shape[1]
    marks = head_marks(heads, width)
    by_patch, by_byte = patch_marks(patch_row_ref, patch_col_ref)
    queries = dot(by_byte, query_ref[...])
    scores = per_head(marks, queries * key_ref[...].astype(f32)) * 0.125
    back, ahead = neighbours(patch_row_ref[...], heads)
    top = scan_max(scan_max(scores, back), ahead)
    shifted = jnp.exp(scores - top)
    total = scan_sum(shifted, back) + scan_sum(shifted, ahead) - shifted
    attention = shifted / total
    attention_ref[...] = attention
    weights = dot_tn(attention.astype(bf16), marks)
    weighted = (weights * value_ref[...].astype(f32)).astype(bf16)
    attended_ref[...] = dot(by_patch, weighted).astype(bf16)


def patch_attention(patch_row, patch_col, queries, key_value):
    groups = D // GROUP
    return pl.pallas_call(
        patch_attention_kernel,
        grid=(groups,),
        in_specs=[
            pl.BlockSpec((1, L), lambda i: (0, 0)),
            pl.BlockSpec((L, 1), lambda i: (0, 0)),
            pl.BlockSpec((P_SIZE, GROUP), lambda i: (0, i)),
            pl.BlockSpec((L, GROUP), lambda i: (0, i)),
            pl.BlockSpec((L, GROUP), lambda i: (0, i + groups)),
        ],
        out_specs=[
            pl.BlockSpec((HEADS // groups, L), lambda i: (i, 0)),
            pl.BlockSpec((P_SIZE, GROUP), lambda i: (0, i)),
        ],
        out_shape=[
            jax.ShapeDtypeStruct((HEADS, L), f32),
            jax.ShapeDtypeStruct((P_SIZE, D), bf16),
        ],
        compiler_params=params("arbitrary"),
        cost_estimate=pl.CostEstimate(flops=4 * 10**9, bytes_accessed=6 * 10**6, transcendentals=16384),
        name="patch_attention",
    )(patch_row, patch_col, queries, key_value, key_value)


def patch_attention_back_kernel(
    patch_row_ref,
    patch_col_ref,
    query_ref,
    key_ref,
    value_ref,
    attention_ref,
    grad_ref,
    grad_query_ref,
    grad_key_ref,
    grad_value_ref,
):
    heads, width = attention_ref.shape[0], query_ref.shape[1]
    marks = head_marks(heads, width)
    by_patch, by_byte = patch_marks(patch_row_ref, patch_col_ref)
    grads = dot(by_byte, grad_ref[...])
    attention = attention_ref[...]
    grad_attention = per_head(marks, grads * value_ref[...].astype(f32))
    weights = dot_tn(attention.astype(bf16), marks)
    grad_value_ref[...] = (weights * grads).astype(bf16)
    back, ahead = neighbours(patch_row_ref[...], heads)
    terms = attention * grad_attention
    total = scan_sum(terms, back) + scan_sum(terms, ahead) - terms
    grad_scores = (attention * (grad_attention - total)).astype(bf16)
    spread_scores = dot_tn(grad_scores, marks) * 0.125
    grad_key_ref[...] = (spread_scores * dot(by_byte, query_ref[...])).astype(bf16)
    weighted = (spread_scores * key_ref[...].astype(f32)).astype(bf16)
    grad_query_ref[...] = dot(by_patch, weighted).astype(bf16)


def patch_attention_back(patch_row, patch_col, queries, key_value, attention, grad_attended):
    groups = D // GROUP
    byte_block = pl.BlockSpec((L, GROUP), lambda i: (0, i))
    patch_block = pl.BlockSpec((P_SIZE, GROUP), lambda i: (0, i))
    return pl.pallas_call(
        patch_attention_back_kernel,
        grid=(groups,),
        in_specs=[
            pl.BlockSpec((1, L), lambda i: (0, 0)),
            pl.BlockSpec((L, 1), lambda i: (0, 0)),
            patch_block,
            byte_block,
            pl.BlockSpec((L, GROUP), lambda i: (0, i + groups)),
            pl.BlockSpec((HEADS // groups, L), lambda i: (i, 0)),
            patch_block,
        ],
        out_specs=[patch_block, byte_block, byte_block],
        out_shape=[
            jax.ShapeDtypeStruct((P_SIZE, D), bf16),
            jax.ShapeDtypeStruct((L, D), bf16),
            jax.ShapeDtypeStruct((L, D), bf16),
        ],
        compiler_params=params("arbitrary"),
        cost_estimate=pl.CostEstimate(flops=6 * 10**9, bytes_accessed=10 * 10**6, transcendentals=0),
        name="patch_attention_back",
    )(patch_row, patch_col, queries, key_value, key_value, attention, grad_attended)


def causal_softmax(queries, keys):
    scores = dot_nt(queries, keys) * 0.125
    size = scores.shape[0]
    allowed = lax.broadcasted_iota(jnp.int32, (size, size), 0) >= lax.broadcasted_iota(
        jnp.int32, (size, size), 1
    )
    scores = jnp.where(allowed, scores, -jnp.inf)
    shifted = jnp.exp(scores - jnp.max(scores, axis=-1, keepdims=True))
    return shifted / jnp.sum(shifted, axis=-1, keepdims=True)


def pair_masks(shape):
    lane = lax.broadcasted_iota(jnp.int32, shape, 1)
    return [lane < HEAD, lane >= HEAD]


def causal_kernel(query_ref, key_ref, value_ref, out_ref):
    queries, keys, values = query_ref[...], key_ref[...], value_ref[...]
    masks = pair_masks(queries.shape)
    parts = []
    for mask in masks:
        attention = causal_softmax(jnp.where(mask, queries, 0), keys).astype(bf16)
        parts.append(dot(attention, values))
    out_ref[...] = jnp.where(masks[0], parts[0], parts[1]).astype(bf16)


def causal_attention(mixed):
    pairs = HEADS // 2
    return pl.pallas_call(
        causal_kernel,
        grid=(pairs,),
        in_specs=[
            pl.BlockSpec((P_SIZE, 2 * HEAD), lambda i: (0, i)),
            pl.BlockSpec((P_SIZE, 2 * HEAD), lambda i: (0, i + pairs)),
            pl.BlockSpec((P_SIZE, 2 * HEAD), lambda i: (0, i + 2 * pairs)),
        ],
        out_specs=pl.BlockSpec((P_SIZE, 2 * HEAD), lambda i: (0, i)),
        out_shape=jax.ShapeDtypeStruct((P_SIZE, D), bf16),
        compiler_params=params("arbitrary"),
        cost_estimate=pl.CostEstimate(flops=2 * 10**9, bytes_accessed=2 * 10**6, transcendentals=10**6),
        name="causal_attention",
    )(mixed, mixed, mixed)


def causal_back_kernel(query_ref, key_ref, value_ref, grad_ref, gq_ref, gk_ref, gv_ref):
    queries, keys, values, grads = query_ref[...], key_ref[...], value_ref[...], grad_ref[...]
    masks = pair_masks(queries.shape)
    results = []
    for mask in masks:
        attention = causal_softmax(jnp.where(mask, queries, 0), keys)
        grad_attention = dot_nt(jnp.where(mask, grads, 0), values)
        total = jnp.sum(attention * grad_attention, axis=-1, keepdims=True)
        grad_scores = (attention * (grad_attention - total)).astype(bf16)
        results.append(
            (
                dot(grad_scores, keys) * 0.125,
                dot_tn(grad_scores, queries) * 0.125,
                dot_tn(attention.astype(bf16), grads),
            )
        )
    for ref, first, second in zip((gq_ref, gk_ref, gv_ref), results[0], results[1]):
        ref[...] = jnp.where(masks[0], first, second).astype(bf16)


def causal_attention_back(mixed, grad_attended):
    pairs = HEADS // 2
    block = pl.BlockSpec((P_SIZE, 2 * HEAD), lambda i: (0, i))
    return pl.pallas_call(
        causal_back_kernel,
        grid=(pairs,),
        in_specs=[
            block,
            pl.BlockSpec((P_SIZE, 2 * HEAD), lambda i: (0, i + pairs)),
            pl.BlockSpec((P_SIZE, 2 * HEAD), lambda i: (0, i + 2 * pairs)),
            block,
        ],
        out_specs=[block] * 3,
        out_shape=[jax.ShapeDtypeStruct((P_SIZE, D), bf16)] * 3,
        compiler_params=params("arbitrary"),
        cost_estimate=pl.CostEstimate(flops=4 * 10**9, bytes_accessed=4 * 10**6, transcendentals=10**6),
        name="causal_attention_back",
    )(mixed, mixed, mixed, grad_attended)


def normalize(inputs, gain):
    inverse = lax.rsqrt(jnp.mean(inputs * inputs, axis=-1, keepdims=True) + epsilon)
    return (inputs * inverse * gain).astype(bf16), inverse


def normalize_back(inputs, gain, inverse, grad_normed):
    scaled = inputs * inverse
    grad_gain = jnp.sum(grad_normed * scaled, axis=0)
    grad_scaled = grad_normed * gain
    grad_inputs = inverse * (
        grad_scaled - scaled * jnp.mean(grad_scaled * scaled, axis=-1, keepdims=True)
    )
    return grad_inputs, grad_gain


def feed_forward(hidden, gain, w_gate_up, w_down):
    normed, inverse = normalize(hidden, gain)
    joined = dot(normed, w_gate_up)
    inner = (jax.nn.silu(joined[:, :FF]) * joined[:, FF:]).astype(bf16)
    return hidden + dot(inner, w_down), (normed, inverse, joined, inner)


def feed_back(hidden, gain, w_gate_up, w_down, kept, grad_out):
    normed, inverse, joined, inner = kept
    gate, up = joined[:, :FF], joined[:, FF:]
    sigmoid = jax.nn.sigmoid(gate)
    grad_branch = grad_out.astype(bf16)
    grad_inner = dot_nt(grad_branch, w_down)
    grad_gate = grad_inner * up * sigmoid * (1.0 + gate * (1.0 - sigmoid))
    grad_up = grad_inner * gate * sigmoid
    grad_joined = jnp.concatenate([grad_gate, grad_up], axis=1).astype(bf16)
    grad_normed = dot_nt(grad_joined, w_gate_up)
    grad_in, grad_gain = normalize_back(hidden, gain, inverse, grad_normed)
    return grad_out + grad_in, grad_gain, grad_joined, grad_branch


def factors(count):
    sides = [1, 1, 1]
    prime = 2
    while count > 1:
        while count % prime == 0:
            sides[sides.index(min(sides))] *= prime
            count //= prime
        prime += 1
    return sides


def at_place(ref, axis, place):
    return ref.at[(slice(None),) * axis + (place,)]


def sum_kernel(sides, plan, counts, *refs):
    devices = sides[0] * sides[1] * sides[2]
    arrays, refs = refs[: counts[0]], refs[counts[0] :]
    blocks_ref, refs = refs[0], refs[1:]
    outs, refs = refs[: counts[1]], refs[counts[1] :]
    gathered_ref, arrived_ref, refs = refs[0], refs[1], refs[2:]
    pieces = len(plan)
    owns, refs = refs[:pieces], refs[pieces:]
    lands, refs = [refs[3 * i : 3 * i + 3] for i in range(pieces)], refs[3 * pieces :]
    send_sems, land_sems, load_sems, trade_send, trade_land, spread_send, spread_land, own_sem = refs
    most = max(sides) - 1

    me = lax.axis_index("rows")
    strides = (sides[1] * sides[2], sides[2], 1)
    places = [(me // strides[d]) % sides[d] for d in range(3)]

    def other(step):
        return lax.rem(me + step, devices)

    barrier = pltpu.get_barrier_semaphore()
    for step in range(1, devices):
        pl.semaphore_signal(
            barrier, inc=1, device_id={"rows": other(step)}, device_id_type=pl.DeviceIdType.MESH
        )
    pl.semaphore_wait(barrier, devices - 1)

    def remote(source, target, send, land, device):
        return pltpu.make_async_remote_copy(
            src_ref=source,
            dst_ref=target,
            send_sem=send,
            recv_sem=land,
            device_id={"rows": device},
            device_id_type=pl.DeviceIdType.MESH,
        )

    def source_of(piece):
        array, first, width, order = plan[piece]
        return arrays[array].at[:, :, :, :, pl.ds(first, width)]

    def sends(piece, phase):
        order = plan[piece][3]
        axis = order[phase]
        left = [d for d in range(3) if d not in order[:phase]]
        at = left.index(axis)
        ref = source_of(piece) if phase == 0 else kept(piece, phase)
        copies = []
        for step in range(1, sides[axis]):
            there = lax.rem(places[axis] + step, sides[axis])
            device = me + (there - places[axis]) * strides[axis]
            slot = (piece * 3 + phase) * most + step - 1
            copies.append(
                remote(
                    at_place(ref, at, there),
                    lands[piece][phase].at[step - 1],
                    send_sems.at[slot],
                    land_sems.at[slot],
                    device,
                )
            )
        return copies

    def kept(piece, phase):
        order = plan[piece][3]
        ref = owns[piece]
        left = [d for d in range(3) if d != order[0]]
        for axis in order[1:phase]:
            ref = at_place(ref, left.index(axis), places[axis])
            left.remove(axis)
        return ref

    def load(piece):
        axis = plan[piece][3][0]
        return pltpu.make_async_copy(
            at_place(source_of(piece), axis, places[axis]), owns[piece], load_sems.at[piece]
        )

    def add(piece, phase):
        target = kept(piece, phase + 1)
        land = lands[piece][phase]
        leads = target.shape[:-2]
        count = 1
        for size in leads:
            count *= size
        rows = 16
        groups = target.shape[-2] // rows

        def body(index, carry):
            at = (pl.ds(pl.multiple_of(index % groups * rows, rows), rows), slice(None))
            lead = index // groups
            if len(leads) == 2:
                at = (lead // leads[1], lead % leads[1]) + at
            elif len(leads) == 1:
                at = (lead,) + at
            value = target[at].astype(f32)
            for step in range(land.shape[0]):
                value = value + land[(step,) + at].astype(f32)
            target[at] = value.astype(bf16)
            return carry

        lax.fori_loop(0, count * groups, body, 0)

    def start(copies):
        for copy in copies:
            copy.start()

    def settle(piece, phase):
        for copy in sends(piece, phase):
            copy.wait_recv()

    def trades():
        return [
            remote(
                blocks_ref.at[other(step)],
                arrived_ref.at[me],
                trade_send.at[step - 1],
                trade_land.at[step - 1],
                other(step),
            )
            for step in range(1, devices)
        ]

    def spreads():
        return [
            remote(
                gathered_ref.at[me],
                gathered_ref.at[me],
                spread_send.at[step - 1],
                spread_land.at[step - 1],
                other(step),
            )
            for step in range(1, devices)
        ]

    def trade_landing(step):
        back = lax.rem(me + devices - step, devices)
        return remote(
            blocks_ref.at[back], arrived_ref.at[back], trade_send.at[step - 1], trade_land.at[step - 1], back
        )

    def spread_landing(step):
        back = lax.rem(me + devices - step, devices)
        return remote(
            gathered_ref.at[me], gathered_ref.at[back], spread_send.at[step - 1], spread_land.at[step - 1], back
        )

    groups = [[i for i in range(pieces) if plan[i][3] == order] for order in (A, B)]
    for rank in range(2):
        for group in groups:
            if rank < len(group):
                start(sends(group[rank], 0))
                load(group[rank]).start()
    start(trades())
    own_block = pltpu.make_async_copy(blocks_ref.at[me], arrived_ref.at[me], own_sem)
    own_block.start()

    def finish(piece):
        settle(piece, 2)
        add(piece, 2)
        array, first, width, order = plan[piece]
        if array < counts[1]:
            outs[array][:, first : first + width] = kept(piece, 3)[...]
        else:
            gathered_ref[me] = kept(piece, 3)[...]
            start(spreads())

    rounds = max(len(group) for group in groups)
    for turn in range(rounds + 2):
        for group in groups:
            if turn < len(group):
                piece = group[turn]
                settle(piece, 0)
                if turn + 2 < len(group):
                    start(sends(group[turn + 2], 0))
                    load(group[turn + 2]).start()
                load(piece).wait()
                add(piece, 0)
                start(sends(piece, 1))
            if 0 <= turn - 1 < len(group):
                piece = group[turn - 1]
                settle(piece, 1)
                add(piece, 1)
                start(sends(piece, 2))
            if 0 <= turn - 2 < len(group):
                finish(group[turn - 2])

    for piece in range(pieces):
        for phase in range(3):
            for copy in sends(piece, phase):
                copy.wait_send()
    own_block.wait()
    for copy in trades():
        copy.wait_send()
    for copy in spreads():
        copy.wait_send()
    for step in range(1, devices):
        trade_landing(step).wait_recv()
        spread_landing(step).wait_recv()


def sum_and_trade(arrays, plan, extra, blocks):
    devices = lax.axis_size("rows")
    sides = factors(devices)
    rows = arrays[0].shape[0] // devices
    plan = plan + [(len(arrays), 0, extra.shape[1], B)]
    operands = [array.reshape(*sides, rows, array.shape[1]) for array in (*arrays, extra)]
    owns, lands = [], []
    for array, first, width, order in plan:
        left = [0, 1, 2]
        for which in order:
            left.remove(which)
            shape = tuple(sides[d] for d in left) + (rows, width)
            if which == order[0]:
                owns.append(pltpu.VMEM(shape, bf16))
            lands.append(pltpu.VMEM((max(sides[which] - 1, 1),) + shape, bf16))
    copies = len(plan) * 3 * (max(sides) - 1)
    return pl.pallas_call(
        functools.partial(sum_kernel, tuple(sides), tuple(plan), (len(operands), len(arrays))),
        in_specs=[pl.BlockSpec(memory_space=pl.ANY)] * (len(operands) + 1),
        out_specs=[pl.BlockSpec(memory_space=pltpu.VMEM)] * (len(arrays) + 1) + [pl.BlockSpec(memory_space=pl.ANY)],
        out_shape=[jax.ShapeDtypeStruct((rows, array.shape[1]), bf16) for array in arrays]
        + [
            jax.ShapeDtypeStruct((devices, rows, extra.shape[1]), bf16),
            jax.ShapeDtypeStruct(blocks.shape, blocks.dtype),
        ],
        scratch_shapes=[
            *owns,
            *lands,
            pltpu.SemaphoreType.DMA((copies,)),
            pltpu.SemaphoreType.DMA((copies,)),
            pltpu.SemaphoreType.DMA((len(plan),)),
            pltpu.SemaphoreType.DMA((devices - 1,)),
            pltpu.SemaphoreType.DMA((devices - 1,)),
            pltpu.SemaphoreType.DMA((devices - 1,)),
            pltpu.SemaphoreType.DMA((devices - 1,)),
            pltpu.SemaphoreType.DMA,
        ],
        compiler_params=pltpu.CompilerParams(
            collective_id=0, has_side_effects=True, vmem_limit_bytes=56 * 1024 * 1024
        ),
        cost_estimate=pl.CostEstimate(flops=10**9, bytes_accessed=6 * 10**8, transcendentals=0),
        name="sum_and_trade",
    )(*operands, blocks)


def swap(array):
    return lax.ppermute(array, "section", [(0, 1), (1, 0)])


def on_device(
    byte_ids,
    hash_ids,
    patch_lengths,
    row_lengths,
    byte_table,
    hash_tables,
    norm_gains,
    w_qkv,
    w_out,
    w_gate_up,
    w_down,
    cotangent,
):
    section = lax.axis_index("section")
    first_core = section == 0
    devices = lax.axis_size("rows")
    count_tables, shard_rows, half_width = hash_tables.shape
    positions = M * L

    def both(array):
        return lax.all_gather(array, "section", axis=0, tiled=True)

    flat_ids = hash_ids.reshape(positions, count_tables).T
    owners = flat_ids // shard_rows
    local_rows = flat_ids % shard_rows + jnp.arange(count_tables, dtype=jnp.int32)[:, None] * shard_rows
    order_key = owners * positions + jnp.arange(positions, dtype=jnp.int32)[None, :]
    order_key, grouped = lax.sort((order_key, local_rows), dimension=1, num_keys=1)

    def by_owner(array):
        return array.reshape(count_tables, devices, -1).transpose(1, 0, 2).reshape(devices, -1)

    slots = by_owner(order_key % positions).reshape(-1)
    requested = lax.all_to_all(by_owner(grouped), "rows", split_axis=0, concat_axis=0, tiled=True)
    flat_tables = hash_tables.reshape(count_tables * shard_rows, half_width)
    found_rows = flat_tables.at[requested].get(mode="promise_in_bounds")
    returned = lax.all_to_all(found_rows, "rows", split_axis=0, concat_axis=0, tiled=True)

    gains = both(norm_gains).astype(f32)
    qkv_both, out_both = both(w_qkv), both(w_out)
    gate_up_both, down_both = both(w_gate_up), both(w_down)

    lengths = lax.dynamic_index_in_dim(patch_lengths, section, 0, keepdims=False)
    row_length = lax.dynamic_index_in_dim(row_lengths, section, 0, keepdims=False)
    starts = jnp.cumsum(lengths) - lengths
    byte_positions = jnp.arange(L, dtype=jnp.int32)
    byte_patch = jnp.sum((starts[:, None] <= byte_positions[None, :]).astype(jnp.int32), axis=0) - 1
    patch_row, patch_col = byte_patch[None, :], byte_patch[:, None]
    patches = jnp.arange(P_SIZE, dtype=jnp.int32)
    member = (patches[:, None] == patch_row).astype(bf16)
    member_byte = (patches[None, :] == patch_col).astype(bf16)
    counts = lengths.astype(f32)[:, None]
    valid = (patches < row_length)[:, None]

    own_cotangent = lax.dynamic_index_in_dim(cotangent[0], section, 0, keepdims=False)
    sent_cotangent = swap(lax.dynamic_index_in_dim(cotangent[0], 1 - section, 0, keepdims=False))
    cotangent_one = jnp.where(first_core, own_cotangent, sent_cotangent).astype(f32)
    cotangent_two = jnp.where(first_core, sent_cotangent, own_cotangent).astype(f32)

    flat_bytes = byte_ids.reshape(positions)
    table_rows = byte_table.shape[0]
    padded = jnp.pad(byte_table, ((0, -table_rows % 128), (0, 0)))
    own_half = combine(
        slots[None, :], flat_bytes[:, None], returned.reshape(-1, half_width), padded
    ).reshape(M, L, half_width)
    kept_half = lax.dynamic_index_in_dim(own_half, section, 0, keepdims=False)
    sent_half = swap(lax.dynamic_index_in_dim(own_half, 1 - section, 0, keepdims=False))
    byte_rows = jnp.concatenate(
        [jnp.where(first_core, kept_half, sent_half), jnp.where(first_core, sent_half, kept_half)], axis=1
    )

    pooled = dot(member, byte_rows) / counts
    normed_one, inverse_one = normalize(pooled, gains[0, 0])
    queries_one = dot(normed_one, qkv_both[0, :, :D]).astype(bf16)
    byte_pairs = dot(byte_rows, qkv_both[0, :, D:]).astype(bf16)
    attention_one, attended_one = patch_attention(patch_row, patch_col, queries_one, byte_pairs)
    middle_one = pooled + dot(attended_one, out_both[0])
    result_one, kept_one = feed_forward(middle_one, gains[0, 1], gate_up_both[0], down_both[0])
    encoded = jnp.where(valid, result_one, pooled).astype(bf16)

    inputs_two = encoded.astype(f32)
    normed_two, inverse_two = normalize(inputs_two, gains[1, 0])
    mixed = dot(normed_two, qkv_both[1]).astype(bf16)
    attended_two = causal_attention(mixed)
    middle_two = inputs_two + dot(attended_two, out_both[1])
    result_two, kept_two = feed_forward(middle_two, gains[1, 1], gate_up_both[1], down_both[1])
    final = jnp.where(valid, result_two, inputs_two).astype(bf16)
    sent_out = swap(jnp.where(first_core, final, encoded))
    kept_out = jnp.where(first_core, encoded, final)
    section_out = jnp.where(
        first_core, jnp.stack([kept_out, sent_out]), jnp.stack([sent_out, kept_out])
    )[None]

    def share(left, right):
        width = right.shape[1] // 2
        mine = lax.dynamic_slice_in_dim(right, section * width, width, axis=1)
        theirs = lax.dynamic_slice_in_dim(right, (1 - section) * width, width, axis=1)
        lefts = jnp.concatenate([left, swap(left)], axis=0)
        rights = jnp.concatenate([mine, swap(theirs)], axis=0)
        return dot_tn(lefts, rights).astype(bf16)

    grad_kept = jnp.where(valid, cotangent_two, 0.0)
    grad_middle, gain_two_second, grad_joined, grad_branch = feed_back(
        middle_two, gains[1, 1], gate_up_both[1], down_both[1], kept_two, grad_kept
    )
    gate_up_two = share(kept_two[0], grad_joined)
    down_two = share(grad_branch, kept_two[3])
    grad_low = grad_middle.astype(bf16)
    grad_attended = dot_nt(grad_low, out_both[1]).astype(bf16)
    grad_mixed = jnp.concatenate(causal_attention_back(mixed, grad_attended), axis=1)
    rest_two = jnp.concatenate([share(normed_two, grad_mixed), share(attended_two, grad_low)], axis=1)
    grad_normed = dot_nt(grad_mixed, qkv_both[1])
    grad_in, gain_two_first = normalize_back(inputs_two, gains[1, 0], inverse_two, grad_normed)
    grad_encoded = jnp.where(valid, 0.0, cotangent_two) + grad_middle + grad_in


    grad_out = cotangent_one + grad_encoded.astype(bf16).astype(f32)
    grad_kept = jnp.where(valid, grad_out, 0.0)
    grad_middle, gain_one_second, grad_joined, grad_branch = feed_back(
        middle_one, gains[0, 1], gate_up_both[0], down_both[0], kept_one, grad_kept
    )
    gate_up_one = share(kept_one[0], grad_joined)
    down_one = share(grad_branch, kept_one[3])
    grad_low = grad_middle.astype(bf16)
    grad_attended = dot_nt(grad_low, out_both[0]).astype(bf16)
    grad_queries, grad_keys, grad_values = patch_attention_back(
        patch_row, patch_col, queries_one, byte_pairs, attention_one, grad_attended
    )
    grad_pairs = jnp.concatenate([grad_keys, grad_values], axis=1)
    grad_normed = dot_nt(grad_queries, qkv_both[0, :, :D])
    grad_in, gain_one_first = normalize_back(pooled, gains[0, 0], inverse_one, grad_normed)
    grad_pooled = jnp.where(valid, 0.0, grad_out) + grad_middle + grad_in
    grad_bytes = dot(member_byte, (grad_pooled / counts).astype(bf16))
    grad_bytes = (grad_bytes + dot_nt(grad_pairs, qkv_both[0, :, D:])).astype(bf16)


    grad_halves = grad_bytes.reshape(L, 2, half_width)
    kept_grad = lax.dynamic_index_in_dim(grad_halves, section, 1, keepdims=False)
    sent_grad = swap(lax.dynamic_index_in_dim(grad_halves, 1 - section, 1, keepdims=False))
    own_grad = jnp.where(
        first_core,
        jnp.concatenate([kept_grad, sent_grad], axis=0),
        jnp.concatenate([sent_grad, kept_grad], axis=0),
    )
    rest_one = jnp.concatenate(
        [share(normed_one, grad_queries), share(byte_rows, grad_pairs), share(attended_one, grad_low)], axis=1
    )
    slot_grads = spread(slots[:, None], own_grad).reshape(devices, -1, half_width)
    words = (flat_bytes[:, None] == jnp.arange(table_rows, dtype=jnp.int32)[None, :]).astype(bf16)
    table_part = dot_tn(words, own_grad).reshape(D, -1)
    gain_part = jnp.stack([gain_one_first, gain_one_second, gain_two_first, gain_two_second], axis=1)
    gain_part = gain_part + swap(gain_part)
    table_columns = table_part.shape[1]
    extra = jnp.concatenate([table_part, gain_part], axis=1)
    extra = jnp.pad(extra, ((0, 0), (0, -extra.shape[1] % 128))).astype(bf16)

    plan = []
    for array in (0, 3):
        width = FF // 2
        plan += [(array, 0, width, A), (array, width, width, A), (array + 1, 0, width, B)]
        plan += [(array + 2, 0, D, B), (array + 2, D, D, B)]
    sums = sum_and_trade(
        [gate_up_two, down_two, rest_two, gate_up_one, down_one, rest_one], plan, extra, slot_grads
    )
    gate_up_two, down_two, rest_two, gate_up_one, down_one, rest_one, gathered, arrived = sums
    hash_grad = jax.ops.segment_sum(
        arrived.reshape(-1, half_width).astype(f32),
        requested.reshape(-1),
        num_segments=count_tables * shard_rows,
    ).reshape(count_tables, shard_rows, half_width)
    byte_table_grad = gathered[:, :, :table_columns].reshape(table_rows, half_width).astype(f32)
    gain_sums = lax.dynamic_index_in_dim(gathered, lax.axis_index("rows"), 0, keepdims=False)
    gain_sums = gain_sums[:, table_columns : table_columns + 4].T.reshape(2, 2, -1).astype(f32)
    gains_grad = lax.dynamic_index_in_dim(gain_sums, section, 0, keepdims=True)

    sums_one = jnp.concatenate([gate_up_one, down_one, rest_one], axis=1)
    sums_two = jnp.concatenate([gate_up_two, down_two, rest_two], axis=1)
    kept_sums = jnp.where(first_core, sums_one, sums_two)
    sent_sums = swap(jnp.where(first_core, sums_two, sums_one))
    lower = jnp.where(first_core, kept_sums, sent_sums).astype(f32)
    upper = jnp.where(first_core, sent_sums, kept_sums).astype(f32)
    half_ff = FF // 2
    gate_up_grad = jnp.concatenate([lower[:, :FF], upper[:, :FF]], axis=1)
    down_grad = jnp.concatenate([lower[:, FF : FF + half_ff], upper[:, FF : FF + half_ff]], axis=1).T
    low_rest, high_rest = lower[:, FF + half_ff :], upper[:, FF + half_ff :]
    half = D // 2
    out_grad = jnp.concatenate([low_rest[:, -half:], high_rest[:, -half:]], axis=1)
    pieces_one = [low_rest[:, :half], high_rest[:, :half], low_rest[:, half : 3 * half], high_rest[:, half : 3 * half]]
    pieces_two = [low_rest[:, : 3 * half], high_rest[:, : 3 * half]]
    qkv_grad = jnp.where(
        first_core, jnp.concatenate(pieces_one, axis=1), jnp.concatenate(pieces_two, axis=1)
    )

    return (
        section_out,
        byte_table_grad,
        hash_grad,
        gains_grad,
        qkv_grad[None],
        out_grad[None],
        gate_up_grad[None],
        down_grad[None],
    )


def solution(mesh):
    return jax.shard_map(
        on_device,
        mesh=mesh,
        in_specs=(
            P("rows", None),
            P("rows", None, None),
            P("rows", None),
            P("rows"),
            P(None, "section"),
            P(None, "rows", "section"),
            P("section", None, None),
            P("section", None, None),
            P("section", None, None),
            P("section", None, None),
            P("section", None, None),
            P("section", "rows", None, None),
        ),
        out_specs=(
            P("section", "rows", None, None),
            P(None, "section"),
            P(None, "rows", "section"),
            P("section", None, "rows"),
            P("section", "rows", None),
            P("section", "rows", None),
            P("section", "rows", None),
            P("section", None, "rows"),
        ),
        check_vma=False,
    )
```

```python
import functools

import jax
import jax.numpy as jnp
from jax import lax
from jax.experimental import pallas as pl
from jax.experimental.pallas import tpu as pltpu
from jax.sharding import PartitionSpec as P

D = 1024
HEADS = 16
HEAD = 64
FF = 2816
L = 1024
MOST = 16
M = 2
P_SIZE = 256
GROUP = 512
VMEM_BYTES = 48 * 1024 * 1024

epsilon = 1e-05
f32 = jnp.float32
bf16 = jnp.bfloat16


def dot(left, right):
    return jnp.dot(left, right, preferred_element_type=f32)


def dot_nt(left, right):
    return lax.dot_general(left, right, (((1,), (1,)), ((), ())), preferred_element_type=f32)


def dot_tn(left, right):
    return lax.dot_general(left, right, (((0,), (0,)), ((), ())), preferred_element_type=f32)


def params(*semantics):
    return pltpu.CompilerParams(vmem_limit_bytes=VMEM_BYTES, dimension_semantics=semantics)


def combine_kernel(slots_ref, ids_ref, rows_ref, table_ref, out_ref):
    tile = out_ref.shape[0]
    first = pl.program_id(0) * tile
    places = first + lax.broadcasted_iota(jnp.int32, (tile, slots_ref.shape[1]), 0)
    chosen = (places == slots_ref[...]).astype(f32).astype(bf16)
    words = lax.broadcasted_iota(jnp.int32, (tile, table_ref.shape[0]), 1)
    word = (words == ids_ref[...]).astype(f32).astype(bf16)
    total = dot(chosen, rows_ref[...]) + dot(word, table_ref[...])
    out_ref[...] = total.astype(bf16)


def combine(slots, ids, rows, table):
    count, width = rows.shape
    positions = ids.shape[0]
    tile = 256
    return pl.pallas_call(
        combine_kernel,
        grid=(positions // tile,),
        in_specs=[
            pl.BlockSpec((1, count), lambda i: (0, 0)),
            pl.BlockSpec((tile, 1), lambda i: (i, 0)),
            pl.BlockSpec((count, width), lambda i: (0, 0)),
            pl.BlockSpec(table.shape, lambda i: (0, 0)),
        ],
        out_specs=pl.BlockSpec((tile, width), lambda i: (i, 0)),
        out_shape=jax.ShapeDtypeStruct((positions, width), bf16),
        compiler_params=params("arbitrary"),
        cost_estimate=pl.CostEstimate(
            flops=2 * positions * count * width, bytes_accessed=12 * count * width // 4, transcendentals=0
        ),
        name="combine_rows",
    )(slots, ids, rows, table)


def head_marks(heads, width):
    feature = lax.shift_right_logical(lax.broadcasted_iota(jnp.int32, (heads, width), 1), 6)
    return (feature == lax.broadcasted_iota(jnp.int32, (heads, width), 0)).astype(f32).astype(bf16)


def patch_marks(patch_row_ref, patch_col_ref):
    by_patch = (
        lax.broadcasted_iota(jnp.int32, (P_SIZE, L), 0) == patch_row_ref[...]
    ).astype(f32).astype(bf16)
    by_byte = (
        lax.broadcasted_iota(jnp.int32, (L, P_SIZE), 1) == patch_col_ref[...]
    ).astype(f32).astype(bf16)
    return by_patch, by_byte


def per_head(marks, products):
    high = products.astype(bf16)
    low = (products - high.astype(f32)).astype(bf16)
    return dot_nt(marks, high) + dot_nt(marks, low)


def neighbours(patches, heads):
    wide = jnp.broadcast_to(patches, (heads, L))
    back = [(d, pltpu.roll(wide, d, 1) == wide) for d in (1, 2, 4, 8)]
    ahead = [(L - d, pltpu.roll(wide, L - d, 1) == wide) for d in (1, 2, 4, 8)]
    return back, ahead


def scan_max(values, steps):
    for distance, same in steps:
        values = jnp.where(same, jnp.maximum(values, pltpu.roll(values, distance, 1)), values)
    return values


def scan_sum(values, steps):
    for distance, same in steps:
        values = jnp.where(same, values + pltpu.roll(values, distance, 1), values)
    return values


def patch_attention_kernel(
    patch_row_ref, patch_col_ref, query_ref, key_ref, value_ref, attention_ref, attended_ref
):
    heads, width = attention_ref.shape[0], query_ref.shape[1]
    marks = head_marks(heads, width)
    by_patch, by_byte = patch_marks(patch_row_ref, patch_col_ref)
    queries = dot(by_byte, query_ref[...])
    scores = per_head(marks, queries * key_ref[...].astype(f32)) * 0.125
    back, ahead = neighbours(patch_row_ref[...], heads)
    top = scan_max(scan_max(scores, back), ahead)
    shifted = jnp.exp(scores - top)
    total = scan_sum(shifted, back) + scan_sum(shifted, ahead) - shifted
    attention = shifted / total
    attention_ref[...] = attention
    weights = dot_tn(attention.astype(bf16), marks)
    weighted = (weights * value_ref[...].astype(f32)).astype(bf16)
    attended_ref[...] = dot(by_patch, weighted).astype(bf16)


def patch_attention(patch_row, patch_col, queries, key_value):
    groups = D // GROUP
    return pl.pallas_call(
        patch_attention_kernel,
        grid=(groups,),
        in_specs=[
            pl.BlockSpec((1, L), lambda i: (0, 0)),
            pl.BlockSpec((L, 1), lambda i: (0, 0)),
            pl.BlockSpec((P_SIZE, GROUP), lambda i: (0, i)),
            pl.BlockSpec((L, GROUP), lambda i: (0, i)),
            pl.BlockSpec((L, GROUP), lambda i: (0, i + groups)),
        ],
        out_specs=[
            pl.BlockSpec((HEADS // groups, L), lambda i: (i, 0)),
            pl.BlockSpec((P_SIZE, GROUP), lambda i: (0, i)),
        ],
        out_shape=[
            jax.ShapeDtypeStruct((HEADS, L), f32),
            jax.ShapeDtypeStruct((P_SIZE, D), bf16),
        ],
        compiler_params=params("arbitrary"),
        cost_estimate=pl.CostEstimate(flops=4 * 10**9, bytes_accessed=6 * 10**6, transcendentals=16384),
        name="patch_attention",
    )(patch_row, patch_col, queries, key_value, key_value)


def patch_attention_back_kernel(
    patch_row_ref,
    patch_col_ref,
    query_ref,
    key_ref,
    value_ref,
    attention_ref,
    grad_ref,
    grad_query_ref,
    grad_pair_ref,
):
    heads, width = attention_ref.shape[0], query_ref.shape[1]
    first = pl.multiple_of(pl.program_id(0) * width, width)
    marks = head_marks(heads, width)
    by_patch, by_byte = patch_marks(patch_row_ref, patch_col_ref)
    grads = dot(by_byte, grad_ref[...])
    attention = attention_ref[...]
    grad_attention = per_head(marks, grads * value_ref[...].astype(f32))
    weights = dot_tn(attention.astype(bf16), marks)
    grad_pair_ref[:, pl.ds(D + first, width)] = (weights * grads).astype(bf16)
    back, ahead = neighbours(patch_row_ref[...], heads)
    terms = attention * grad_attention
    total = scan_sum(terms, back) + scan_sum(terms, ahead) - terms
    grad_scores = (attention * (grad_attention - total)).astype(bf16)
    spread_scores = dot_tn(grad_scores, marks) * 0.125
    grad_pair_ref[:, pl.ds(first, width)] = (spread_scores * dot(by_byte, query_ref[...])).astype(bf16)
    weighted = (spread_scores * key_ref[...].astype(f32)).astype(bf16)
    grad_query_ref[...] = dot(by_patch, weighted).astype(bf16)


def patch_attention_back(patch_row, patch_col, queries, key_value, attention, grad_attended):
    groups = D // GROUP
    byte_block = pl.BlockSpec((L, GROUP), lambda i: (0, i))
    patch_block = pl.BlockSpec((P_SIZE, GROUP), lambda i: (0, i))
    return pl.pallas_call(
        patch_attention_back_kernel,
        grid=(groups,),
        in_specs=[
            pl.BlockSpec((1, L), lambda i: (0, 0)),
            pl.BlockSpec((L, 1), lambda i: (0, 0)),
            patch_block,
            byte_block,
            pl.BlockSpec((L, GROUP), lambda i: (0, i + groups)),
            pl.BlockSpec((HEADS // groups, L), lambda i: (i, 0)),
            patch_block,
        ],
        out_specs=[patch_block, pl.BlockSpec((L, 2 * D), lambda i: (0, 0))],
        out_shape=[
            jax.ShapeDtypeStruct((P_SIZE, D), bf16),
            jax.ShapeDtypeStruct((L, 2 * D), bf16),
        ],
        compiler_params=params("arbitrary"),
        cost_estimate=pl.CostEstimate(flops=6 * 10**9, bytes_accessed=10 * 10**6, transcendentals=0),
        name="patch_attention_back",
    )(patch_row, patch_col, queries, key_value, key_value, attention, grad_attended)


def causal_softmax(queries, keys):
    scores = dot_nt(queries, keys) * 0.125
    size = scores.shape[0]
    allowed = lax.broadcasted_iota(jnp.int32, (size, size), 0) >= lax.broadcasted_iota(
        jnp.int32, (size, size), 1
    )
    scores = jnp.where(allowed, scores, -jnp.inf)
    shifted = jnp.exp(scores - jnp.max(scores, axis=-1, keepdims=True))
    return shifted / jnp.sum(shifted, axis=-1, keepdims=True)


def pair_masks(shape):
    lane = lax.broadcasted_iota(jnp.int32, shape, 1)
    return [lane < HEAD, lane >= HEAD]


def causal_kernel(query_ref, key_ref, value_ref, out_ref):
    queries, keys, values = query_ref[...], key_ref[...], value_ref[...]
    masks = pair_masks(queries.shape)
    parts = []
    for mask in masks:
        attention = causal_softmax(jnp.where(mask, queries, 0), keys).astype(bf16)
        parts.append(dot(attention, values))
    out_ref[...] = jnp.where(masks[0], parts[0], parts[1]).astype(bf16)


def causal_attention(mixed):
    pairs = HEADS // 2
    return pl.pallas_call(
        causal_kernel,
        grid=(pairs,),
        in_specs=[
            pl.BlockSpec((P_SIZE, 2 * HEAD), lambda i: (0, i)),
            pl.BlockSpec((P_SIZE, 2 * HEAD), lambda i: (0, i + pairs)),
            pl.BlockSpec((P_SIZE, 2 * HEAD), lambda i: (0, i + 2 * pairs)),
        ],
        out_specs=pl.BlockSpec((P_SIZE, 2 * HEAD), lambda i: (0, i)),
        out_shape=jax.ShapeDtypeStruct((P_SIZE, D), bf16),
        compiler_params=params("arbitrary"),
        cost_estimate=pl.CostEstimate(flops=2 * 10**9, bytes_accessed=2 * 10**6, transcendentals=10**6),
        name="causal_attention",
    )(mixed, mixed, mixed)


def causal_back_kernel(query_ref, key_ref, value_ref, grad_ref, out_ref):
    pair = pl.program_id(0) * 2 * HEAD
    queries, keys, values, grads = query_ref[...], key_ref[...], value_ref[...], grad_ref[...]
    masks = pair_masks(queries.shape)
    results = []
    for mask in masks:
        attention = causal_softmax(jnp.where(mask, queries, 0), keys)
        grad_attention = dot_nt(jnp.where(mask, grads, 0), values)
        total = jnp.sum(attention * grad_attention, axis=-1, keepdims=True)
        grad_scores = (attention * (grad_attention - total)).astype(bf16)
        results.append(
            (
                dot(grad_scores, keys) * 0.125,
                dot_tn(grad_scores, queries) * 0.125,
                dot_tn(attention.astype(bf16), grads),
            )
        )
    for index, (first, second) in enumerate(zip(results[0], results[1])):
        columns = pl.ds(pl.multiple_of(index * D + pair, 2 * HEAD), 2 * HEAD)
        out_ref[:, columns] = jnp.where(masks[0], first, second).astype(bf16)


def causal_attention_back(mixed, grad_attended):
    pairs = HEADS // 2
    block = pl.BlockSpec((P_SIZE, 2 * HEAD), lambda i: (0, i))
    return pl.pallas_call(
        causal_back_kernel,
        grid=(pairs,),
        in_specs=[
            block,
            pl.BlockSpec((P_SIZE, 2 * HEAD), lambda i: (0, i + pairs)),
            pl.BlockSpec((P_SIZE, 2 * HEAD), lambda i: (0, i + 2 * pairs)),
            block,
        ],
        out_specs=pl.BlockSpec((P_SIZE, 3 * D), lambda i: (0, 0)),
        out_shape=jax.ShapeDtypeStruct((P_SIZE, 3 * D), bf16),
        compiler_params=params("arbitrary"),
        cost_estimate=pl.CostEstimate(flops=4 * 10**9, bytes_accessed=4 * 10**6, transcendentals=10**6),
        name="causal_attention_back",
    )(mixed, mixed, mixed, grad_attended)


def normalize(inputs, gain):
    inverse = lax.rsqrt(jnp.mean(inputs * inputs, axis=-1, keepdims=True) + epsilon)
    return (inputs * inverse * gain).astype(bf16), inverse


def normalize_back(inputs, gain, inverse, grad_normed):
    scaled = inputs * inverse
    grad_gain = jnp.sum(grad_normed * scaled, axis=0)
    grad_scaled = grad_normed * gain
    grad_inputs = inverse * (
        grad_scaled - scaled * jnp.mean(grad_scaled * scaled, axis=-1, keepdims=True)
    )
    return grad_inputs, grad_gain


def feed_forward(hidden, gain, w_gate_up, w_down):
    normed, inverse = normalize(hidden, gain)
    joined = dot(normed, w_gate_up)
    inner = (jax.nn.silu(joined[:, :FF]) * joined[:, FF:]).astype(bf16)
    return hidden + dot(inner, w_down), (normed, inverse, joined, inner)


def feed_back(hidden, gain, w_gate_up, w_down, kept, grad_out):
    normed, inverse, joined, inner = kept
    gate, up = joined[:, :FF], joined[:, FF:]
    sigmoid = jax.nn.sigmoid(gate)
    grad_branch = grad_out.astype(bf16)
    grad_inner = dot_nt(grad_branch, w_down)
    grad_gate = grad_inner * up * sigmoid * (1.0 + gate * (1.0 - sigmoid))
    grad_up = grad_inner * gate * sigmoid
    grad_joined = jnp.concatenate([grad_gate, grad_up], axis=1).astype(bf16)
    grad_normed = dot_nt(grad_joined, w_gate_up)
    grad_in, grad_gain = normalize_back(hidden, gain, inverse, grad_normed)
    return grad_out + grad_in, grad_gain, grad_joined, grad_branch


def chip_bits(devices):
    bits = devices.bit_length() - 1
    first = tuple(reversed(range(bits)))
    return bits, {"A": first, "B": (first[1], first[0]) + first[2:], "C": first[2:4] + first[:2] + first[4:]}


def at_place(ref, axis, place):
    return ref.at[(slice(None),) * axis + (place,)]


def plan_pieces():
    ff, half = FF // 2, D // 2
    pieces = []
    for layer in (1, 0):
        pieces += [
            (layer, "A", [("gate_up", 0, ff)]),
            (layer, "A", [("gate_up", ff, ff)]),
            (layer, "B", [("down", 0, ff)]),
            (layer, "B", [("query", 0, half), ("key", 0, half)]),
            (layer, "C", [("value", 0, half), ("out", 0, half)]),
        ]
    return pieces


def backward_kernel(devices, table_rows, *refs):
    bits, orders = chip_bits(devices)
    half, ff = D // 2, FF // 2
    rows = D // devices
    table_block = table_block_rows(devices, table_rows)
    plan = plan_pieces()
    extra = len(plan)
    pieces = extra + 1
    names = [piece[1] for piece in plan] + ["C"]
    widths = [sum(width for _, _, width in piece[2]) for piece in plan] + [half]

    layers, refs = {1: refs[:8], 0: refs[8:16]}, refs[16:]
    bytes_ref, pairs_ref, grad_ref, slots_ref, ids_ref, gains_ref = refs[:6]
    sums_ref, theirs_ref, gathered_ref, arrived_ref, staged_ref = refs[6:11]
    refs = refs[11:]
    landed, refs = {1: refs[:8], 0: refs[8:16]}, refs[16:]
    bytes_landed, pairs_landed, refs = refs[0], refs[1], refs[2:]
    owns, refs = refs[:pieces], refs[pieces:]
    lands, refs = [refs[bits * i : bits * i + bits] for i in range(pieces)], refs[bits * pieces :]
    left_ref, right_ref, total_ref, send_ref, extra_ref, own_ref, slot_ref, block_ref = refs[:8]
    swap_send, swap_land, load_sems, grad_sems, slot_sems, block_sems, refs = *refs[8:14], refs[14:]
    send_sems, land_sems, trade_send, trade_land, spread_send, spread_land, last_sems = refs

    me = lax.axis_index("rows")
    section = lax.axis_index("section")
    partner = 1 - section
    places = [(me // 2 ** (bits - 1 - d)) % 2 for d in range(bits)]
    peers = [me + (1 - 2 * places[d]) * 2 ** (bits - 1 - d) for d in range(bits)]

    def other(step):
        return lax.rem(me + step, devices)

    barrier = pltpu.get_barrier_semaphore()
    mesh_id = pl.DeviceIdType.MESH
    pl.semaphore_signal(barrier, inc=1, device_id={"section": partner}, device_id_type=mesh_id)
    for step in range(1, devices):
        pl.semaphore_signal(barrier, inc=1, device_id={"rows": other(step)}, device_id_type=mesh_id)
    pl.semaphore_wait(barrier, devices)

    def remote(source, target, send, land, **device):
        return pltpu.make_async_remote_copy(
            src_ref=source, dst_ref=target, send_sem=send, recv_sem=land, device_id=device, device_id_type=mesh_id
        )

    def part_of(array, index, core):
        size = array.shape[1]
        if size == 3 * D:
            first = index * D + core * half
        elif size == 2 * D:
            first = index * D + core * half
        else:
            first = core * (size // 2)
            return array.at[:, pl.ds(pl.multiple_of(first, 128), size // 2)]
        return array.at[:, pl.ds(pl.multiple_of(first, 128), half)]

    swaps = {}

    def swap_of(key, source, target):
        slot = len(swaps)
        swaps[key] = remote(source, target, swap_send.at[slot], swap_land.at[slot], section=partner)
        swaps[key].start()

    def swap_layer(layer, which):
        for index in which:
            array, target = layers[layer][index], landed[layer][index]
            if index < 4:
                swap_of((layer, index, 0), array, target)
            else:
                wide = array.shape[1] // D if index == 4 else 1
                for part in range(wide):
                    there = target.at[:, pl.ds(part * half, half)] if index == 4 else target
                    swap_of((layer, index, part), part_of(array, part, partner), there)

    ready = set()

    def settled(key):
        if key not in ready:
            ready.add(key)
            swaps[key].wait_recv()

    swap_layer(1, (2, 6, 3, 7))
    own_rows = own_ref.at[pl.ds(pl.multiple_of(section * L, L), L)]
    swap_of(("grads",), grad_ref.at[:, pl.ds(pl.multiple_of(partner * half, half), half)], own_rows)
    own_copy = pltpu.make_async_copy(
        grad_ref.at[:, pl.ds(pl.multiple_of(section * half, half), half)], own_rows, grad_sems
    )
    own_copy.start()
    swap_layer(1, (0, 1, 4, 5))
    swap_layer(0, (2, 6, 3, 7, 0, 1, 4, 5))
    swap_of(("bytes",), bytes_ref, bytes_landed)
    for part in range(2):
        swap_of(
            ("pairs", part), part_of(pairs_ref, part, partner), pairs_landed.at[:, pl.ds(part * half, half)]
        )

    def jobs_of(piece):
        layer, _, segments = plan[piece]
        own, land = layers[layer], landed[layer]
        result, column = [], 0
        for kind, first, width in segments:
            if layer == 0 and kind in ("key", "value"):
                part = 0 if kind == "key" else 1
                for chunk in range(4):
                    depth = pl.ds(chunk % 2 * 512, 512)
                    if chunk < 2:
                        left, right = bytes_ref, part_of(pairs_ref, part, section)
                        keys = []
                    else:
                        left, right = bytes_landed, pairs_landed.at[:, pl.ds(part * half, half)]
                        keys = [("bytes",), ("pairs", part)]
                    copies = [("left", left.at[depth], 0, 512), ("right", right.at[depth], 0, 512)]
                    result.append((piece, column, width, chunk, 4, keys, copies))
            else:
                index, other_index, part = {
                    "gate_up": (2, 6, 0),
                    "down": (3, 7, 0),
                    "query": (0, 4, 0),
                    "key": (0, 4, 1),
                    "value": (0, 4, 2),
                    "out": (1, 5, 0),
                }[kind]
                if other_index == 4:
                    right = part_of(own[4], part, section)
                    right_landed = land[4].at[:, pl.ds(part * half, half)]
                elif kind == "gate_up":
                    start = pl.multiple_of(section * FF + first, 128)
                    right = own[6].at[:, pl.ds(start, width)]
                    right_landed = land[6].at[:, pl.ds(first, width)]
                else:
                    right, right_landed = part_of(own[other_index], 0, section), land[other_index]
                copies = [
                    ("left", own[index], 0, P_SIZE),
                    ("left", land[index], P_SIZE, P_SIZE),
                    ("right", right, 0, P_SIZE),
                    ("right", right_landed, P_SIZE, P_SIZE),
                ]
                keys = [(layer, index, 0), (layer, other_index, part)]
                result.append((piece, column, width, 0, 1, keys, copies))
            column += width
        return result

    groups = [[i for i in range(pieces) if names[i] == name] for name in "ABC"]
    order_made = []
    for rank in range(max(len(group) for group in groups)):
        order_made += [group[rank] for group in groups if rank < len(group)]
    jobs = [job for piece in order_made if piece != extra for job in jobs_of(piece)]

    def loads(number):
        piece, column, width, chunk, chunks, keys, copies = jobs[number]
        slot = number % 2
        result = []
        for index, (side, source, first, count) in enumerate(copies):
            buffer = left_ref if side == "left" else right_ref
            columns = D if side == "left" else width
            target = buffer.at[slot, pl.ds(first, count), pl.ds(0, columns)]
            result.append(pltpu.make_async_copy(source, target, load_sems.at[slot, index]))
        return result

    def start_loads(number):
        if number < len(jobs):
            for key in jobs[number][5]:
                settled(key)
            for copy in loads(number):
                copy.start()

    slots_of = {piece: index % send_ref.shape[0] for index, piece in enumerate(order_made) if piece != extra}

    def sent_part(piece):
        if piece == extra:
            return extra_ref
        return send_ref.at[slots_of[piece]].at[(slice(None),) * bits + (pl.ds(0, widths[piece]),)]

    def store(piece, device, value, column, width):
        axis = orders[names[piece]][0]
        at = [(device // 2 ** (bits - 1 - d)) % 2 for d in range(bits)]
        bit = at.pop(axis)
        at = tuple(at) + (slice(None), pl.ds(column, width))
        target = sent_part(piece)

        @pl.when(bit == places[axis])
        def _():
            owns[piece][at] = value

        @pl.when(bit != places[axis])
        def _():
            target[at] = value

    def run_job(number):
        piece, column, width, chunk, chunks, keys, copies = jobs[number]
        slot = number % 2
        for copy in loads(number):
            copy.wait()
        start_loads(number + 1)
        tile = 128

        def body(index, carry):
            at = pl.ds(pl.multiple_of(index * tile, tile), tile)
            value = dot_tn(left_ref[slot, :, at], right_ref[slot, :, pl.ds(0, width)])
            if chunk > 0:
                value = value + total_ref[at, :]
            if chunk < chunks - 1:
                total_ref[at, :] = value
            else:
                for part in range(tile // rows):
                    block = value[part * rows : (part + 1) * rows].astype(bf16)
                    store(piece, index * (tile // rows) + part, block, column, width)
            return carry

        lax.fori_loop(0, D // tile, body, 0)

    def left_of(piece, phase):
        order = orders[names[piece]]
        return [d for d in range(bits) if d not in order[:phase]]

    def kept(piece, phase):
        order = orders[names[piece]]
        ref = owns[piece]
        for step in range(1, phase):
            ref = at_place(ref, left_of(piece, step).index(order[step]), places[order[step]])
        return ref

    def send(piece, phase):
        axis = orders[names[piece]][phase]
        if phase == 0:
            source = sent_part(piece)
        else:
            source = at_place(kept(piece, phase), left_of(piece, phase).index(axis), 1 - places[axis])
        slot = piece * bits + phase
        return remote(source, lands[piece][phase], send_sems.at[slot], land_sems.at[slot], rows=peers[axis])

    made = [0, 0]
    sent = set()

    def make(piece):
        if piece == extra:
            make_extra()
        else:
            index = order_made.index(piece)
            count = send_ref.shape[0]
            earlier = [p for p in order_made[:index] if p != extra and slots_of[p] == slots_of[piece]]
            if earlier and (earlier[-1], 0) not in sent:
                sent.add((earlier[-1], 0))
                send(earlier[-1], 0).wait_send()
            while made[0] < len(jobs) and jobs[made[0]][0] == piece:
                run_job(made[0])
                made[0] += 1
        send(piece, 0).start()

    def make_extra():
        tile = table_block
        first_gain = table_rows // 16 * 16
        positions = M * L

        def body(index, carry):
            words = index * tile + lax.broadcasted_iota(jnp.int32, (tile, positions), 0)
            chosen = (words == ids_ref[...]).astype(f32).astype(bf16)
            value = dot(chosen, own_ref[...])
            row = index * tile + lax.broadcasted_iota(jnp.int32, (tile, half), 0)
            gains = jnp.concatenate([gains_ref[...]] * (tile // 16), axis=0)
            inside = (row >= first_gain) & (row < first_gain + 16)
            value = value + jnp.where(inside, gains, 0.0)
            store(extra, index, value.astype(bf16), 0, half)
            return carry

        lax.fori_loop(0, devices, body, 0)

    def add(piece, phase):
        target = kept(piece, phase + 1)
        land = lands[piece][phase]
        leads = len(target.shape) - 2
        count = 16
        groups_in = target.shape[-2] // count

        def body(index, carry):
            at = (pl.ds(pl.multiple_of(index % groups_in * count, count), count), slice(None))
            lead = index // groups_in
            at = tuple((lead // 2 ** (leads - 1 - d)) % 2 for d in range(leads)) + at
            target[at] = (target[at].astype(f32) + land[at].astype(f32)).astype(bf16)
            return carry

        lax.fori_loop(0, 2**leads * groups_in, body, 0)

    block_rows = block_ref.shape[1]
    block_slots = block_ref.shape[0]

    def slot_copy(step):
        return pltpu.make_async_copy(
            slots_ref.at[pl.ds(pl.multiple_of(other(step) * block_rows, 16), block_rows)],
            slot_ref.at[step % 2],
            slot_sems.at[step % 2],
        )

    def block_copy(step):
        target = staged_ref.at[step] if step else arrived_ref.at[me]
        slot = (step - 1) % devices % block_slots
        return pltpu.make_async_copy(block_ref.at[slot], target, block_sems.at[slot])

    def trade(step):
        return remote(
            staged_ref.at[step], arrived_ref.at[me], trade_send.at[step - 1], trade_land.at[step - 1], rows=other(step)
        )

    def trade_landing(step):
        back = lax.rem(me + devices - step, devices)
        return remote(
            staged_ref.at[step], arrived_ref.at[back], trade_send.at[step - 1], trade_land.at[step - 1], rows=back
        )

    def make_blocks():
        own_copy.wait()
        settled(("grads",))
        steps = list(range(1, devices)) + [0]
        slot_copy(steps[0]).start()
        behind = block_slots - 1

        def pass_on(step):
            block_copy(step).wait()
            if step:
                trade(step).start()

        for index, step in enumerate(steps):
            if index + 1 < devices:
                slot_copy(steps[index + 1]).start()
            slot_copy(step).wait()
            if index >= behind:
                pass_on(steps[index - behind])
            where = lax.broadcasted_iota(jnp.int32, (block_rows, M * L), 1)
            chosen = (where == slot_ref[step % 2]).astype(f32).astype(bf16)
            block_ref[index % block_slots] = dot(chosen, own_ref[...]).astype(bf16)
            block_copy(step).start()
        for step in steps[devices - behind :]:
            pass_on(step)

    def spreads():
        return [
            remote(
                gathered_ref.at[me],
                gathered_ref.at[me],
                spread_send.at[step - 1],
                spread_land.at[step - 1],
                rows=other(step),
            )
            for step in range(1, devices)
        ]

    def spread_landing(step):
        back = lax.rem(me + devices - step, devices)
        return remote(
            gathered_ref.at[me], gathered_ref.at[back], spread_send.at[step - 1], spread_land.at[step - 1], rows=back
        )

    def finish(piece):
        if piece == extra:
            gathered_ref[me] = kept(piece, bits)[...]
            for copy in spreads():
                copy.start()
        else:
            layer = plan[piece][0]
            first = sum(widths[p] for p in range(piece) if plan[p][0] == layer)
            sums_ref[layer, :, first : first + widths[piece]] = kept(piece, bits)[...]

    start_loads(0)
    for group in groups:
        make(group[0])
    make_blocks()
    for group in groups:
        if len(group) > 1:
            make(group[1])
    rounds = max(len(group) for group in groups)
    for turn in range(rounds + bits - 1):
        for phase in range(bits):
            for group in groups:
                if not 0 <= turn - phase < len(group):
                    continue
                piece = group[turn - phase]
                send(piece, phase).wait_recv()
                if phase == 0 and turn + 2 < len(group):
                    make(group[turn + 2])
                add(piece, phase)
                if phase + 1 < bits:
                    send(piece, phase + 1).start()
                else:
                    finish(piece)

    last = remote(sums_ref.at[partner], theirs_ref, last_sems.at[0], last_sems.at[1], section=partner)
    last.start()
    for piece in range(pieces):
        for phase in range(bits):
            if (piece, phase) not in sent:
                send(piece, phase).wait_send()
    for key, copy in swaps.items():
        copy.wait_send()
        settled(key)
    for step in range(1, devices):
        trade(step).wait_send()
    for copy in spreads():
        copy.wait_send()
    for step in range(1, devices):
        trade_landing(step).wait_recv()
        spread_landing(step).wait_recv()
    last.wait()


def table_block_rows(devices, table_rows):
    return -(-(table_rows + 12) // (16 * devices)) * 16


def backward_sums(layer_two, layer_one, byte_rows, grad_pairs, grad_bytes, slots, ids, gains, table_rows):
    devices = lax.axis_size("rows")
    bits, orders = chip_bits(devices)
    rows = D // devices
    plan = plan_pieces()
    table_block = table_block_rows(devices, table_rows)
    half, ff = D // 2, FF // 2
    block_rows = slots.shape[0] // devices
    widths = [sum(width for _, _, width in piece[2]) for piece in plan]
    shapes = [(rows, width) for width in widths] + [(table_block, half)]
    owns, lands = [], []
    for shape in shapes:
        owns.append(pltpu.VMEM((2,) * (bits - 1) + shape, bf16))
        lands += [pltpu.VMEM((2,) * (bits - 1 - phase) + shape, bf16) for phase in range(bits)]
    total = sum(widths) // 2
    landed = []
    for layer in (layer_two, layer_one):
        for index, array in enumerate(layer):
            shape = array.shape if index < 4 else (array.shape[0], array.shape[1] // 2)
            landed.append(jax.ShapeDtypeStruct(shape, bf16))
    landed += [
        jax.ShapeDtypeStruct(byte_rows.shape, bf16),
        jax.ShapeDtypeStruct((grad_pairs.shape[0], grad_pairs.shape[1] // 2), bf16),
    ]
    swaps = 2 * 7 + 3 + 1 + 4
    copies = len(shapes) * bits
    any_space = pl.BlockSpec(memory_space=pl.ANY)
    vmem = pl.BlockSpec(memory_space=pltpu.VMEM)
    blocks = jax.ShapeDtypeStruct((devices, block_rows, half), bf16)
    dma = pltpu.SemaphoreType.DMA
    results = pl.pallas_call(
        functools.partial(backward_kernel, devices, table_rows),
        in_specs=[any_space] * 20 + [vmem] * 2,
        out_specs=[vmem, any_space, vmem] + [any_space] * (2 + len(landed)),
        out_shape=[
            jax.ShapeDtypeStruct((2, rows, total), bf16),
            jax.ShapeDtypeStruct((rows, total), bf16),
            jax.ShapeDtypeStruct((devices, table_block, half), bf16),
            blocks,
            blocks,
            *landed,
        ],
        scratch_shapes=[
            *owns,
            *lands,
            pltpu.VMEM((2, 2 * P_SIZE, D), bf16),
            pltpu.VMEM((2, 2 * P_SIZE, ff), bf16),
            pltpu.VMEM((D, half), f32),
            pltpu.VMEM((4,) + (2,) * (bits - 1) + (rows, ff), bf16),
            pltpu.VMEM((2,) * (bits - 1) + (table_block, half), bf16),
            pltpu.VMEM((M * L, half), bf16),
            pltpu.VMEM((2, block_rows, 1), jnp.int32),
            pltpu.VMEM((3, block_rows, half), bf16),
            dma((swaps,)),
            dma((swaps,)),
            dma((2, 4)),
            dma,
            dma((2,)),
            dma((3,)),
            dma((copies,)),
            dma((copies,)),
            dma((devices - 1,)),
            dma((devices - 1,)),
            dma((devices - 1,)),
            dma((devices - 1,)),
            dma((2,)),
        ],
        compiler_params=pltpu.CompilerParams(
            collective_id=0, has_side_effects=True, vmem_limit_bytes=60 * 1024 * 1024
        ),
        cost_estimate=pl.CostEstimate(flops=5 * 10**10, bytes_accessed=6 * 10**8, transcendentals=0),
        name="backward_sums",
    )(*layer_two, *layer_one, byte_rows, grad_pairs, grad_bytes, slots, ids, gains)
    return results[:4]


def swap(array):
    return lax.ppermute(array, "section", [(0, 1), (1, 0)])


def on_device(
    byte_ids,
    hash_ids,
    patch_lengths,
    row_lengths,
    byte_table,
    hash_tables,
    norm_gains,
    w_qkv,
    w_out,
    w_gate_up,
    w_down,
    cotangent,
):
    section = lax.axis_index("section")
    first_core = section == 0
    devices = lax.axis_size("rows")
    count_tables, shard_rows, half_width = hash_tables.shape
    positions = M * L

    def both(array):
        return lax.all_gather(array, "section", axis=0, tiled=True)

    flat_ids = hash_ids.reshape(positions, count_tables).T
    owners = flat_ids // shard_rows
    local_rows = flat_ids % shard_rows + jnp.arange(count_tables, dtype=jnp.int32)[:, None] * shard_rows
    order_key = owners * positions + jnp.arange(positions, dtype=jnp.int32)[None, :]
    order_key, grouped = lax.sort((order_key, local_rows), dimension=1, num_keys=1)

    def by_owner(array):
        return array.reshape(count_tables, devices, -1).transpose(1, 0, 2).reshape(devices, -1)

    slots = by_owner(order_key % positions).reshape(-1)
    requested = lax.all_to_all(by_owner(grouped), "rows", split_axis=0, concat_axis=0, tiled=True)
    flat_tables = hash_tables.reshape(count_tables * shard_rows, half_width)
    found_rows = flat_tables.at[requested].get(mode="promise_in_bounds")
    returned = lax.all_to_all(found_rows, "rows", split_axis=0, concat_axis=0, tiled=True)

    gains = both(norm_gains).astype(f32)
    qkv_both, out_both = both(w_qkv), both(w_out)
    gate_up_both, down_both = both(w_gate_up), both(w_down)

    lengths = lax.dynamic_index_in_dim(patch_lengths, section, 0, keepdims=False)
    row_length = lax.dynamic_index_in_dim(row_lengths, section, 0, keepdims=False)
    starts = jnp.cumsum(lengths) - lengths
    byte_positions = jnp.arange(L, dtype=jnp.int32)
    byte_patch = jnp.sum((starts[:, None] <= byte_positions[None, :]).astype(jnp.int32), axis=0) - 1
    patch_row, patch_col = byte_patch[None, :], byte_patch[:, None]
    patches = jnp.arange(P_SIZE, dtype=jnp.int32)
    member = (patches[:, None] == patch_row).astype(bf16)
    member_byte = (patches[None, :] == patch_col).astype(bf16)
    counts = lengths.astype(f32)[:, None]
    valid = (patches < row_length)[:, None]

    own_cotangent = lax.dynamic_index_in_dim(cotangent[0], section, 0, keepdims=False)
    sent_cotangent = swap(lax.dynamic_index_in_dim(cotangent[0], 1 - section, 0, keepdims=False))
    cotangent_one = jnp.where(first_core, own_cotangent, sent_cotangent).astype(f32)
    cotangent_two = jnp.where(first_core, sent_cotangent, own_cotangent).astype(f32)

    flat_bytes = byte_ids.reshape(positions)
    table_rows = byte_table.shape[0]
    padded = jnp.pad(byte_table, ((0, -table_rows % 128), (0, 0)))
    own_half = combine(
        slots[None, :], flat_bytes[:, None], returned.reshape(-1, half_width), padded
    ).reshape(M, L, half_width)
    kept_half = lax.dynamic_index_in_dim(own_half, section, 0, keepdims=False)
    sent_half = swap(lax.dynamic_index_in_dim(own_half, 1 - section, 0, keepdims=False))
    byte_rows = jnp.concatenate(
        [jnp.where(first_core, kept_half, sent_half), jnp.where(first_core, sent_half, kept_half)], axis=1
    )

    pooled = dot(member, byte_rows) / counts
    normed_one, inverse_one = normalize(pooled, gains[0, 0])
    queries_one = dot(normed_one, qkv_both[0, :, :D]).astype(bf16)
    byte_pairs = dot(byte_rows, qkv_both[0, :, D:]).astype(bf16)
    attention_one, attended_one = patch_attention(patch_row, patch_col, queries_one, byte_pairs)
    middle_one = pooled + dot(attended_one, out_both[0])
    result_one, kept_one = feed_forward(middle_one, gains[0, 1], gate_up_both[0], down_both[0])
    encoded = jnp.where(valid, result_one, pooled).astype(bf16)

    inputs_two = encoded.astype(f32)
    normed_two, inverse_two = normalize(inputs_two, gains[1, 0])
    mixed = dot(normed_two, qkv_both[1]).astype(bf16)
    attended_two = causal_attention(mixed)
    middle_two = inputs_two + dot(attended_two, out_both[1])
    result_two, kept_two = feed_forward(middle_two, gains[1, 1], gate_up_both[1], down_both[1])
    final = jnp.where(valid, result_two, inputs_two).astype(bf16)
    sent_out = swap(jnp.where(first_core, final, encoded))
    kept_out = jnp.where(first_core, encoded, final)
    section_out = jnp.where(
        first_core, jnp.stack([kept_out, sent_out]), jnp.stack([sent_out, kept_out])
    )[None]

    grad_kept = jnp.where(valid, cotangent_two, 0.0)
    grad_middle, gain_two_second, grad_joined, grad_branch = feed_back(
        middle_two, gains[1, 1], gate_up_both[1], down_both[1], kept_two, grad_kept
    )
    grad_low = grad_middle.astype(bf16)
    factors_two = [normed_two, attended_two, kept_two[0], grad_branch, None, grad_low, grad_joined, kept_two[3]]
    grad_attended = dot_nt(grad_low, out_both[1]).astype(bf16)
    grad_mixed = causal_attention_back(mixed, grad_attended)
    grad_normed = dot_nt(grad_mixed, qkv_both[1])
    grad_in, gain_two_first = normalize_back(inputs_two, gains[1, 0], inverse_two, grad_normed)
    grad_encoded = jnp.where(valid, 0.0, cotangent_two) + grad_middle + grad_in


    grad_out = cotangent_one + grad_encoded.astype(bf16).astype(f32)
    grad_kept = jnp.where(valid, grad_out, 0.0)
    grad_middle, gain_one_second, grad_joined, grad_branch = feed_back(
        middle_one, gains[0, 1], gate_up_both[0], down_both[0], kept_one, grad_kept
    )
    grad_low = grad_middle.astype(bf16)
    factors_one = [normed_one, attended_one, kept_one[0], grad_branch, None, grad_low, grad_joined, kept_one[3]]
    grad_attended = dot_nt(grad_low, out_both[0]).astype(bf16)
    grad_queries, grad_pairs = patch_attention_back(
        patch_row, patch_col, queries_one, byte_pairs, attention_one, grad_attended
    )
    grad_normed = dot_nt(grad_queries, qkv_both[0, :, :D])
    grad_in, gain_one_first = normalize_back(pooled, gains[0, 0], inverse_one, grad_normed)
    grad_pooled = jnp.where(valid, 0.0, grad_out) + grad_middle + grad_in
    grad_bytes = dot(member_byte, (grad_pooled / counts).astype(bf16))
    grad_bytes = (grad_bytes + dot_nt(grad_pairs, qkv_both[0, :, D:])).astype(bf16)


    factors_two[4], factors_one[4] = grad_mixed, grad_queries
    gain_part = jnp.stack([gain_one_first, gain_one_second, gain_two_first, gain_two_second])
    gain_part = jnp.pad(gain_part.reshape(8, half_width), ((8, 0), (0, 0)))
    sums, theirs, gathered, arrived = backward_sums(
        factors_two,
        factors_one,
        byte_rows,
        grad_pairs,
        grad_bytes,
        slots[:, None],
        flat_bytes[None, :],
        gain_part,
        table_rows,
    )
    hash_grad = jax.ops.segment_sum(
        arrived.reshape(-1, half_width).astype(f32),
        requested.reshape(-1),
        num_segments=count_tables * shard_rows,
    ).reshape(count_tables, shard_rows, half_width)
    gathered = gathered.reshape(-1, half_width)
    byte_table_grad = gathered[:table_rows].astype(f32)
    first_gain = table_rows // 16 * 16 + 8
    gain_sums = gathered[first_gain : first_gain + 8].reshape(2, 2, D)
    gain_sums = (gain_sums.astype(f32) + swap(gain_sums).astype(f32)).reshape(2, 2, devices, -1)
    gains_grad = lax.dynamic_index_in_dim(gain_sums, section, 0, keepdims=True)
    gains_grad = lax.dynamic_index_in_dim(gains_grad, lax.axis_index("rows"), 2, keepdims=False)

    mine = lax.dynamic_index_in_dim(sums, section, 0, keepdims=False)
    lower = jnp.where(first_core, mine, theirs).astype(f32)
    upper = jnp.where(first_core, theirs, mine).astype(f32)
    half, half_ff = D // 2, FF // 2
    gate_up_grad = jnp.concatenate([lower[:, :FF], upper[:, :FF]], axis=1)
    down_grad = jnp.concatenate([lower[:, FF : FF + half_ff], upper[:, FF : FF + half_ff]], axis=1).T
    low_rest, high_rest = lower[:, FF + half_ff :], upper[:, FF + half_ff :]
    columns = []
    for index in range(4):
        part = slice(index * half, (index + 1) * half)
        columns.append(jnp.concatenate([low_rest[:, part], high_rest[:, part]], axis=1))
    qkv_grad = jnp.concatenate(columns[:3], axis=1)
    out_grad = columns[3]

    return (
        section_out,
        byte_table_grad,
        hash_grad,
        gains_grad,
        qkv_grad[None],
        out_grad[None],
        gate_up_grad[None],
        down_grad[None],
    )


def solution(mesh):
    return jax.shard_map(
        on_device,
        mesh=mesh,
        in_specs=(
            P("rows", None),
            P("rows", None, None),
            P("rows", None),
            P("rows"),
            P(None, "section"),
            P(None, "rows", "section"),
            P("section", None, None),
            P("section", None, None),
            P("section", None, None),
            P("section", None, None),
            P("section", None, None),
            P("section", "rows", None, None),
        ),
        out_specs=(
            P("section", "rows", None, None),
            P(None, "section"),
            P(None, "rows", "section"),
            P("section", None, "rows"),
            P("section", "rows", None),
            P("section", "rows", None),
            P("section", "rows", None),
            P("section", None, "rows"),
        ),
        check_vma=False,
    )
```

```python
import functools

import jax
import jax.numpy as jnp
from jax import lax
from jax.experimental import pallas as pl
from jax.experimental.pallas import tpu as pltpu
from jax.sharding import PartitionSpec as P

D = 1024
HEADS = 16
HEAD = 64
FF = 2816
L = 1024
MOST = 16
M = 2
P_SIZE = 256
GROUP = 512
VMEM_BYTES = 48 * 1024 * 1024
SORT_TURN = 3

epsilon = 1e-05
f32 = jnp.float32
bf16 = jnp.bfloat16


def dot(left, right):
    return jnp.dot(left, right, preferred_element_type=f32)


def dot_nt(left, right):
    return lax.dot_general(left, right, (((1,), (1,)), ((), ())), preferred_element_type=f32)


def dot_tn(left, right):
    return lax.dot_general(left, right, (((0,), (0,)), ((), ())), preferred_element_type=f32)


def params(*semantics):
    return pltpu.CompilerParams(vmem_limit_bytes=VMEM_BYTES, dimension_semantics=semantics)


def as_column(row):
    shape = (row.shape[1], row.shape[1])
    same = lax.broadcasted_iota(jnp.int32, shape, 0) == lax.broadcasted_iota(jnp.int32, shape, 1)
    return jnp.sum(jnp.where(same, jnp.broadcast_to(row, shape), 0), axis=1, keepdims=True)


def gather_kernel(devices, *refs):
    requests_ref, tables_ref, slots_ref, ids_ref, bytes_ref = refs[:5]
    weights, refs = refs[5:9], refs[9:]
    out_ref, requested_ref = refs[:2]
    layers, refs = refs[2:6], refs[6:]
    held_ref, staged_ref, landed_ref, part_ref, total_ref, mine_ref, theirs_ref = refs[:7]
    load_sems, ask_send, ask_land, send_sems, land_sems, last_sems = refs[7:13]
    weight_send, weight_land = refs[13:]
    count_tables, shard_rows, half = tables_ref.shape
    each = requests_ref.shape[2]
    bits = devices.bit_length() - 1

    me = lax.axis_index("rows")
    section = lax.axis_index("section")
    partner = 1 - section
    mesh_id = pl.DeviceIdType.MESH
    places = [(me // 2**d) % 2 for d in range(bits)]

    def across(step):
        device = me
        for d in range(bits):
            if step // 2**d % 2:
                device = device + (1 - 2 * places[d]) * 2**d
        return device

    steps = [0]
    for d in range(bits):
        steps = list(range(2**d, 2 ** (d + 1))) + steps

    def load(table):
        return pltpu.make_async_copy(tables_ref.at[table], held_ref.at[table], load_sems.at[table])

    for table in range(count_tables):
        load(table).start()

    barrier = pltpu.get_barrier_semaphore()
    pl.semaphore_signal(barrier, inc=1, device_id={"section": partner}, device_id_type=mesh_id)
    for step in range(1, devices):
        pl.semaphore_signal(barrier, inc=1, device_id={"rows": across(step)}, device_id_type=mesh_id)
    pl.semaphore_wait(barrier, devices)

    def remote(source, target, send, land, **device):
        return pltpu.make_async_remote_copy(
            src_ref=source, dst_ref=target, send_sem=send, recv_sem=land, device_id=device, device_id_type=mesh_id
        )

    def ask(step):
        return remote(
            requests_ref.at[across(step)],
            requested_ref.at[me],
            ask_send.at[step - 1],
            ask_land.at[step - 1],
            rows=across(step),
        )

    def asked(step):
        return remote(
            requests_ref.at[across(step)],
            requested_ref.at[across(step)],
            ask_send.at[step - 1],
            ask_land.at[step - 1],
            rows=across(step),
        )

    for step in range(1, devices):
        ask(step).start()
    requested_ref[me] = requests_ref[me]

    def shared(index):
        return remote(
            weights[index],
            layers[index],
            weight_send.at[index],
            weight_land.at[index],
            section=partner,
        )

    tile = 512
    def own_row(index, carry):
        at = pl.ds(pl.multiple_of(index * tile, tile), tile)
        words = lax.broadcasted_iota(jnp.int32, (tile, bytes_ref.shape[0]), 1)
        word = (words == ids_ref[at, :]).astype(f32).astype(bf16)
        total_ref[at, :] = dot(word, bytes_ref[...])
        return carry

    lax.fori_loop(0, M * L // tile, own_row, 0)
    for step in range(1, devices):
        asked(step).wait_recv()

    groups = 4
    size = devices // groups

    def send(position, table):
        step = steps[position]
        slot = position * count_tables + table
        return remote(
            staged_ref.at[table, position],
            landed_ref.at[table, position],
            send_sems.at[slot],
            land_sems.at[slot],
            rows=across(step),
        )

    def find(table, group):
        positions = range(group * size, (group + 1) * size)
        ids = jnp.concatenate(
            [as_column(requested_ref[across(steps[p]), table : table + 1, :]) for p in positions], axis=0
        )
        depth = 1024
        part_ref[...] = jnp.zeros_like(part_ref)

        def body(index, carry):
            first = pl.multiple_of(index * depth, depth)
            places_in = first + lax.broadcasted_iota(jnp.int32, (size * each, depth), 1)
            chosen = (places_in == ids).astype(f32).astype(bf16)
            part_ref[...] += dot(chosen, held_ref[table, pl.ds(first, depth), :])
            return carry

        lax.fori_loop(0, shard_rows // depth, body, 0)
        for index, position in enumerate(positions):
            block = part_ref[index * each : (index + 1) * each, :].astype(bf16)
            if steps[position]:
                staged_ref[table, position] = block
                send(position, table).start()
            else:
                landed_ref[table, position] = block

    def combine(table, group):
        positions = range(group * size, (group + 1) * size)
        for position in positions:
            if steps[position]:
                send(position, table).wait_recv()
        rows = landed_ref[table, group * size : (group + 1) * size].reshape(size * each, half)
        slots = jnp.concatenate(
            [slots_ref[across(steps[p]), table : table + 1, :] for p in positions], axis=1
        )

        def body(index, carry):
            at = pl.ds(pl.multiple_of(index * tile, tile), tile)
            places_in = index * tile + lax.broadcasted_iota(jnp.int32, (tile, size * each), 0)
            chosen = (places_in == slots).astype(f32).astype(bf16)
            total_ref[at, :] += dot(chosen, rows)
            return carry

        lax.fori_loop(0, M * L // tile, body, 0)

    for index in range(len(weights)):
        shared(index).start()
    far, near = (0, 1), (2, 3)
    for table in range(count_tables):
        load(table).wait()
        for group in far:
            find(table, group)
    for table in range(count_tables):
        for group in near:
            find(table, group)
    for table in range(count_tables):
        for group in near:
            combine(table, group)
    for table in range(count_tables):
        for group in far:
            combine(table, group)

    theirs_ref[...] = total_ref[pl.ds(pl.multiple_of(partner * L, L), L), :].astype(bf16)
    mine = out_ref.at[:, pl.ds(pl.multiple_of(section * half, half), half)]
    last = remote(theirs_ref, mine, last_sems.at[0], last_sems.at[1], section=partner)
    last.start()
    mine_ref[...] = total_ref[pl.ds(pl.multiple_of(section * L, L), L), :].astype(bf16)
    own = pltpu.make_async_copy(mine_ref, mine, last_sems.at[2])
    own.start()
    for step in range(1, devices):
        ask(step).wait_send()
    for position in range(devices):
        for table in range(count_tables):
            if steps[position]:
                send(position, table).wait_send()
    for index in range(len(weights)):
        shared(index).wait()
    own.wait()
    last.wait()


def gather_rows(requests, tables, slots, ids, table, weights):
    devices, count_tables, each = requests.shape
    half = tables.shape[2]
    vmem = pl.BlockSpec(memory_space=pltpu.VMEM)
    any_space = pl.BlockSpec(memory_space=pl.ANY)
    dma = pltpu.SemaphoreType.DMA
    blocks = (count_tables, devices, each, half)
    return pl.pallas_call(
        functools.partial(gather_kernel, devices),
        in_specs=[vmem, any_space, vmem, vmem, vmem] + [any_space] * len(weights),
        out_specs=[vmem, vmem] + [any_space] * len(weights),
        out_shape=[
            jax.ShapeDtypeStruct((L, 2 * half), bf16),
            jax.ShapeDtypeStruct(requests.shape, jnp.int32),
            *[jax.ShapeDtypeStruct(weight.shape, weight.dtype) for weight in weights],
        ],
        scratch_shapes=[
            pltpu.VMEM(tables.shape, bf16),
            pltpu.VMEM(blocks, bf16),
            pltpu.VMEM(blocks, bf16),
            pltpu.VMEM((devices // 4 * each, half), f32),
            pltpu.VMEM((M * L, half), f32),
            pltpu.VMEM((L, half), bf16),
            pltpu.VMEM((L, half), bf16),
            dma((count_tables,)),
            dma((devices - 1,)),
            dma((devices - 1,)),
            dma((devices * count_tables,)),
            dma((devices * count_tables,)),
            dma((3,)),
            *[dma((len(weights),))] * 2,
        ],
        compiler_params=pltpu.CompilerParams(
            collective_id=1, has_side_effects=True, vmem_limit_bytes=56 * 1024 * 1024
        ),
        cost_estimate=pl.CostEstimate(flops=5 * 10**10, bytes_accessed=4 * 10**8, transcendentals=0),
        name="gather_rows",
    )(requests, tables, slots, ids, table, *weights)


def head_marks(heads, width):
    feature = lax.shift_right_logical(lax.broadcasted_iota(jnp.int32, (heads, width), 1), 6)
    return (feature == lax.broadcasted_iota(jnp.int32, (heads, width), 0)).astype(f32).astype(bf16)


def patch_marks(patch_row_ref, patch_col_ref):
    by_patch = (
        lax.broadcasted_iota(jnp.int32, (P_SIZE, L), 0) == patch_row_ref[...]
    ).astype(f32).astype(bf16)
    by_byte = (
        lax.broadcasted_iota(jnp.int32, (L, P_SIZE), 1) == patch_col_ref[...]
    ).astype(f32).astype(bf16)
    return by_patch, by_byte


def per_head(marks, products):
    high = products.astype(bf16)
    low = (products - high.astype(f32)).astype(bf16)
    return dot_nt(marks, high) + dot_nt(marks, low)


def neighbours(patches, heads):
    wide = jnp.broadcast_to(patches, (heads, L))
    back = [(d, pltpu.roll(wide, d, 1) == wide) for d in (1, 2, 4, 8)]
    ahead = [(L - d, pltpu.roll(wide, L - d, 1) == wide) for d in (1, 2, 4, 8)]
    return back, ahead


def scan_max(values, steps):
    for distance, same in steps:
        values = jnp.where(same, jnp.maximum(values, pltpu.roll(values, distance, 1)), values)
    return values


def scan_sum(values, steps):
    for distance, same in steps:
        values = jnp.where(same, values + pltpu.roll(values, distance, 1), values)
    return values


def patch_attention_kernel(
    patch_row_ref, patch_col_ref, query_ref, key_ref, value_ref, attention_ref, attended_ref
):
    heads, width = attention_ref.shape[0], query_ref.shape[1]
    marks = head_marks(heads, width)
    by_patch, by_byte = patch_marks(patch_row_ref, patch_col_ref)
    queries = dot(by_byte, query_ref[...])
    scores = per_head(marks, queries * key_ref[...].astype(f32)) * 0.125
    back, ahead = neighbours(patch_row_ref[...], heads)
    top = scan_max(scan_max(scores, back), ahead)
    shifted = jnp.exp(scores - top)
    total = scan_sum(shifted, back) + scan_sum(shifted, ahead) - shifted
    attention = shifted / total
    attention_ref[...] = attention
    weights = dot_tn(attention.astype(bf16), marks)
    weighted = (weights * value_ref[...].astype(f32)).astype(bf16)
    attended_ref[...] = dot(by_patch, weighted).astype(bf16)


def patch_attention(patch_row, patch_col, queries, key_value):
    groups = D // GROUP
    return pl.pallas_call(
        patch_attention_kernel,
        grid=(groups,),
        in_specs=[
            pl.BlockSpec((1, L), lambda i: (0, 0)),
            pl.BlockSpec((L, 1), lambda i: (0, 0)),
            pl.BlockSpec((P_SIZE, GROUP), lambda i: (0, i)),
            pl.BlockSpec((L, GROUP), lambda i: (0, i)),
            pl.BlockSpec((L, GROUP), lambda i: (0, i + groups)),
        ],
        out_specs=[
            pl.BlockSpec((HEADS // groups, L), lambda i: (i, 0)),
            pl.BlockSpec((P_SIZE, GROUP), lambda i: (0, i)),
        ],
        out_shape=[
            jax.ShapeDtypeStruct((HEADS, L), f32),
            jax.ShapeDtypeStruct((P_SIZE, D), bf16),
        ],
        compiler_params=params("arbitrary"),
        cost_estimate=pl.CostEstimate(flops=4 * 10**9, bytes_accessed=6 * 10**6, transcendentals=16384),
        name="patch_attention",
    )(patch_row, patch_col, queries, key_value, key_value)


def patch_attention_back_kernel(
    patch_row_ref,
    patch_col_ref,
    query_ref,
    key_ref,
    value_ref,
    attention_ref,
    grad_ref,
    grad_query_ref,
    grad_pair_ref,
):
    heads, width = attention_ref.shape[0], query_ref.shape[1]
    first = pl.multiple_of(pl.program_id(0) * width, width)
    marks = head_marks(heads, width)
    by_patch, by_byte = patch_marks(patch_row_ref, patch_col_ref)
    grads = dot(by_byte, grad_ref[...])
    attention = attention_ref[...]
    grad_attention = per_head(marks, grads * value_ref[...].astype(f32))
    weights = dot_tn(attention.astype(bf16), marks)
    grad_pair_ref[:, pl.ds(D + first, width)] = (weights * grads).astype(bf16)
    back, ahead = neighbours(patch_row_ref[...], heads)
    terms = attention * grad_attention
    total = scan_sum(terms, back) + scan_sum(terms, ahead) - terms
    grad_scores = (attention * (grad_attention - total)).astype(bf16)
    spread_scores = dot_tn(grad_scores, marks) * 0.125
    grad_pair_ref[:, pl.ds(first, width)] = (spread_scores * dot(by_byte, query_ref[...])).astype(bf16)
    weighted = (spread_scores * key_ref[...].astype(f32)).astype(bf16)
    grad_query_ref[...] = dot(by_patch, weighted).astype(bf16)


def patch_attention_back(patch_row, patch_col, queries, key_value, attention, grad_attended):
    groups = D // GROUP
    byte_block = pl.BlockSpec((L, GROUP), lambda i: (0, i))
    patch_block = pl.BlockSpec((P_SIZE, GROUP), lambda i: (0, i))
    return pl.pallas_call(
        patch_attention_back_kernel,
        grid=(groups,),
        in_specs=[
            pl.BlockSpec((1, L), lambda i: (0, 0)),
            pl.BlockSpec((L, 1), lambda i: (0, 0)),
            patch_block,
            byte_block,
            pl.BlockSpec((L, GROUP), lambda i: (0, i + groups)),
            pl.BlockSpec((HEADS // groups, L), lambda i: (i, 0)),
            patch_block,
        ],
        out_specs=[patch_block, pl.BlockSpec((L, 2 * D), lambda i: (0, 0))],
        out_shape=[
            jax.ShapeDtypeStruct((P_SIZE, D), bf16),
            jax.ShapeDtypeStruct((L, 2 * D), bf16),
        ],
        compiler_params=params("arbitrary"),
        cost_estimate=pl.CostEstimate(flops=6 * 10**9, bytes_accessed=10 * 10**6, transcendentals=0),
        name="patch_attention_back",
    )(patch_row, patch_col, queries, key_value, key_value, attention, grad_attended)


def causal_softmax(queries, keys):
    scores = dot_nt(queries, keys) * 0.125
    size = scores.shape[0]
    allowed = lax.broadcasted_iota(jnp.int32, (size, size), 0) >= lax.broadcasted_iota(
        jnp.int32, (size, size), 1
    )
    scores = jnp.where(allowed, scores, -jnp.inf)
    shifted = jnp.exp(scores - jnp.max(scores, axis=-1, keepdims=True))
    return shifted / jnp.sum(shifted, axis=-1, keepdims=True)


def pair_masks(shape):
    lane = lax.broadcasted_iota(jnp.int32, shape, 1)
    return [lane < HEAD, lane >= HEAD]


def causal_kernel(query_ref, key_ref, value_ref, out_ref):
    queries, keys, values = query_ref[...], key_ref[...], value_ref[...]
    masks = pair_masks(queries.shape)
    parts = []
    for mask in masks:
        attention = causal_softmax(jnp.where(mask, queries, 0), keys).astype(bf16)
        parts.append(dot(attention, values))
    out_ref[...] = jnp.where(masks[0], parts[0], parts[1]).astype(bf16)


def causal_attention(mixed):
    pairs = HEADS // 2
    return pl.pallas_call(
        causal_kernel,
        grid=(pairs,),
        in_specs=[
            pl.BlockSpec((P_SIZE, 2 * HEAD), lambda i: (0, i)),
            pl.BlockSpec((P_SIZE, 2 * HEAD), lambda i: (0, i + pairs)),
            pl.BlockSpec((P_SIZE, 2 * HEAD), lambda i: (0, i + 2 * pairs)),
        ],
        out_specs=pl.BlockSpec((P_SIZE, 2 * HEAD), lambda i: (0, i)),
        out_shape=jax.ShapeDtypeStruct((P_SIZE, D), bf16),
        compiler_params=params("arbitrary"),
        cost_estimate=pl.CostEstimate(flops=2 * 10**9, bytes_accessed=2 * 10**6, transcendentals=10**6),
        name="causal_attention",
    )(mixed, mixed, mixed)


def causal_back_kernel(query_ref, key_ref, value_ref, grad_ref, out_ref):
    pair = pl.program_id(0) * 2 * HEAD
    queries, keys, values, grads = query_ref[...], key_ref[...], value_ref[...], grad_ref[...]
    masks = pair_masks(queries.shape)
    results = []
    for mask in masks:
        attention = causal_softmax(jnp.where(mask, queries, 0), keys)
        grad_attention = dot_nt(jnp.where(mask, grads, 0), values)
        total = jnp.sum(attention * grad_attention, axis=-1, keepdims=True)
        grad_scores = (attention * (grad_attention - total)).astype(bf16)
        results.append(
            (
                dot(grad_scores, keys) * 0.125,
                dot_tn(grad_scores, queries) * 0.125,
                dot_tn(attention.astype(bf16), grads),
            )
        )
    for index, (first, second) in enumerate(zip(results[0], results[1])):
        columns = pl.ds(pl.multiple_of(index * D + pair, 2 * HEAD), 2 * HEAD)
        out_ref[:, columns] = jnp.where(masks[0], first, second).astype(bf16)


def causal_attention_back(mixed, grad_attended):
    pairs = HEADS // 2
    block = pl.BlockSpec((P_SIZE, 2 * HEAD), lambda i: (0, i))
    return pl.pallas_call(
        causal_back_kernel,
        grid=(pairs,),
        in_specs=[
            block,
            pl.BlockSpec((P_SIZE, 2 * HEAD), lambda i: (0, i + pairs)),
            pl.BlockSpec((P_SIZE, 2 * HEAD), lambda i: (0, i + 2 * pairs)),
            block,
        ],
        out_specs=pl.BlockSpec((P_SIZE, 3 * D), lambda i: (0, 0)),
        out_shape=jax.ShapeDtypeStruct((P_SIZE, 3 * D), bf16),
        compiler_params=params("arbitrary"),
        cost_estimate=pl.CostEstimate(flops=4 * 10**9, bytes_accessed=4 * 10**6, transcendentals=10**6),
        name="causal_attention_back",
    )(mixed, mixed, mixed, grad_attended)


def normalize(inputs, gain):
    inverse = lax.rsqrt(jnp.mean(inputs * inputs, axis=-1, keepdims=True) + epsilon)
    return (inputs * inverse * gain).astype(bf16), inverse


def normalize_back(inputs, gain, inverse, grad_normed):
    scaled = inputs * inverse
    grad_gain = jnp.sum(grad_normed * scaled, axis=0)
    grad_scaled = grad_normed * gain
    grad_inputs = inverse * (
        grad_scaled - scaled * jnp.mean(grad_scaled * scaled, axis=-1, keepdims=True)
    )
    return grad_inputs, grad_gain


def feed_forward(hidden, gain, w_gate_up, w_down):
    normed, inverse = normalize(hidden, gain)
    joined = dot(normed, w_gate_up)
    inner = (jax.nn.silu(joined[:, :FF]) * joined[:, FF:]).astype(bf16)
    return hidden + dot(inner, w_down), (normed, inverse, joined, inner)


def feed_back(hidden, gain, w_gate_up, w_down, kept, grad_out):
    normed, inverse, joined, inner = kept
    gate, up = joined[:, :FF], joined[:, FF:]
    sigmoid = jax.nn.sigmoid(gate)
    grad_branch = grad_out.astype(bf16)
    grad_inner = dot_nt(grad_branch, w_down)
    grad_gate = grad_inner * up * sigmoid * (1.0 + gate * (1.0 - sigmoid))
    grad_up = grad_inner * gate * sigmoid
    grad_joined = jnp.concatenate([grad_gate, grad_up], axis=1).astype(bf16)
    grad_normed = dot_nt(grad_joined, w_gate_up)
    grad_in, grad_gain = normalize_back(hidden, gain, inverse, grad_normed)
    return grad_out + grad_in, grad_gain, grad_joined, grad_branch


def chip_bits(devices):
    bits = devices.bit_length() - 1
    first = tuple(reversed(range(bits)))
    return bits, {"A": first, "B": (first[1], first[0]) + first[2:], "C": first[2:4] + first[:2] + first[4:]}


def at_place(ref, axis, place):
    return ref.at[(slice(None),) * axis + (place,)]


def plan_pieces():
    ff, half = FF // 2, D // 2
    pieces = []
    for layer in (1, 0):
        pieces += [
            (layer, "A", [("gate_up", 0, ff)]),
            (layer, "A", [("gate_up", ff, ff)]),
            (layer, "B", [("down", 0, ff)]),
            (layer, "B", [("query", 0, half), ("key", 0, half)]),
            (layer, "C", [("value", 0, half), ("out", 0, half)]),
        ]
    return pieces


def backward_kernel(devices, table_rows, count_tables, *refs):
    bits, orders = chip_bits(devices)
    half, ff = D // 2, FF // 2
    rows = D // devices
    table_block = table_block_rows(devices, table_rows)
    plan = plan_pieces()
    extra = len(plan)
    pieces = extra + 1
    names = [piece[1] for piece in plan] + ["C"]
    widths = [sum(width for _, _, width in piece[2]) for piece in plan] + [half]

    layers, refs = {1: refs[:8], 0: refs[8:16]}, refs[16:]
    bytes_ref, pairs_ref, grad_ref, slots_ref, places_ref, ids_ref, gains_ref = refs[:7]
    sums_ref, theirs_ref, gathered_ref, sorted_ref, arrived_ref, staged_ref = refs[7:13]
    refs = refs[13:]
    landed, refs = {1: refs[:8], 0: refs[8:16]}, refs[16:]
    bytes_landed, pairs_landed, refs = refs[0], refs[1], refs[2:]
    owns, refs = refs[:pieces], refs[pieces:]
    lands, refs = [refs[bits * i : bits * i + bits] for i in range(pieces)], refs[bits * pieces :]
    left_ref, right_ref, total_ref, send_ref, extra_ref, own_ref, table_ref, tile_ref, block_ref = refs[:9]
    swap_send, swap_land, load_sems, grad_sems, table_sem, tile_sems, block_sems, refs = *refs[9:16], refs[16:]
    send_sems, land_sems, trade_send, trade_land, spread_send, spread_land, last_sems = refs

    me = lax.axis_index("rows")
    section = lax.axis_index("section")
    partner = 1 - section
    places = [(me // 2 ** (bits - 1 - d)) % 2 for d in range(bits)]
    peers = [me + (1 - 2 * places[d]) * 2 ** (bits - 1 - d) for d in range(bits)]

    def other(step):
        return lax.rem(me + step, devices)

    barrier = pltpu.get_barrier_semaphore()
    mesh_id = pl.DeviceIdType.MESH
    pl.semaphore_signal(barrier, inc=1, device_id={"section": partner}, device_id_type=mesh_id)
    for step in range(1, devices):
        pl.semaphore_signal(barrier, inc=1, device_id={"rows": other(step)}, device_id_type=mesh_id)
    pl.semaphore_wait(barrier, devices)

    def remote(source, target, send, land, **device):
        return pltpu.make_async_remote_copy(
            src_ref=source, dst_ref=target, send_sem=send, recv_sem=land, device_id=device, device_id_type=mesh_id
        )

    def part_of(array, index, core):
        size = array.shape[1]
        if size == 3 * D:
            first = index * D + core * half
        elif size == 2 * D:
            first = index * D + core * half
        else:
            first = core * (size // 2)
            return array.at[:, pl.ds(pl.multiple_of(first, 128), size // 2)]
        return array.at[:, pl.ds(pl.multiple_of(first, 128), half)]

    swaps = {}

    def swap_of(key, source, target):
        slot = len(swaps)
        swaps[key] = remote(source, target, swap_send.at[slot], swap_land.at[slot], section=partner)
        swaps[key].start()

    def swap_layer(layer, which):
        for index in which:
            array, target = layers[layer][index], landed[layer][index]
            if index < 4:
                swap_of((layer, index, 0), array, target)
            else:
                wide = array.shape[1] // D if index == 4 else 1
                for part in range(wide):
                    there = target.at[:, pl.ds(part * half, half)] if index == 4 else target
                    swap_of((layer, index, part), part_of(array, part, partner), there)

    ready = set()

    def settled(key):
        if key not in ready:
            ready.add(key)
            swaps[key].wait_recv()

    swap_layer(1, (2, 6, 3, 7))
    own_rows = own_ref.at[pl.ds(pl.multiple_of(section * L, L), L)]
    swap_of(("grads",), grad_ref.at[:, pl.ds(pl.multiple_of(partner * half, half), half)], own_rows)
    own_copy = pltpu.make_async_copy(
        grad_ref.at[:, pl.ds(pl.multiple_of(section * half, half), half)], own_rows, grad_sems
    )
    own_copy.start()
    swap_layer(1, (0, 1, 4, 5))
    swap_layer(0, (2, 6, 3, 7, 0, 1, 4, 5))
    swap_of(("bytes",), bytes_ref, bytes_landed)
    for part in range(2):
        swap_of(
            ("pairs", part), part_of(pairs_ref, part, partner), pairs_landed.at[:, pl.ds(part * half, half)]
        )

    def jobs_of(piece):
        layer, _, segments = plan[piece]
        own, land = layers[layer], landed[layer]
        result, column = [], 0
        for kind, first, width in segments:
            if layer == 0 and kind in ("key", "value"):
                part = 0 if kind == "key" else 1
                for chunk in range(4):
                    depth = pl.ds(chunk % 2 * 512, 512)
                    if chunk < 2:
                        left, right = bytes_ref, part_of(pairs_ref, part, section)
                        keys = []
                    else:
                        left, right = bytes_landed, pairs_landed.at[:, pl.ds(part * half, half)]
                        keys = [("bytes",), ("pairs", part)]
                    copies = [("left", left.at[depth], 0, 512), ("right", right.at[depth], 0, 512)]
                    result.append((piece, column, width, chunk, 4, keys, copies))
            else:
                index, other_index, part = {
                    "gate_up": (2, 6, 0),
                    "down": (3, 7, 0),
                    "query": (0, 4, 0),
                    "key": (0, 4, 1),
                    "value": (0, 4, 2),
                    "out": (1, 5, 0),
                }[kind]
                if other_index == 4:
                    right = part_of(own[4], part, section)
                    right_landed = land[4].at[:, pl.ds(part * half, half)]
                elif kind == "gate_up":
                    start = pl.multiple_of(section * FF + first, 128)
                    right = own[6].at[:, pl.ds(start, width)]
                    right_landed = land[6].at[:, pl.ds(first, width)]
                else:
                    right, right_landed = part_of(own[other_index], 0, section), land[other_index]
                copies = [
                    ("left", own[index], 0, P_SIZE),
                    ("left", land[index], P_SIZE, P_SIZE),
                    ("right", right, 0, P_SIZE),
                    ("right", right_landed, P_SIZE, P_SIZE),
                ]
                keys = [(layer, index, 0), (layer, other_index, part)]
                result.append((piece, column, width, 0, 1, keys, copies))
            column += width
        return result

    groups = [[i for i in range(pieces) if names[i] == name] for name in "ABC"]
    order_made = []
    for rank in range(max(len(group) for group in groups)):
        order_made += [group[rank] for group in groups if rank < len(group)]
    jobs = [job for piece in order_made if piece != extra for job in jobs_of(piece)]

    def loads(number):
        piece, column, width, chunk, chunks, keys, copies = jobs[number]
        slot = number % 2
        result = []
        for index, (side, source, first, count) in enumerate(copies):
            buffer = left_ref if side == "left" else right_ref
            columns = D if side == "left" else width
            target = buffer.at[slot, pl.ds(first, count), pl.ds(0, columns)]
            result.append(pltpu.make_async_copy(source, target, load_sems.at[slot, index]))
        return result

    def start_loads(number):
        if number < len(jobs):
            for key in jobs[number][5]:
                settled(key)
            for copy in loads(number):
                copy.start()

    slots_of = {piece: index % send_ref.shape[0] for index, piece in enumerate(order_made) if piece != extra}

    def sent_part(piece):
        if piece == extra:
            return extra_ref
        return send_ref.at[slots_of[piece]].at[(slice(None),) * bits + (pl.ds(0, widths[piece]),)]

    def store(piece, device, value, column, width):
        axis = orders[names[piece]][0]
        at = [(device // 2 ** (bits - 1 - d)) % 2 for d in range(bits)]
        bit = at.pop(axis)
        at = tuple(at) + (slice(None), pl.ds(column, width))
        target = sent_part(piece)

        @pl.when(bit == places[axis])
        def _():
            owns[piece][at] = value

        @pl.when(bit != places[axis])
        def _():
            target[at] = value

    def run_job(number):
        piece, column, width, chunk, chunks, keys, copies = jobs[number]
        slot = number % 2
        for copy in loads(number):
            copy.wait()
        start_loads(number + 1)
        tile = 128

        def body(index, carry):
            at = pl.ds(pl.multiple_of(index * tile, tile), tile)
            value = dot_tn(left_ref[slot, :, at], right_ref[slot, :, pl.ds(0, width)])
            if chunk > 0:
                value = value + total_ref[at, :]
            if chunk < chunks - 1:
                total_ref[at, :] = value
            else:
                for part in range(tile // rows):
                    block = value[part * rows : (part + 1) * rows].astype(bf16)
                    store(piece, index * (tile // rows) + part, block, column, width)
            return carry

        lax.fori_loop(0, D // tile, body, 0)

    def left_of(piece, phase):
        order = orders[names[piece]]
        return [d for d in range(bits) if d not in order[:phase]]

    def kept(piece, phase):
        order = orders[names[piece]]
        ref = owns[piece]
        for step in range(1, phase):
            ref = at_place(ref, left_of(piece, step).index(order[step]), places[order[step]])
        return ref

    def send(piece, phase):
        axis = orders[names[piece]][phase]
        if phase == 0:
            source = sent_part(piece)
        else:
            source = at_place(kept(piece, phase), left_of(piece, phase).index(axis), 1 - places[axis])
        slot = piece * bits + phase
        return remote(source, lands[piece][phase], send_sems.at[slot], land_sems.at[slot], rows=peers[axis])

    made = [0, 0]
    sent = set()

    def make(piece):
        if piece == extra:
            make_extra()
        else:
            index = order_made.index(piece)
            count = send_ref.shape[0]
            earlier = [p for p in order_made[:index] if p != extra and slots_of[p] == slots_of[piece]]
            if earlier and (earlier[-1], 0) not in sent:
                sent.add((earlier[-1], 0))
                send(earlier[-1], 0).wait_send()
            while made[0] < len(jobs) and jobs[made[0]][0] == piece:
                run_job(made[0])
                made[0] += 1
        send(piece, 0).start()

    def make_extra():
        tile = table_block
        first_gain = table_rows // 16 * 16
        positions = M * L

        def body(index, carry):
            words = index * tile + lax.broadcasted_iota(jnp.int32, (tile, positions), 0)
            chosen = (words == ids_ref[...]).astype(f32).astype(bf16)
            value = dot(chosen, own_ref[...])
            row = index * tile + lax.broadcasted_iota(jnp.int32, (tile, half), 0)
            gains = jnp.concatenate([gains_ref[...]] * (tile // 16), axis=0)
            inside = (row >= first_gain) & (row < first_gain + 16)
            value = value + jnp.where(inside, gains, 0.0)
            store(extra, index, value.astype(bf16), 0, half)
            return carry

        lax.fori_loop(0, devices, body, 0)

    def add(piece, phase):
        target = kept(piece, phase + 1)
        land = lands[piece][phase]
        leads = len(target.shape) - 2
        count = 16
        groups_in = target.shape[-2] // count

        def body(index, carry):
            at = (pl.ds(pl.multiple_of(index % groups_in * count, count), count), slice(None))
            lead = index // groups_in
            at = tuple((lead // 2 ** (leads - 1 - d)) % 2 for d in range(leads)) + at
            target[at] = (target[at].astype(f32) + land[at].astype(f32)).astype(bf16)
            return carry

        lax.fori_loop(0, 2**leads * groups_in, body, 0)

    block_rows = block_ref.shape[1]
    block_slots = block_ref.shape[0]

    def block_copy(step):
        target = staged_ref.at[step] if step else arrived_ref.at[me]
        slot = (step - 1) % devices % block_slots
        return pltpu.make_async_copy(block_ref.at[slot], target, block_sems.at[slot])

    def trade(step):
        return remote(
            staged_ref.at[step], arrived_ref.at[me], trade_send.at[step - 1], trade_land.at[step - 1], rows=other(step)
        )

    def trade_landing(step):
        back = lax.rem(me + devices - step, devices)
        return remote(
            staged_ref.at[step], arrived_ref.at[back], trade_send.at[step - 1], trade_land.at[step - 1], rows=back
        )

    own_block = block_copy(0)

    def make_blocks():
        own_copy.wait()
        settled(("grads",))
        steps = list(range(1, devices)) + [0]
        behind = block_slots - 1

        def pass_on(step):
            if step:
                block_copy(step).wait()
                trade(step).start()

        for index, step in enumerate(steps):
            if index >= behind:
                pass_on(steps[index - behind])
            each = block_rows // count_tables
            where = lax.broadcasted_iota(jnp.int32, (each, M * L), 1)
            for table in range(count_tables):
                slot = as_column(slots_ref[other(step), table : table + 1, :])
                chosen = (where == slot).astype(f32).astype(bf16)
                part = pl.ds(table * each, each)
                block_ref[index % block_slots, part] = dot(chosen, own_ref[...]).astype(bf16)
            block_copy(step).start()
        for step in steps[devices - behind :]:
            pass_on(step)


    def tile_copy(table, index):
        tile = tile_ref.shape[1]
        return pltpu.make_async_copy(
            tile_ref.at[index % 2],
            sorted_ref.at[table, pl.ds(pl.multiple_of(index * tile, tile), tile)],
            tile_sems.at[index % 2],
        )

    def sort_rows(table):
        if table == 0:
            own_block.wait()
            for step in range(1, devices):
                trade_landing(step).wait_recv()
        each = block_rows // count_tables
        copy = pltpu.make_async_copy(arrived_ref.at[:, pl.ds(table * each, each)], table_ref, table_sem)
        copy.start()
        copy.wait()
        tile = tile_ref.shape[1]
        for index in range(M * L // tile):
            if index >= 2:
                tile_copy(table, index - 2).wait()
            place = lax.broadcasted_iota(jnp.int32, (tile, M * L), 1)
            wanted = as_column(places_ref[table, :, index * tile : (index + 1) * tile])
            chosen = (place == wanted).astype(f32).astype(bf16)
            rows_in = table_ref[...].reshape(M * L, half)
            tile_ref[index % 2] = dot(chosen, rows_in).astype(bf16)
            tile_copy(table, index).start()
        for index in range(M * L // tile - 2, M * L // tile):
            tile_copy(table, index).wait()

    def spreads():
        return [
            remote(
                gathered_ref.at[me],
                gathered_ref.at[me],
                spread_send.at[step - 1],
                spread_land.at[step - 1],
                rows=other(step),
            )
            for step in range(1, devices)
        ]

    def spread_landing(step):
        back = lax.rem(me + devices - step, devices)
        return remote(
            gathered_ref.at[me], gathered_ref.at[back], spread_send.at[step - 1], spread_land.at[step - 1], rows=back
        )

    def finish(piece):
        if piece == extra:
            gathered_ref[me] = kept(piece, bits)[...]
            for copy in spreads():
                copy.start()
        else:
            layer = plan[piece][0]
            first = sum(widths[p] for p in range(piece) if plan[p][0] == layer)
            sums_ref[layer, :, first : first + widths[piece]] = kept(piece, bits)[...]

    start_loads(0)
    for group in groups:
        make(group[0])
    make_blocks()
    for group in groups:
        if len(group) > 1:
            make(group[1])
    rounds = max(len(group) for group in groups)
    for turn in range(rounds + bits - 1):
        for phase in range(bits):
            for group in groups:
                if not 0 <= turn - phase < len(group):
                    continue
                piece = group[turn - phase]
                send(piece, phase).wait_recv()
                if phase == 0 and turn + 2 < len(group):
                    make(group[turn + 2])
                add(piece, phase)
                if phase + 1 < bits:
                    send(piece, phase + 1).start()
                else:
                    finish(piece)
        if 0 <= turn - SORT_TURN < count_tables:
            sort_rows(turn - SORT_TURN)

    last = remote(sums_ref.at[partner], theirs_ref, last_sems.at[0], last_sems.at[1], section=partner)
    last.start()
    for piece in range(pieces):
        for phase in range(bits):
            if (piece, phase) not in sent:
                send(piece, phase).wait_send()
    for key, copy in swaps.items():
        copy.wait_send()
        settled(key)
    for step in range(1, devices):
        trade(step).wait_send()
    for copy in spreads():
        copy.wait_send()
    for step in range(1, devices):
        spread_landing(step).wait_recv()
    last.wait()


def place_kernel(starts_ref, ids_ref, rows_ref, out_ref):
    table, tile = pl.program_id(0), pl.program_id(1)
    height, window = out_ref.shape[1], 256
    at = table * (pl.num_programs(1) + 1) + tile
    places = tile * height + lax.broadcasted_iota(jnp.int32, (height, window), 0)
    out_ref[...] = jnp.zeros(out_ref.shape, f32)

    def body(index, carry):
        part = pl.ds(pl.multiple_of(index * window, window), window)
        chosen = (places == ids_ref[0, :, part]).astype(f32).astype(bf16)
        out_ref[0] += dot(chosen, rows_ref[0, part, :])
        return carry

    lax.fori_loop(starts_ref[at] // window, (starts_ref[at + 1] + window - 1) // window, body, 0)


def place_rows(ids, rows, shard_rows):
    count_tables, count, width = rows.shape
    height = 1024
    tiles = shard_rows // height
    edges = jnp.arange(tiles + 1, dtype=jnp.int32) * height
    starts = jnp.sum((ids[:, None, :] < edges[None, :, None]).astype(jnp.int32), axis=2).reshape(-1)
    return pl.pallas_call(
        place_kernel,
        grid_spec=pltpu.PrefetchScalarGridSpec(
            num_scalar_prefetch=1,
            grid=(count_tables, tiles),
            in_specs=[
                pl.BlockSpec((1, 1, count), lambda i, j, starts: (i, 0, 0)),
                pl.BlockSpec((1, count, width), lambda i, j, starts: (i, 0, 0)),
            ],
            out_specs=pl.BlockSpec((1, height, width), lambda i, j, starts: (i, j, 0)),
        ),
        out_shape=jax.ShapeDtypeStruct((count_tables, shard_rows, width), f32),
        compiler_params=params("arbitrary", "arbitrary"),
        cost_estimate=pl.CostEstimate(flops=10**10, bytes_accessed=6 * 10**7, transcendentals=0),
        name="place_rows",
    )(starts, ids[:, None, :], rows)


def table_block_rows(devices, table_rows):
    return -(-(table_rows + 12) // (16 * devices)) * 16


def backward_sums(layer_two, layer_one, byte_rows, grad_pairs, grad_bytes, slots, places, ids, gains, table_rows):
    devices = lax.axis_size("rows")
    bits, orders = chip_bits(devices)
    rows = D // devices
    plan = plan_pieces()
    table_block = table_block_rows(devices, table_rows)
    half, ff = D // 2, FF // 2
    count_tables, each = slots.shape[1:]
    block_rows = count_tables * each
    widths = [sum(width for _, _, width in piece[2]) for piece in plan]
    shapes = [(rows, width) for width in widths] + [(table_block, half)]
    owns, lands = [], []
    for shape in shapes:
        owns.append(pltpu.VMEM((2,) * (bits - 1) + shape, bf16))
        lands += [pltpu.VMEM((2,) * (bits - 1 - phase) + shape, bf16) for phase in range(bits)]
    total = sum(widths) // 2
    landed = []
    for layer in (layer_two, layer_one):
        for index, array in enumerate(layer):
            shape = array.shape if index < 4 else (array.shape[0], array.shape[1] // 2)
            landed.append(jax.ShapeDtypeStruct(shape, bf16))
    landed += [
        jax.ShapeDtypeStruct(byte_rows.shape, bf16),
        jax.ShapeDtypeStruct((grad_pairs.shape[0], grad_pairs.shape[1] // 2), bf16),
    ]
    swaps = 2 * 7 + 3 + 1 + 4
    copies = len(shapes) * bits
    any_space = pl.BlockSpec(memory_space=pl.ANY)
    vmem = pl.BlockSpec(memory_space=pltpu.VMEM)
    blocks = jax.ShapeDtypeStruct((devices, block_rows, half), bf16)
    dma = pltpu.SemaphoreType.DMA
    results = pl.pallas_call(
        functools.partial(backward_kernel, devices, table_rows, count_tables),
        in_specs=[any_space] * 19 + [vmem] * 4,
        out_specs=[vmem, any_space, vmem] + [any_space] * (3 + len(landed)),
        out_shape=[
            jax.ShapeDtypeStruct((2, rows, total), bf16),
            jax.ShapeDtypeStruct((rows, total), bf16),
            jax.ShapeDtypeStruct((devices, table_block, half), bf16),
            jax.ShapeDtypeStruct((count_tables, M * L, half), bf16),
            blocks,
            blocks,
            *landed,
        ],
        scratch_shapes=[
            *owns,
            *lands,
            pltpu.VMEM((2, 2 * P_SIZE, D), bf16),
            pltpu.VMEM((2, 2 * P_SIZE, ff), bf16),
            pltpu.VMEM((D, half), f32),
            pltpu.VMEM((4,) + (2,) * (bits - 1) + (rows, ff), bf16),
            pltpu.VMEM((2,) * (bits - 1) + (table_block, half), bf16),
            pltpu.VMEM((M * L, half), bf16),
            pltpu.VMEM((devices, each, half), bf16),
            pltpu.VMEM((2, 256, half), bf16),
            pltpu.VMEM((3, block_rows, half), bf16),
            dma((swaps,)),
            dma((swaps,)),
            dma((2, 4)),
            dma,
            dma,
            dma((2,)),
            dma((3,)),
            dma((copies,)),
            dma((copies,)),
            dma((devices - 1,)),
            dma((devices - 1,)),
            dma((devices - 1,)),
            dma((devices - 1,)),
            dma((2,)),
        ],
        compiler_params=pltpu.CompilerParams(
            collective_id=0, has_side_effects=True, vmem_limit_bytes=60 * 1024 * 1024
        ),
        cost_estimate=pl.CostEstimate(flops=5 * 10**10, bytes_accessed=6 * 10**8, transcendentals=0),
        name="backward_sums",
    )(*layer_two, *layer_one, byte_rows, grad_pairs, grad_bytes, slots, places, ids, gains)
    return results[:4]


def swap(array):
    return lax.ppermute(array, "section", [(0, 1), (1, 0)])


def on_device(
    byte_ids,
    hash_ids,
    patch_lengths,
    row_lengths,
    byte_table,
    hash_tables,
    norm_gains,
    w_qkv,
    w_out,
    w_gate_up,
    w_down,
    cotangent,
):
    section = lax.axis_index("section")
    first_core = section == 0
    devices = lax.axis_size("rows")
    count_tables, shard_rows, half_width = hash_tables.shape
    positions = M * L

    def both(array):
        return lax.all_gather(array, "section", axis=0, tiled=True)

    flat_ids = hash_ids.reshape(positions, count_tables).T
    owners = flat_ids // shard_rows
    order_key = owners * positions + jnp.arange(positions, dtype=jnp.int32)[None, :]
    order_key, grouped = lax.sort((order_key, flat_ids % shard_rows), dimension=1, num_keys=1)

    def by_owner(array):
        return array.reshape(count_tables, devices, -1).transpose(1, 0, 2)

    byte_of_slot = order_key % positions
    numbers = jnp.arange(positions, dtype=jnp.int32)[None, :]
    flat_bytes = byte_ids.reshape(positions)
    table_rows = byte_table.shape[0]
    padded = jnp.pad(byte_table, ((0, -table_rows % 128), (0, 0)))
    slots = by_owner(byte_of_slot)
    weights = [w_qkv[0], w_out[0], w_gate_up[0], w_down[0]]
    byte_rows, requested, *other_weights = gather_rows(
        by_owner(grouped), hash_tables, slots, flat_bytes[:, None], padded, weights
    )
    table_ids = requested.transpose(1, 0, 2).reshape(count_tables, -1)
    id_key = lax.sort(table_ids * positions + numbers, dimension=1)
    sorted_ids = id_key // positions
    places = (id_key % positions)[:, None, :]

    gains = both(norm_gains).astype(f32)

    lengths = lax.dynamic_index_in_dim(patch_lengths, section, 0, keepdims=False)
    row_length = lax.dynamic_index_in_dim(row_lengths, section, 0, keepdims=False)
    starts = jnp.cumsum(lengths) - lengths
    byte_positions = jnp.arange(L, dtype=jnp.int32)
    byte_patch = jnp.sum((starts[:, None] <= byte_positions[None, :]).astype(jnp.int32), axis=0) - 1
    patch_row, patch_col = byte_patch[None, :], byte_patch[:, None]
    patches = jnp.arange(P_SIZE, dtype=jnp.int32)
    member = (patches[:, None] == patch_row).astype(bf16)
    member_byte = (patches[None, :] == patch_col).astype(bf16)
    counts = lengths.astype(f32)[:, None]
    valid = (patches < row_length)[:, None]

    own_cotangent = lax.dynamic_index_in_dim(cotangent[0], section, 0, keepdims=False)
    sent_cotangent = swap(lax.dynamic_index_in_dim(cotangent[0], 1 - section, 0, keepdims=False))
    cotangent_one = jnp.where(first_core, own_cotangent, sent_cotangent).astype(f32)
    cotangent_two = jnp.where(first_core, sent_cotangent, own_cotangent).astype(f32)

    def both_layers(one, two):
        pooled = dot(member, byte_rows) / counts
        normed_one, inverse_one = normalize(pooled, gains[0, 0])
        queries_one = dot(normed_one, one[0][:, :D]).astype(bf16)
        byte_pairs = dot(byte_rows, one[0][:, D:]).astype(bf16)
        attention_one, attended_one = patch_attention(patch_row, patch_col, queries_one, byte_pairs)
        middle_one = pooled + dot(attended_one, one[1])
        result_one, kept_one = feed_forward(middle_one, gains[0, 1], one[2], one[3])
        encoded = jnp.where(valid, result_one, pooled).astype(bf16)

        inputs_two = encoded.astype(f32)
        normed_two, inverse_two = normalize(inputs_two, gains[1, 0])
        mixed = dot(normed_two, two[0]).astype(bf16)
        attended_two = causal_attention(mixed)
        middle_two = inputs_two + dot(attended_two, two[1])
        result_two, kept_two = feed_forward(middle_two, gains[1, 1], two[2], two[3])
        final = jnp.where(valid, result_two, inputs_two).astype(bf16)
        grad_kept = jnp.where(valid, cotangent_two, 0.0)
        grad_middle, gain_two_second, grad_joined, grad_branch = feed_back(
            middle_two, gains[1, 1], two[2], two[3], kept_two, grad_kept
        )
        grad_low = grad_middle.astype(bf16)
        factors_two = [normed_two, attended_two, kept_two[0], grad_branch, None, grad_low, grad_joined, kept_two[3]]
        grad_attended = dot_nt(grad_low, two[1]).astype(bf16)
        grad_mixed = causal_attention_back(mixed, grad_attended)
        grad_normed = dot_nt(grad_mixed, two[0])
        grad_in, gain_two_first = normalize_back(inputs_two, gains[1, 0], inverse_two, grad_normed)
        grad_encoded = jnp.where(valid, 0.0, cotangent_two) + grad_middle + grad_in


        grad_out = cotangent_one + grad_encoded.astype(bf16).astype(f32)
        grad_kept = jnp.where(valid, grad_out, 0.0)
        grad_middle, gain_one_second, grad_joined, grad_branch = feed_back(
            middle_one, gains[0, 1], one[2], one[3], kept_one, grad_kept
        )
        grad_low = grad_middle.astype(bf16)
        factors_one = [normed_one, attended_one, kept_one[0], grad_branch, None, grad_low, grad_joined, kept_one[3]]
        grad_attended = dot_nt(grad_low, one[1]).astype(bf16)
        grad_queries, grad_pairs = patch_attention_back(
            patch_row, patch_col, queries_one, byte_pairs, attention_one, grad_attended
        )
        grad_normed = dot_nt(grad_queries, one[0][:, :D])
        grad_in, gain_one_first = normalize_back(pooled, gains[0, 0], inverse_one, grad_normed)
        grad_pooled = jnp.where(valid, 0.0, grad_out) + grad_middle + grad_in
        grad_bytes = dot(member_byte, (grad_pooled / counts).astype(bf16))
        grad_bytes = (grad_bytes + dot_nt(grad_pairs, one[0][:, D:])).astype(bf16)

        factors_two[4], factors_one[4] = grad_mixed, grad_queries
        gain_part = jnp.stack([gain_one_first, gain_one_second, gain_two_first, gain_two_second])
        return encoded, final, factors_two, factors_one, grad_pairs, grad_bytes, gain_part

    encoded, final, factors_two, factors_one, grad_pairs, grad_bytes, gain_part = lax.cond(
        first_core, both_layers, lambda one, two: both_layers(two, one), weights, other_weights
    )
    sent_out = swap(jnp.where(first_core, final, encoded))
    kept_out = jnp.where(first_core, encoded, final)
    section_out = jnp.where(
        first_core, jnp.stack([kept_out, sent_out]), jnp.stack([sent_out, kept_out])
    )[None]

    gain_part = jnp.pad(gain_part.reshape(8, half_width), ((8, 0), (0, 0)))
    sums, theirs, gathered, sorted_rows = backward_sums(
        factors_two,
        factors_one,
        byte_rows,
        grad_pairs,
        grad_bytes,
        slots,
        places,
        flat_bytes[None, :],
        gain_part,
        table_rows,
    )
    hash_grad = place_rows(sorted_ids, sorted_rows, shard_rows)
    gathered = gathered.reshape(-1, half_width)
    byte_table_grad = gathered[:table_rows].astype(f32)
    first_gain = table_rows // 16 * 16 + 8
    gain_sums = gathered[first_gain : first_gain + 8].reshape(2, 2, D)
    gain_sums = (gain_sums.astype(f32) + swap(gain_sums).astype(f32)).reshape(2, 2, devices, -1)
    gains_grad = lax.dynamic_index_in_dim(gain_sums, section, 0, keepdims=True)
    gains_grad = lax.dynamic_index_in_dim(gains_grad, lax.axis_index("rows"), 2, keepdims=False)

    mine = lax.dynamic_index_in_dim(sums, section, 0, keepdims=False)
    lower = jnp.where(first_core, mine, theirs).astype(f32)
    upper = jnp.where(first_core, theirs, mine).astype(f32)
    half, half_ff = D // 2, FF // 2
    gate_up_grad = jnp.concatenate([lower[:, :FF], upper[:, :FF]], axis=1)
    down_grad = jnp.concatenate([lower[:, FF : FF + half_ff], upper[:, FF : FF + half_ff]], axis=1).T
    low_rest, high_rest = lower[:, FF + half_ff :], upper[:, FF + half_ff :]
    columns = []
    for index in range(4):
        part = slice(index * half, (index + 1) * half)
        columns.append(jnp.concatenate([low_rest[:, part], high_rest[:, part]], axis=1))
    qkv_grad = jnp.concatenate(columns[:3], axis=1)
    out_grad = columns[3]

    return (
        section_out,
        byte_table_grad,
        hash_grad,
        gains_grad,
        qkv_grad[None],
        out_grad[None],
        gate_up_grad[None],
        down_grad[None],
    )


def solution(mesh):
    return jax.shard_map(
        on_device,
        mesh=mesh,
        in_specs=(
            P("rows", None),
            P("rows", None, None),
            P("rows", None),
            P("rows"),
            P(None, "section"),
            P(None, "rows", "section"),
            P("section", None, None),
            P("section", None, None),
            P("section", None, None),
            P("section", None, None),
            P("section", None, None),
            P("section", "rows", None, None),
        ),
        out_specs=(
            P("section", "rows", None, None),
            P(None, "section"),
            P(None, "rows", "section"),
            P("section", None, "rows"),
            P("section", "rows", None),
            P("section", "rows", None),
            P("section", "rows", None),
            P("section", None, "rows"),
        ),
        check_vma=False,
    )
```

```python
import functools

import jax
import jax.numpy as jnp
from jax import lax
from jax.experimental import pallas as pl
from jax.experimental.pallas import tpu as pltpu
from jax.sharding import PartitionSpec as P

D = 1024
HEADS = 16
HEAD = 64
FF = 2816
L = 1024
MOST = 16
M = 2
P_SIZE = 256
GROUP = 512
VMEM_BYTES = 48 * 1024 * 1024
FAR_FIRST = (4, 12, 8, 5, 11, 7, 9, 6, 10, 3, 13, 2, 14, 1, 15)
SORT_TURN = 3

epsilon = 1e-05
f32 = jnp.float32
bf16 = jnp.bfloat16


def dot(left, right):
    return jnp.dot(left, right, preferred_element_type=f32)


def dot_nt(left, right):
    return lax.dot_general(left, right, (((1,), (1,)), ((), ())), preferred_element_type=f32)


def dot_tn(left, right):
    return lax.dot_general(left, right, (((0,), (0,)), ((), ())), preferred_element_type=f32)


def params(*semantics):
    return pltpu.CompilerParams(vmem_limit_bytes=VMEM_BYTES, dimension_semantics=semantics)


def as_column(row):
    shape = (row.shape[1], row.shape[1])
    same = lax.broadcasted_iota(jnp.int32, shape, 0) == lax.broadcasted_iota(jnp.int32, shape, 1)
    return jnp.sum(jnp.where(same, jnp.broadcast_to(row, shape), 0), axis=1, keepdims=True)


def gather_kernel(devices, *refs):
    requests_ref, tables_ref, slots_ref, ids_ref, bytes_ref = refs[:5]
    weights, refs = refs[5:9], refs[9:]
    out_ref, requested_ref = refs[:2]
    layers, refs = refs[2:6], refs[6:]
    held_ref, staged_ref, landed_ref, part_ref, total_ref, mine_ref, theirs_ref = refs[:7]
    load_sems, ask_send, ask_land, send_sems, land_sems, last_sems = refs[7:13]
    weight_send, weight_land = refs[13:]
    count_tables, shard_rows, half = tables_ref.shape
    each = requests_ref.shape[2]
    bits = devices.bit_length() - 1

    me = lax.axis_index("rows")
    section = lax.axis_index("section")
    partner = 1 - section
    mesh_id = pl.DeviceIdType.MESH
    places = [(me // 2**d) % 2 for d in range(bits)]

    def across(step):
        device = me
        for d in range(bits):
            if step // 2**d % 2:
                device = device + (1 - 2 * places[d]) * 2**d
        return device

    steps = [0]
    for d in range(bits):
        steps = list(range(2**d, 2 ** (d + 1))) + steps

    def load(table):
        return pltpu.make_async_copy(tables_ref.at[table], held_ref.at[table], load_sems.at[table])

    for table in range(count_tables):
        load(table).start()

    barrier = pltpu.get_barrier_semaphore()
    pl.semaphore_signal(barrier, inc=1, device_id={"section": partner}, device_id_type=mesh_id)
    for step in range(1, devices):
        pl.semaphore_signal(barrier, inc=1, device_id={"rows": across(step)}, device_id_type=mesh_id)
    pl.semaphore_wait(barrier, devices)

    def remote(source, target, send, land, **device):
        return pltpu.make_async_remote_copy(
            src_ref=source, dst_ref=target, send_sem=send, recv_sem=land, device_id=device, device_id_type=mesh_id
        )

    def ask(step):
        return remote(
            requests_ref.at[across(step)],
            requested_ref.at[me],
            ask_send.at[step - 1],
            ask_land.at[step - 1],
            rows=across(step),
        )

    def asked(step):
        return remote(
            requests_ref.at[across(step)],
            requested_ref.at[across(step)],
            ask_send.at[step - 1],
            ask_land.at[step - 1],
            rows=across(step),
        )

    for step in range(1, devices):
        ask(step).start()
    requested_ref[me] = requests_ref[me]

    def shared(index):
        return remote(
            weights[index],
            layers[index],
            weight_send.at[index],
            weight_land.at[index],
            section=partner,
        )

    tile = 512
    def own_row(index, carry):
        at = pl.ds(pl.multiple_of(index * tile, tile), tile)
        words = lax.broadcasted_iota(jnp.int32, (tile, bytes_ref.shape[0]), 1)
        word = (words == ids_ref[at, :]).astype(f32).astype(bf16)
        total_ref[at, :] = dot(word, bytes_ref[...])
        return carry

    lax.fori_loop(0, M * L // tile, own_row, 0)
    for step in range(1, devices):
        asked(step).wait_recv()

    groups = 4
    size = devices // groups

    def send(position, table):
        step = steps[position]
        slot = position * count_tables + table
        return remote(
            staged_ref.at[table, position],
            landed_ref.at[table, position],
            send_sems.at[slot],
            land_sems.at[slot],
            rows=across(step),
        )

    def find(table, group):
        positions = range(group * size, (group + 1) * size)
        ids = jnp.concatenate(
            [as_column(requested_ref[across(steps[p]), table : table + 1, :]) for p in positions], axis=0
        )
        depth = 1024
        part_ref[...] = jnp.zeros_like(part_ref)

        def body(index, carry):
            first = pl.multiple_of(index * depth, depth)
            places_in = first + lax.broadcasted_iota(jnp.int32, (size * each, depth), 1)
            chosen = (places_in == ids).astype(f32).astype(bf16)
            part_ref[...] += dot(chosen, held_ref[table, pl.ds(first, depth), :])
            return carry

        lax.fori_loop(0, shard_rows // depth, body, 0)
        for index, position in enumerate(positions):
            block = part_ref[index * each : (index + 1) * each, :].astype(bf16)
            if steps[position]:
                staged_ref[table, position] = block
                send(position, table).start()
            else:
                landed_ref[table, position] = block

    def combine(table, group):
        positions = range(group * size, (group + 1) * size)
        for position in positions:
            if steps[position]:
                send(position, table).wait_recv()
        rows = landed_ref[table, group * size : (group + 1) * size].reshape(size * each, half)
        slots = jnp.concatenate(
            [slots_ref[across(steps[p]), table : table + 1, :] for p in positions], axis=1
        )

        def body(index, carry):
            at = pl.ds(pl.multiple_of(index * tile, tile), tile)
            places_in = index * tile + lax.broadcasted_iota(jnp.int32, (tile, size * each), 0)
            chosen = (places_in == slots).astype(f32).astype(bf16)
            total_ref[at, :] += dot(chosen, rows)
            return carry

        lax.fori_loop(0, M * L // tile, body, 0)

    for index in range(len(weights)):
        shared(index).start()
    far, near = (0, 1), (2, 3)
    for table in range(count_tables):
        load(table).wait()
        for group in far:
            find(table, group)
    for table in range(count_tables):
        for group in near:
            find(table, group)
    for table in range(count_tables):
        for group in near:
            combine(table, group)
    for table in range(count_tables):
        for group in far:
            combine(table, group)

    theirs_ref[...] = total_ref[pl.ds(pl.multiple_of(partner * L, L), L), :].astype(bf16)
    mine = out_ref.at[:, pl.ds(pl.multiple_of(section * half, half), half)]
    last = remote(theirs_ref, mine, last_sems.at[0], last_sems.at[1], section=partner)
    last.start()
    mine_ref[...] = total_ref[pl.ds(pl.multiple_of(section * L, L), L), :].astype(bf16)
    own = pltpu.make_async_copy(mine_ref, mine, last_sems.at[2])
    own.start()
    for step in range(1, devices):
        ask(step).wait_send()
    for position in range(devices):
        for table in range(count_tables):
            if steps[position]:
                send(position, table).wait_send()
    for index in range(len(weights)):
        shared(index).wait()
    own.wait()
    last.wait()


def gather_rows(requests, tables, slots, ids, table, weights):
    devices, count_tables, each = requests.shape
    half = tables.shape[2]
    vmem = pl.BlockSpec(memory_space=pltpu.VMEM)
    any_space = pl.BlockSpec(memory_space=pl.ANY)
    dma = pltpu.SemaphoreType.DMA
    blocks = (count_tables, devices, each, half)
    return pl.pallas_call(
        functools.partial(gather_kernel, devices),
        in_specs=[vmem, any_space, vmem, vmem, vmem] + [any_space] * len(weights),
        out_specs=[vmem, vmem] + [any_space] * len(weights),
        out_shape=[
            jax.ShapeDtypeStruct((L, 2 * half), bf16),
            jax.ShapeDtypeStruct(requests.shape, jnp.int32),
            *[jax.ShapeDtypeStruct(weight.shape, weight.dtype) for weight in weights],
        ],
        scratch_shapes=[
            pltpu.VMEM(tables.shape, bf16),
            pltpu.VMEM(blocks, bf16),
            pltpu.VMEM(blocks, bf16),
            pltpu.VMEM((devices // 4 * each, half), f32),
            pltpu.VMEM((M * L, half), f32),
            pltpu.VMEM((L, half), bf16),
            pltpu.VMEM((L, half), bf16),
            dma((count_tables,)),
            dma((devices - 1,)),
            dma((devices - 1,)),
            dma((devices * count_tables,)),
            dma((devices * count_tables,)),
            dma((3,)),
            *[dma((len(weights),))] * 2,
        ],
        compiler_params=pltpu.CompilerParams(
            collective_id=1, has_side_effects=True, vmem_limit_bytes=56 * 1024 * 1024
        ),
        cost_estimate=pl.CostEstimate(flops=5 * 10**10, bytes_accessed=4 * 10**8, transcendentals=0),
        name="gather_rows",
    )(requests, tables, slots, ids, table, *weights)


def head_marks(heads, width):
    feature = lax.shift_right_logical(lax.broadcasted_iota(jnp.int32, (heads, width), 1), 6)
    return (feature == lax.broadcasted_iota(jnp.int32, (heads, width), 0)).astype(f32).astype(bf16)


def patch_marks(patch_row_ref, patch_col_ref):
    by_patch = (
        lax.broadcasted_iota(jnp.int32, (P_SIZE, L), 0) == patch_row_ref[...]
    ).astype(f32).astype(bf16)
    by_byte = (
        lax.broadcasted_iota(jnp.int32, (L, P_SIZE), 1) == patch_col_ref[...]
    ).astype(f32).astype(bf16)
    return by_patch, by_byte


def per_head(marks, products):
    high = products.astype(bf16)
    low = (products - high.astype(f32)).astype(bf16)
    return dot_nt(marks, high) + dot_nt(marks, low)


def neighbours(patches, heads):
    wide = jnp.broadcast_to(patches, (heads, L))
    back = [(d, pltpu.roll(wide, d, 1) == wide) for d in (1, 2, 4, 8)]
    ahead = [(L - d, pltpu.roll(wide, L - d, 1) == wide) for d in (1, 2, 4, 8)]
    return back, ahead


def scan_max(values, steps):
    for distance, same in steps:
        values = jnp.where(same, jnp.maximum(values, pltpu.roll(values, distance, 1)), values)
    return values


def scan_sum(values, steps):
    for distance, same in steps:
        values = jnp.where(same, values + pltpu.roll(values, distance, 1), values)
    return values


def patch_attention_kernel(
    patch_row_ref, patch_col_ref, query_ref, key_ref, value_ref, attention_ref, attended_ref
):
    heads, width = attention_ref.shape[0], query_ref.shape[1]
    marks = head_marks(heads, width)
    by_patch, by_byte = patch_marks(patch_row_ref, patch_col_ref)
    queries = dot(by_byte, query_ref[...])
    scores = per_head(marks, queries * key_ref[...].astype(f32)) * 0.125
    back, ahead = neighbours(patch_row_ref[...], heads)
    top = scan_max(scan_max(scores, back), ahead)
    shifted = jnp.exp(scores - top)
    total = scan_sum(shifted, back) + scan_sum(shifted, ahead) - shifted
    attention = shifted / total
    attention_ref[...] = attention
    weights = dot_tn(attention.astype(bf16), marks)
    weighted = (weights * value_ref[...].astype(f32)).astype(bf16)
    attended_ref[...] = dot(by_patch, weighted).astype(bf16)


def patch_attention(patch_row, patch_col, queries, key_value):
    groups = D // GROUP
    return pl.pallas_call(
        patch_attention_kernel,
        grid=(groups,),
        in_specs=[
            pl.BlockSpec((1, L), lambda i: (0, 0)),
            pl.BlockSpec((L, 1), lambda i: (0, 0)),
            pl.BlockSpec((P_SIZE, GROUP), lambda i: (0, i)),
            pl.BlockSpec((L, GROUP), lambda i: (0, i)),
            pl.BlockSpec((L, GROUP), lambda i: (0, i + groups)),
        ],
        out_specs=[
            pl.BlockSpec((HEADS // groups, L), lambda i: (i, 0)),
            pl.BlockSpec((P_SIZE, GROUP), lambda i: (0, i)),
        ],
        out_shape=[
            jax.ShapeDtypeStruct((HEADS, L), f32),
            jax.ShapeDtypeStruct((P_SIZE, D), bf16),
        ],
        compiler_params=params("arbitrary"),
        cost_estimate=pl.CostEstimate(flops=4 * 10**9, bytes_accessed=6 * 10**6, transcendentals=16384),
        name="patch_attention",
    )(patch_row, patch_col, queries, key_value, key_value)


def patch_attention_back_kernel(
    patch_row_ref,
    patch_col_ref,
    query_ref,
    key_ref,
    value_ref,
    attention_ref,
    grad_ref,
    grad_query_ref,
    grad_pair_ref,
):
    heads, width = attention_ref.shape[0], query_ref.shape[1]
    first = pl.multiple_of(pl.program_id(0) * width, width)
    marks = head_marks(heads, width)
    by_patch, by_byte = patch_marks(patch_row_ref, patch_col_ref)
    grads = dot(by_byte, grad_ref[...])
    attention = attention_ref[...]
    grad_attention = per_head(marks, grads * value_ref[...].astype(f32))
    weights = dot_tn(attention.astype(bf16), marks)
    grad_pair_ref[:, pl.ds(D + first, width)] = (weights * grads).astype(bf16)
    back, ahead = neighbours(patch_row_ref[...], heads)
    terms = attention * grad_attention
    total = scan_sum(terms, back) + scan_sum(terms, ahead) - terms
    grad_scores = (attention * (grad_attention - total)).astype(bf16)
    spread_scores = dot_tn(grad_scores, marks) * 0.125
    grad_pair_ref[:, pl.ds(first, width)] = (spread_scores * dot(by_byte, query_ref[...])).astype(bf16)
    weighted = (spread_scores * key_ref[...].astype(f32)).astype(bf16)
    grad_query_ref[...] = dot(by_patch, weighted).astype(bf16)


def patch_attention_back(patch_row, patch_col, queries, key_value, attention, grad_attended):
    groups = D // GROUP
    byte_block = pl.BlockSpec((L, GROUP), lambda i: (0, i))
    patch_block = pl.BlockSpec((P_SIZE, GROUP), lambda i: (0, i))
    return pl.pallas_call(
        patch_attention_back_kernel,
        grid=(groups,),
        in_specs=[
            pl.BlockSpec((1, L), lambda i: (0, 0)),
            pl.BlockSpec((L, 1), lambda i: (0, 0)),
            patch_block,
            byte_block,
            pl.BlockSpec((L, GROUP), lambda i: (0, i + groups)),
            pl.BlockSpec((HEADS // groups, L), lambda i: (i, 0)),
            patch_block,
        ],
        out_specs=[patch_block, pl.BlockSpec((L, 2 * D), lambda i: (0, 0))],
        out_shape=[
            jax.ShapeDtypeStruct((P_SIZE, D), bf16),
            jax.ShapeDtypeStruct((L, 2 * D), bf16),
        ],
        compiler_params=params("arbitrary"),
        cost_estimate=pl.CostEstimate(flops=6 * 10**9, bytes_accessed=10 * 10**6, transcendentals=0),
        name="patch_attention_back",
    )(patch_row, patch_col, queries, key_value, key_value, attention, grad_attended)


def causal_softmax(queries, keys):
    scores = dot_nt(queries, keys) * 0.125
    size = scores.shape[0]
    allowed = lax.broadcasted_iota(jnp.int32, (size, size), 0) >= lax.broadcasted_iota(
        jnp.int32, (size, size), 1
    )
    scores = jnp.where(allowed, scores, -jnp.inf)
    shifted = jnp.exp(scores - jnp.max(scores, axis=-1, keepdims=True))
    return shifted / jnp.sum(shifted, axis=-1, keepdims=True)


def pair_masks(shape):
    lane = lax.broadcasted_iota(jnp.int32, shape, 1)
    return [lane < HEAD, lane >= HEAD]


def causal_kernel(query_ref, key_ref, value_ref, out_ref):
    queries, keys, values = query_ref[...], key_ref[...], value_ref[...]
    masks = pair_masks(queries.shape)
    parts = []
    for mask in masks:
        attention = causal_softmax(jnp.where(mask, queries, 0), keys).astype(bf16)
        parts.append(dot(attention, values))
    out_ref[...] = jnp.where(masks[0], parts[0], parts[1]).astype(bf16)


def causal_attention(mixed):
    pairs = HEADS // 2
    return pl.pallas_call(
        causal_kernel,
        grid=(pairs,),
        in_specs=[
            pl.BlockSpec((P_SIZE, 2 * HEAD), lambda i: (0, i)),
            pl.BlockSpec((P_SIZE, 2 * HEAD), lambda i: (0, i + pairs)),
            pl.BlockSpec((P_SIZE, 2 * HEAD), lambda i: (0, i + 2 * pairs)),
        ],
        out_specs=pl.BlockSpec((P_SIZE, 2 * HEAD), lambda i: (0, i)),
        out_shape=jax.ShapeDtypeStruct((P_SIZE, D), bf16),
        compiler_params=params("arbitrary"),
        cost_estimate=pl.CostEstimate(flops=2 * 10**9, bytes_accessed=2 * 10**6, transcendentals=10**6),
        name="causal_attention",
    )(mixed, mixed, mixed)


def causal_back_kernel(query_ref, key_ref, value_ref, grad_ref, out_ref):
    pair = pl.program_id(0) * 2 * HEAD
    queries, keys, values, grads = query_ref[...], key_ref[...], value_ref[...], grad_ref[...]
    masks = pair_masks(queries.shape)
    results = []
    for mask in masks:
        attention = causal_softmax(jnp.where(mask, queries, 0), keys)
        grad_attention = dot_nt(jnp.where(mask, grads, 0), values)
        total = jnp.sum(attention * grad_attention, axis=-1, keepdims=True)
        grad_scores = (attention * (grad_attention - total)).astype(bf16)
        results.append(
            (
                dot(grad_scores, keys) * 0.125,
                dot_tn(grad_scores, queries) * 0.125,
                dot_tn(attention.astype(bf16), grads),
            )
        )
    for index, (first, second) in enumerate(zip(results[0], results[1])):
        columns = pl.ds(pl.multiple_of(index * D + pair, 2 * HEAD), 2 * HEAD)
        out_ref[:, columns] = jnp.where(masks[0], first, second).astype(bf16)


def causal_attention_back(mixed, grad_attended):
    pairs = HEADS // 2
    block = pl.BlockSpec((P_SIZE, 2 * HEAD), lambda i: (0, i))
    return pl.pallas_call(
        causal_back_kernel,
        grid=(pairs,),
        in_specs=[
            block,
            pl.BlockSpec((P_SIZE, 2 * HEAD), lambda i: (0, i + pairs)),
            pl.BlockSpec((P_SIZE, 2 * HEAD), lambda i: (0, i + 2 * pairs)),
            block,
        ],
        out_specs=pl.BlockSpec((P_SIZE, 3 * D), lambda i: (0, 0)),
        out_shape=jax.ShapeDtypeStruct((P_SIZE, 3 * D), bf16),
        compiler_params=params("arbitrary"),
        cost_estimate=pl.CostEstimate(flops=4 * 10**9, bytes_accessed=4 * 10**6, transcendentals=10**6),
        name="causal_attention_back",
    )(mixed, mixed, mixed, grad_attended)


def normalize(inputs, gain):
    inverse = lax.rsqrt(jnp.mean(inputs * inputs, axis=-1, keepdims=True) + epsilon)
    return (inputs * inverse * gain).astype(bf16), inverse


def normalize_back(inputs, gain, inverse, grad_normed):
    scaled = inputs * inverse
    grad_gain = jnp.sum(grad_normed * scaled, axis=0)
    grad_scaled = grad_normed * gain
    grad_inputs = inverse * (
        grad_scaled - scaled * jnp.mean(grad_scaled * scaled, axis=-1, keepdims=True)
    )
    return grad_inputs, grad_gain


def feed_kernel(
    hidden_ref, gain_ref, w_gate_ref, w_up_ref, w_down_ref, out_ref, normed_ref, gate_ref, up_ref, inner_ref
):
    @pl.when(pl.program_id(0) == 0)
    def _():
        hidden = hidden_ref[...]
        normed_ref[...] = normalize(hidden, gain_ref[...])[0]
        out_ref[...] = hidden

    gate, up = dot(normed_ref[...], w_gate_ref[...]), dot(normed_ref[...], w_up_ref[...])
    inner = (gate * jax.nn.sigmoid(gate) * up).astype(bf16)
    gate_ref[...] = gate.astype(bf16)
    up_ref[...] = up.astype(bf16)
    inner_ref[...] = inner
    out_ref[...] += dot(inner, w_down_ref[...])


def feed_specs():
    tile = FF // 2
    tiles = FF // tile
    whole = pl.BlockSpec((P_SIZE, D), lambda j: (0, 0))
    row = pl.BlockSpec((1, D), lambda j: (0, 0))
    gate = pl.BlockSpec((D, tile), lambda j: (0, j))
    up = pl.BlockSpec((D, tile), lambda j: (0, j + tiles))
    down = pl.BlockSpec((tile, D), lambda j: (j, 0))
    part = pl.BlockSpec((P_SIZE, tile), lambda j: (0, j))
    return tiles, whole, row, gate, up, down, part


def feed_forward(hidden, gain, w_gate_up, w_down):
    tiles, whole, row, gate, up, down, part = feed_specs()
    narrow = jax.ShapeDtypeStruct((P_SIZE, FF), bf16)
    out, normed, gates, ups, inner = pl.pallas_call(
        feed_kernel,
        grid=(tiles,),
        in_specs=[whole, row, gate, up, down],
        out_specs=[whole, whole, part, part, part],
        out_shape=[
            jax.ShapeDtypeStruct((P_SIZE, D), f32),
            jax.ShapeDtypeStruct((P_SIZE, D), bf16),
            narrow,
            narrow,
            narrow,
        ],
        compiler_params=params("arbitrary"),
        cost_estimate=pl.CostEstimate(flops=6 * P_SIZE * D * FF, bytes_accessed=24 * 10**6, transcendentals=P_SIZE * FF),
        name="feed_forward",
    )(hidden, gain[None, :], w_gate_up, w_gate_up, w_down)
    return out, (normed, gates, ups, inner)


def feed_back_kernel(
    grad_ref,
    hidden_ref,
    gain_ref,
    gate_ref,
    up_ref,
    w_gate_ref,
    w_up_ref,
    w_down_ref,
    out_ref,
    low_ref,
    branch_ref,
    joined_ref,
    grad_gain_ref,
    total_ref,
):
    step = pl.program_id(0)
    tile = gate_ref.shape[1]

    @pl.when(step == 0)
    def _():
        branch_ref[...] = grad_ref[...].astype(bf16)
        total_ref[...] = jnp.zeros_like(total_ref)

    grad_inner = dot_nt(branch_ref[...], w_down_ref[...])
    gate, up = gate_ref[...].astype(f32), up_ref[...].astype(f32)
    sigmoid = jax.nn.sigmoid(gate)
    grad_gate = (grad_inner * up * sigmoid * (1.0 + gate * (1.0 - sigmoid))).astype(bf16)
    grad_up = (grad_inner * gate * sigmoid).astype(bf16)
    joined_ref[:, pl.ds(pl.multiple_of(step * tile, 128), tile)] = grad_gate
    joined_ref[:, pl.ds(pl.multiple_of(FF + step * tile, 128), tile)] = grad_up
    total_ref[...] += dot_nt(grad_gate, w_gate_ref[...]) + dot_nt(grad_up, w_up_ref[...])

    @pl.when(step == pl.num_programs(0) - 1)
    def _():
        hidden = hidden_ref[...]
        inverse = lax.rsqrt(jnp.mean(hidden * hidden, axis=-1, keepdims=True) + epsilon)
        grad_in, grad_gain = normalize_back(hidden, gain_ref[...], inverse, total_ref[...])
        result = grad_ref[...] + grad_in
        out_ref[...] = result
        low_ref[...] = result.astype(bf16)
        grad_gain_ref[...] = grad_gain[None, :]


def feed_back(hidden, gain, w_gate_up, w_down, kept, grad_out):
    normed, gates, ups, inner = kept
    tiles, whole, row, gate, up, down, part = feed_specs()
    out, low, branch, joined, grad_gain = pl.pallas_call(
        feed_back_kernel,
        grid=(tiles,),
        in_specs=[whole, whole, row, part, part, gate, up, down],
        out_specs=[whole, whole, whole, pl.BlockSpec((P_SIZE, 2 * FF), lambda j: (0, 0)), row],
        out_shape=[
            jax.ShapeDtypeStruct((P_SIZE, D), f32),
            jax.ShapeDtypeStruct((P_SIZE, D), bf16),
            jax.ShapeDtypeStruct((P_SIZE, D), bf16),
            jax.ShapeDtypeStruct((P_SIZE, 2 * FF), bf16),
            jax.ShapeDtypeStruct((1, D), f32),
        ],
        scratch_shapes=[pltpu.VMEM((P_SIZE, D), f32)],
        compiler_params=params("arbitrary"),
        cost_estimate=pl.CostEstimate(flops=6 * P_SIZE * D * FF, bytes_accessed=24 * 10**6, transcendentals=P_SIZE * FF),
        name="feed_back",
    )(grad_out, hidden, gain[None, :], gates, ups, w_gate_up, w_gate_up, w_down)
    return out, low, grad_gain[0], joined, branch


def byte_grad_kernel(patch_col_ref, grad_ref, keys_ref, values_ref, w_key_ref, w_value_ref, out_ref):
    tile = out_ref.shape[0]
    owner = lax.broadcasted_iota(jnp.int32, (tile, P_SIZE), 1)
    member = (owner == patch_col_ref[...]).astype(f32).astype(bf16)
    total = dot(member, grad_ref[...]) + dot_nt(keys_ref[...], w_key_ref[...])
    out_ref[...] = (total + dot_nt(values_ref[...], w_value_ref[...])).astype(bf16)


def byte_grads(patch_col, grad_patches, grad_pairs, w_qkv):
    tile = 256
    part = lambda column: pl.BlockSpec((tile, D), lambda i: (i, column))
    weight = lambda column: pl.BlockSpec((D, D), lambda i: (0, column))
    return pl.pallas_call(
        byte_grad_kernel,
        grid=(L // tile,),
        in_specs=[
            pl.BlockSpec((tile, 1), lambda i: (i, 0)),
            pl.BlockSpec((P_SIZE, D), lambda i: (0, 0)),
            part(0),
            part(1),
            weight(1),
            weight(2),
        ],
        out_specs=pl.BlockSpec((tile, D), lambda i: (i, 0)),
        out_shape=jax.ShapeDtypeStruct((L, D), bf16),
        compiler_params=params("arbitrary"),
        cost_estimate=pl.CostEstimate(flops=5 * L * D * D, bytes_accessed=11 * 10**6, transcendentals=0),
        name="byte_grads",
    )(patch_col, grad_patches, grad_pairs, grad_pairs, w_qkv, w_qkv)


def chip_bits(devices):
    bits = devices.bit_length() - 1
    first = tuple(reversed(range(bits)))
    return bits, {"A": first, "B": (first[1], first[0]) + first[2:], "C": first[2:4] + first[:2] + first[4:]}


def at_place(ref, axis, place):
    return ref.at[(slice(None),) * axis + (place,)]


def plan_pieces():
    ff, half = FF // 2, D // 2
    pieces = []
    for layer in (1, 0):
        pieces += [
            (layer, "A", [("gate_up", 0, ff)]),
            (layer, "A", [("gate_up", ff, ff)]),
            (layer, "B", [("down", 0, ff)]),
            (layer, "B", [("query", 0, half), ("key", 0, half)]),
            (layer, "C", [("value", 0, half), ("out", 0, half)]),
        ]
    return pieces


def backward_kernel(devices, table_rows, count_tables, *refs):
    bits, orders = chip_bits(devices)
    half, ff = D // 2, FF // 2
    rows = D // devices
    table_block = table_block_rows(devices, table_rows)
    plan = plan_pieces()
    extra = len(plan)
    pieces = extra + 1
    names = [piece[1] for piece in plan] + ["C"]
    widths = [sum(width for _, _, width in piece[2]) for piece in plan] + [half]

    layers, refs = {1: refs[:8], 0: refs[8:16]}, refs[16:]
    bytes_ref, pairs_ref, grad_ref, slots_ref, places_ref, ids_ref, gains_ref = refs[:7]
    sums_ref, theirs_ref, gathered_ref, sorted_ref, arrived_ref, staged_ref = refs[7:13]
    refs = refs[13:]
    landed, refs = {1: refs[:8], 0: refs[8:16]}, refs[16:]
    bytes_landed, pairs_landed, refs = refs[0], refs[1], refs[2:]
    owns, refs = refs[:pieces], refs[pieces:]
    lands, refs = [refs[bits * i : bits * i + bits] for i in range(pieces)], refs[bits * pieces :]
    left_ref, right_ref, total_ref, send_ref, extra_ref, own_ref, table_ref, tile_ref, block_ref = refs[:9]
    swap_send, swap_land, load_sems, grad_sems, table_sem, tile_sems, block_sems, refs = *refs[9:16], refs[16:]
    send_sems, land_sems, trade_send, trade_land, spread_send, spread_land, last_sems = refs

    me = lax.axis_index("rows")
    section = lax.axis_index("section")
    partner = 1 - section
    places = [(me // 2 ** (bits - 1 - d)) % 2 for d in range(bits)]
    peers = [me + (1 - 2 * places[d]) * 2 ** (bits - 1 - d) for d in range(bits)]

    def other(step):
        return lax.rem(me + step, devices)

    barrier = pltpu.get_barrier_semaphore()
    mesh_id = pl.DeviceIdType.MESH
    pl.semaphore_signal(barrier, inc=1, device_id={"section": partner}, device_id_type=mesh_id)
    for step in range(1, devices):
        pl.semaphore_signal(barrier, inc=1, device_id={"rows": other(step)}, device_id_type=mesh_id)
    pl.semaphore_wait(barrier, devices)

    def remote(source, target, send, land, **device):
        return pltpu.make_async_remote_copy(
            src_ref=source, dst_ref=target, send_sem=send, recv_sem=land, device_id=device, device_id_type=mesh_id
        )

    def part_of(array, index, core):
        size = array.shape[1]
        if size == 3 * D:
            first = index * D + core * half
        elif size == 2 * D:
            first = index * D + core * half
        else:
            first = core * (size // 2)
            return array.at[:, pl.ds(pl.multiple_of(first, 128), size // 2)]
        return array.at[:, pl.ds(pl.multiple_of(first, 128), half)]

    swaps = {}

    def swap_of(key, source, target):
        slot = len(swaps)
        swaps[key] = remote(source, target, swap_send.at[slot], swap_land.at[slot], section=partner)
        swaps[key].start()

    def swap_layer(layer, which):
        for index in which:
            array, target = layers[layer][index], landed[layer][index]
            if index < 4:
                swap_of((layer, index, 0), array, target)
            else:
                wide = array.shape[1] // D if index == 4 else 1
                for part in range(wide):
                    there = target.at[:, pl.ds(part * half, half)] if index == 4 else target
                    swap_of((layer, index, part), part_of(array, part, partner), there)

    ready = set()

    def settled(key):
        if key not in ready:
            ready.add(key)
            swaps[key].wait_recv()

    swap_layer(1, (2, 6, 3, 7))
    own_rows = own_ref.at[pl.ds(pl.multiple_of(section * L, L), L)]
    swap_of(("grads",), grad_ref.at[:, pl.ds(pl.multiple_of(partner * half, half), half)], own_rows)
    own_copy = pltpu.make_async_copy(
        grad_ref.at[:, pl.ds(pl.multiple_of(section * half, half), half)], own_rows, grad_sems
    )
    own_copy.start()
    swap_layer(1, (0, 1, 4, 5))
    swap_layer(0, (2, 6, 3, 7, 0, 1, 4, 5))
    swap_of(("bytes",), bytes_ref, bytes_landed)
    for part in range(2):
        swap_of(
            ("pairs", part), part_of(pairs_ref, part, partner), pairs_landed.at[:, pl.ds(part * half, half)]
        )

    def jobs_of(piece):
        layer, _, segments = plan[piece]
        own, land = layers[layer], landed[layer]
        result, column = [], 0
        for kind, first, width in segments:
            if layer == 0 and kind in ("key", "value"):
                part = 0 if kind == "key" else 1
                for chunk in range(4):
                    depth = pl.ds(chunk % 2 * 512, 512)
                    if chunk < 2:
                        left, right = bytes_ref, part_of(pairs_ref, part, section)
                        keys = []
                    else:
                        left, right = bytes_landed, pairs_landed.at[:, pl.ds(part * half, half)]
                        keys = [("bytes",), ("pairs", part)]
                    copies = [("left", left.at[depth], 0, 512), ("right", right.at[depth], 0, 512)]
                    result.append((piece, column, width, chunk, 4, keys, copies))
            else:
                index, other_index, part = {
                    "gate_up": (2, 6, 0),
                    "down": (3, 7, 0),
                    "query": (0, 4, 0),
                    "key": (0, 4, 1),
                    "value": (0, 4, 2),
                    "out": (1, 5, 0),
                }[kind]
                if other_index == 4:
                    right = part_of(own[4], part, section)
                    right_landed = land[4].at[:, pl.ds(part * half, half)]
                elif kind == "gate_up":
                    start = pl.multiple_of(section * FF + first, 128)
                    right = own[6].at[:, pl.ds(start, width)]
                    right_landed = land[6].at[:, pl.ds(first, width)]
                else:
                    right, right_landed = part_of(own[other_index], 0, section), land[other_index]
                copies = [
                    ("left", own[index], 0, P_SIZE),
                    ("left", land[index], P_SIZE, P_SIZE),
                    ("right", right, 0, P_SIZE),
                    ("right", right_landed, P_SIZE, P_SIZE),
                ]
                keys = [(layer, index, 0), (layer, other_index, part)]
                result.append((piece, column, width, 0, 1, keys, copies))
            column += width
        return result

    groups = [[i for i in range(pieces) if names[i] == name] for name in "ABC"]
    order_made = []
    for rank in range(max(len(group) for group in groups)):
        order_made += [group[rank] for group in groups if rank < len(group)]
    jobs = [job for piece in order_made if piece != extra for job in jobs_of(piece)]

    def loads(number):
        piece, column, width, chunk, chunks, keys, copies = jobs[number]
        slot = number % 2
        result = []
        for index, (side, source, first, count) in enumerate(copies):
            buffer = left_ref if side == "left" else right_ref
            columns = D if side == "left" else width
            target = buffer.at[slot, pl.ds(first, count), pl.ds(0, columns)]
            result.append(pltpu.make_async_copy(source, target, load_sems.at[slot, index]))
        return result

    def start_loads(number):
        if number < len(jobs):
            for key in jobs[number][5]:
                settled(key)
            for copy in loads(number):
                copy.start()

    slots_of = {piece: index % send_ref.shape[0] for index, piece in enumerate(order_made) if piece != extra}

    def sent_part(piece):
        if piece == extra:
            return extra_ref
        return send_ref.at[slots_of[piece]].at[(slice(None),) * bits + (pl.ds(0, widths[piece]),)]

    def store(piece, device, value, column, width):
        axis = orders[names[piece]][0]
        at = [(device // 2 ** (bits - 1 - d)) % 2 for d in range(bits)]
        bit = at.pop(axis)
        at = tuple(at) + (slice(None), pl.ds(column, width))
        target = sent_part(piece)

        @pl.when(bit == places[axis])
        def _():
            owns[piece][at] = value

        @pl.when(bit != places[axis])
        def _():
            target[at] = value

    def run_job(number):
        piece, column, width, chunk, chunks, keys, copies = jobs[number]
        slot = number % 2
        for copy in loads(number):
            copy.wait()
        start_loads(number + 1)
        tile = 128

        def body(index, carry):
            at = pl.ds(pl.multiple_of(index * tile, tile), tile)
            value = dot_tn(left_ref[slot, :, at], right_ref[slot, :, pl.ds(0, width)])
            if chunk > 0:
                value = value + total_ref[at, :]
            if chunk < chunks - 1:
                total_ref[at, :] = value
            else:
                for part in range(tile // rows):
                    block = value[part * rows : (part + 1) * rows].astype(bf16)
                    store(piece, index * (tile // rows) + part, block, column, width)
            return carry

        lax.fori_loop(0, D // tile, body, 0)

    def left_of(piece, phase):
        order = orders[names[piece]]
        return [d for d in range(bits) if d not in order[:phase]]

    def kept(piece, phase):
        order = orders[names[piece]]
        ref = owns[piece]
        for step in range(1, phase):
            ref = at_place(ref, left_of(piece, step).index(order[step]), places[order[step]])
        return ref

    def send(piece, phase):
        axis = orders[names[piece]][phase]
        if phase == 0:
            source = sent_part(piece)
        else:
            source = at_place(kept(piece, phase), left_of(piece, phase).index(axis), 1 - places[axis])
        slot = piece * bits + phase
        return remote(source, lands[piece][phase], send_sems.at[slot], land_sems.at[slot], rows=peers[axis])

    made = [0, 0]
    sent = set()

    def make(piece):
        if piece == extra:
            make_extra()
        else:
            index = order_made.index(piece)
            count = send_ref.shape[0]
            earlier = [p for p in order_made[:index] if p != extra and slots_of[p] == slots_of[piece]]
            if earlier and (earlier[-1], 0) not in sent:
                sent.add((earlier[-1], 0))
                send(earlier[-1], 0).wait_send()
            while made[0] < len(jobs) and jobs[made[0]][0] == piece:
                run_job(made[0])
                made[0] += 1
        send(piece, 0).start()

    def make_extra():
        tile = table_block
        first_gain = table_rows // 16 * 16
        positions = M * L

        def body(index, carry):
            words = index * tile + lax.broadcasted_iota(jnp.int32, (tile, positions), 0)
            chosen = (words == ids_ref[...]).astype(f32).astype(bf16)
            value = dot(chosen, own_ref[...])
            row = index * tile + lax.broadcasted_iota(jnp.int32, (tile, half), 0)
            gains = jnp.concatenate([gains_ref[...]] * (tile // 16), axis=0)
            inside = (row >= first_gain) & (row < first_gain + 16)
            value = value + jnp.where(inside, gains, 0.0)
            store(extra, index, value.astype(bf16), 0, half)
            return carry

        lax.fori_loop(0, devices, body, 0)

    def add(piece, phase):
        target = kept(piece, phase + 1)
        land = lands[piece][phase]
        leads = len(target.shape) - 2
        count = 16
        groups_in = target.shape[-2] // count

        def body(index, carry):
            at = (pl.ds(pl.multiple_of(index % groups_in * count, count), count), slice(None))
            lead = index // groups_in
            at = tuple((lead // 2 ** (leads - 1 - d)) % 2 for d in range(leads)) + at
            target[at] = (target[at].astype(f32) + land[at].astype(f32)).astype(bf16)
            return carry

        lax.fori_loop(0, 2**leads * groups_in, body, 0)

    block_rows = block_ref.shape[1]
    block_slots = block_ref.shape[0]
    block_steps = [*(FAR_FIRST if devices == 16 else range(1, devices)), 0]

    def block_copy(step):
        target = staged_ref.at[step] if step else arrived_ref.at[me]
        slot = block_steps.index(step) % block_slots
        return pltpu.make_async_copy(block_ref.at[slot], target, block_sems.at[slot])

    def trade(step):
        return remote(
            staged_ref.at[step], arrived_ref.at[me], trade_send.at[step - 1], trade_land.at[step - 1], rows=other(step)
        )

    def trade_landing(step):
        back = lax.rem(me + devices - step, devices)
        return remote(
            staged_ref.at[step], arrived_ref.at[back], trade_send.at[step - 1], trade_land.at[step - 1], rows=back
        )

    own_block = block_copy(0)

    def make_blocks():
        own_copy.wait()
        settled(("grads",))
        steps = block_steps
        behind = block_slots - 1

        def pass_on(step):
            if step:
                block_copy(step).wait()
                trade(step).start()

        for index, step in enumerate(steps):
            if index >= behind:
                pass_on(steps[index - behind])
            each = block_rows // count_tables
            where = lax.broadcasted_iota(jnp.int32, (each, M * L), 1)
            for table in range(count_tables):
                slot = as_column(slots_ref[other(step), table : table + 1, :])
                chosen = (where == slot).astype(f32).astype(bf16)
                part = pl.ds(table * each, each)
                block_ref[index % block_slots, part] = dot(chosen, own_ref[...]).astype(bf16)
            block_copy(step).start()
        for step in steps[devices - behind :]:
            pass_on(step)


    def tile_copy(table, index):
        tile = tile_ref.shape[1]
        return pltpu.make_async_copy(
            tile_ref.at[index % 2],
            sorted_ref.at[table, pl.ds(pl.multiple_of(index * tile, tile), tile)],
            tile_sems.at[index % 2],
        )

    def sort_rows(table):
        if table == 0:
            own_block.wait()
            for step in range(1, devices):
                trade_landing(step).wait_recv()
        each = block_rows // count_tables
        copy = pltpu.make_async_copy(arrived_ref.at[:, pl.ds(table * each, each)], table_ref, table_sem)
        copy.start()
        copy.wait()
        tile = tile_ref.shape[1]
        for index in range(M * L // tile):
            if index >= 2:
                tile_copy(table, index - 2).wait()
            place = lax.broadcasted_iota(jnp.int32, (tile, M * L), 1)
            wanted = as_column(places_ref[table, :, index * tile : (index + 1) * tile])
            chosen = (place == wanted).astype(f32).astype(bf16)
            rows_in = table_ref[...].reshape(M * L, half)
            tile_ref[index % 2] = dot(chosen, rows_in).astype(bf16)
            tile_copy(table, index).start()
        for index in range(M * L // tile - 2, M * L // tile):
            tile_copy(table, index).wait()

    def spreads():
        return [
            remote(
                gathered_ref.at[me],
                gathered_ref.at[me],
                spread_send.at[step - 1],
                spread_land.at[step - 1],
                rows=other(step),
            )
            for step in range(1, devices)
        ]

    def spread_landing(step):
        back = lax.rem(me + devices - step, devices)
        return remote(
            gathered_ref.at[me], gathered_ref.at[back], spread_send.at[step - 1], spread_land.at[step - 1], rows=back
        )

    def finish(piece):
        if piece == extra:
            gathered_ref[me] = kept(piece, bits)[...]
            for copy in spreads():
                copy.start()
        else:
            layer = plan[piece][0]
            first = sum(widths[p] for p in range(piece) if plan[p][0] == layer)
            sums_ref[layer, :, first : first + widths[piece]] = kept(piece, bits)[...]

    start_loads(0)
    for group in groups:
        make(group[0])
    make_blocks()
    for group in groups:
        if len(group) > 1:
            make(group[1])
    rounds = max(len(group) for group in groups)
    for turn in range(rounds + bits - 1):
        for phase in range(bits):
            for group in groups:
                if not 0 <= turn - phase < len(group):
                    continue
                piece = group[turn - phase]
                send(piece, phase).wait_recv()
                if phase == 0 and turn + 2 < len(group):
                    make(group[turn + 2])
                add(piece, phase)
                if phase + 1 < bits:
                    send(piece, phase + 1).start()
                else:
                    finish(piece)
        if 0 <= turn - SORT_TURN < count_tables:
            sort_rows(turn - SORT_TURN)

    last = remote(sums_ref.at[partner], theirs_ref, last_sems.at[0], last_sems.at[1], section=partner)
    last.start()
    for piece in range(pieces):
        for phase in range(bits):
            if (piece, phase) not in sent:
                send(piece, phase).wait_send()
    for key, copy in swaps.items():
        copy.wait_send()
        settled(key)
    for step in range(1, devices):
        trade(step).wait_send()
    for copy in spreads():
        copy.wait_send()
    for step in range(1, devices):
        spread_landing(step).wait_recv()
    last.wait()


def place_kernel(starts_ref, ids_ref, rows_ref, out_ref):
    table, tile = pl.program_id(0), pl.program_id(1)
    height, window = out_ref.shape[1], 256
    at = table * (pl.num_programs(1) + 1) + tile
    places = tile * height + lax.broadcasted_iota(jnp.int32, (height, window), 0)
    out_ref[...] = jnp.zeros(out_ref.shape, f32)

    def body(index, carry):
        part = pl.ds(pl.multiple_of(index * window, window), window)
        chosen = (places == ids_ref[0, :, part]).astype(f32).astype(bf16)
        out_ref[0] += dot(chosen, rows_ref[0, part, :])
        return carry

    lax.fori_loop(starts_ref[at] // window, (starts_ref[at + 1] + window - 1) // window, body, 0)


def place_rows(ids, rows, shard_rows):
    count_tables, count, width = rows.shape
    height = 1024
    tiles = shard_rows // height
    edges = jnp.arange(tiles + 1, dtype=jnp.int32) * height
    starts = jnp.sum((ids[:, None, :] < edges[None, :, None]).astype(jnp.int32), axis=2).reshape(-1)
    return pl.pallas_call(
        place_kernel,
        grid_spec=pltpu.PrefetchScalarGridSpec(
            num_scalar_prefetch=1,
            grid=(count_tables, tiles),
            in_specs=[
                pl.BlockSpec((1, 1, count), lambda i, j, starts: (i, 0, 0)),
                pl.BlockSpec((1, count, width), lambda i, j, starts: (i, 0, 0)),
            ],
            out_specs=pl.BlockSpec((1, height, width), lambda i, j, starts: (i, j, 0)),
        ),
        out_shape=jax.ShapeDtypeStruct((count_tables, shard_rows, width), f32),
        compiler_params=params("arbitrary", "arbitrary"),
        cost_estimate=pl.CostEstimate(flops=10**10, bytes_accessed=6 * 10**7, transcendentals=0),
        name="place_rows",
    )(starts, ids[:, None, :], rows)


def table_block_rows(devices, table_rows):
    return -(-(table_rows + 12) // (16 * devices)) * 16


def backward_sums(layer_two, layer_one, byte_rows, grad_pairs, grad_bytes, slots, places, ids, gains, table_rows):
    devices = lax.axis_size("rows")
    bits, orders = chip_bits(devices)
    rows = D // devices
    plan = plan_pieces()
    table_block = table_block_rows(devices, table_rows)
    half, ff = D // 2, FF // 2
    count_tables, each = slots.shape[1:]
    block_rows = count_tables * each
    widths = [sum(width for _, _, width in piece[2]) for piece in plan]
    shapes = [(rows, width) for width in widths] + [(table_block, half)]
    owns, lands = [], []
    for shape in shapes:
        owns.append(pltpu.VMEM((2,) * (bits - 1) + shape, bf16))
        lands += [pltpu.VMEM((2,) * (bits - 1 - phase) + shape, bf16) for phase in range(bits)]
    total = sum(widths) // 2
    landed = []
    for layer in (layer_two, layer_one):
        for index, array in enumerate(layer):
            shape = array.shape if index < 4 else (array.shape[0], array.shape[1] // 2)
            landed.append(jax.ShapeDtypeStruct(shape, bf16))
    landed += [
        jax.ShapeDtypeStruct(byte_rows.shape, bf16),
        jax.ShapeDtypeStruct((grad_pairs.shape[0], grad_pairs.shape[1] // 2), bf16),
    ]
    swaps = 2 * 7 + 3 + 1 + 4
    copies = len(shapes) * bits
    any_space = pl.BlockSpec(memory_space=pl.ANY)
    vmem = pl.BlockSpec(memory_space=pltpu.VMEM)
    blocks = jax.ShapeDtypeStruct((devices, block_rows, half), bf16)
    dma = pltpu.SemaphoreType.DMA
    results = pl.pallas_call(
        functools.partial(backward_kernel, devices, table_rows, count_tables),
        in_specs=[any_space] * 19 + [vmem] * 4,
        out_specs=[vmem, any_space, vmem] + [any_space] * (3 + len(landed)),
        out_shape=[
            jax.ShapeDtypeStruct((2, rows, total), bf16),
            jax.ShapeDtypeStruct((rows, total), bf16),
            jax.ShapeDtypeStruct((devices, table_block, half), bf16),
            jax.ShapeDtypeStruct((count_tables, M * L, half), bf16),
            blocks,
            blocks,
            *landed,
        ],
        scratch_shapes=[
            *owns,
            *lands,
            pltpu.VMEM((2, 2 * P_SIZE, D), bf16),
            pltpu.VMEM((2, 2 * P_SIZE, ff), bf16),
            pltpu.VMEM((D, half), f32),
            pltpu.VMEM((4,) + (2,) * (bits - 1) + (rows, ff), bf16),
            pltpu.VMEM((2,) * (bits - 1) + (table_block, half), bf16),
            pltpu.VMEM((M * L, half), bf16),
            pltpu.VMEM((devices, each, half), bf16),
            pltpu.VMEM((2, 256, half), bf16),
            pltpu.VMEM((3, block_rows, half), bf16),
            dma((swaps,)),
            dma((swaps,)),
            dma((2, 4)),
            dma,
            dma,
            dma((2,)),
            dma((3,)),
            dma((copies,)),
            dma((copies,)),
            dma((devices - 1,)),
            dma((devices - 1,)),
            dma((devices - 1,)),
            dma((devices - 1,)),
            dma((2,)),
        ],
        compiler_params=pltpu.CompilerParams(
            collective_id=0, has_side_effects=True, vmem_limit_bytes=60 * 1024 * 1024
        ),
        cost_estimate=pl.CostEstimate(flops=5 * 10**10, bytes_accessed=6 * 10**8, transcendentals=0),
        name="backward_sums",
    )(*layer_two, *layer_one, byte_rows, grad_pairs, grad_bytes, slots, places, ids, gains)
    return results[:4]


def swap(array):
    return lax.ppermute(array, "section", [(0, 1), (1, 0)])


def on_device(
    byte_ids,
    hash_ids,
    patch_lengths,
    row_lengths,
    byte_table,
    hash_tables,
    norm_gains,
    w_qkv,
    w_out,
    w_gate_up,
    w_down,
    cotangent,
):
    section = lax.axis_index("section")
    first_core = section == 0
    devices = lax.axis_size("rows")
    count_tables, shard_rows, half_width = hash_tables.shape
    positions = M * L

    def both(array):
        return lax.all_gather(array, "section", axis=0, tiled=True)

    flat_ids = hash_ids.reshape(positions, count_tables).T
    owners = flat_ids // shard_rows
    order_key = owners * positions + jnp.arange(positions, dtype=jnp.int32)[None, :]
    order_key, grouped = lax.sort((order_key, flat_ids % shard_rows), dimension=1, num_keys=1)

    def by_owner(array):
        return array.reshape(count_tables, devices, -1).transpose(1, 0, 2)

    byte_of_slot = order_key % positions
    numbers = jnp.arange(positions, dtype=jnp.int32)[None, :]
    flat_bytes = byte_ids.reshape(positions)
    table_rows = byte_table.shape[0]
    padded = jnp.pad(byte_table, ((0, -table_rows % 128), (0, 0)))
    slots = by_owner(byte_of_slot)
    weights = [w_qkv[0], w_out[0], w_gate_up[0], w_down[0]]
    byte_rows, requested, *other_weights = gather_rows(
        by_owner(grouped), hash_tables, slots, flat_bytes[:, None], padded, weights
    )
    gains = both(norm_gains).astype(f32)

    lengths = lax.dynamic_index_in_dim(patch_lengths, section, 0, keepdims=False)
    row_length = lax.dynamic_index_in_dim(row_lengths, section, 0, keepdims=False)
    starts = jnp.cumsum(lengths) - lengths
    byte_positions = jnp.arange(L, dtype=jnp.int32)
    byte_patch = jnp.sum((starts[:, None] <= byte_positions[None, :]).astype(jnp.int32), axis=0) - 1
    patch_row, patch_col = byte_patch[None, :], byte_patch[:, None]
    patches = jnp.arange(P_SIZE, dtype=jnp.int32)
    member = (patches[:, None] == patch_row).astype(bf16)
    counts = lengths.astype(f32)[:, None]
    valid = (patches < row_length)[:, None]

    own_cotangent = lax.dynamic_index_in_dim(cotangent[0], section, 0, keepdims=False)
    sent_cotangent = swap(lax.dynamic_index_in_dim(cotangent[0], 1 - section, 0, keepdims=False))
    cotangent_one = jnp.where(first_core, own_cotangent, sent_cotangent).astype(f32)
    cotangent_two = jnp.where(first_core, sent_cotangent, own_cotangent).astype(f32)

    def both_layers(one, two):
        pooled = dot(member, byte_rows) / counts
        normed_one, inverse_one = normalize(pooled, gains[0, 0])
        queries_one = dot(normed_one, one[0][:, :D]).astype(bf16)
        byte_pairs = dot(byte_rows, one[0][:, D:]).astype(bf16)
        attention_one, attended_one = patch_attention(patch_row, patch_col, queries_one, byte_pairs)
        middle_one = pooled + dot(attended_one, one[1])
        result_one, kept_one = feed_forward(middle_one, gains[0, 1], one[2], one[3])
        encoded = jnp.where(valid, result_one, pooled).astype(bf16)

        inputs_two = encoded.astype(f32)
        normed_two, inverse_two = normalize(inputs_two, gains[1, 0])
        mixed = dot(normed_two, two[0]).astype(bf16)
        attended_two = causal_attention(mixed)
        middle_two = inputs_two + dot(attended_two, two[1])
        result_two, kept_two = feed_forward(middle_two, gains[1, 1], two[2], two[3])
        final = jnp.where(valid, result_two, inputs_two).astype(bf16)
        grad_kept = jnp.where(valid, cotangent_two, 0.0)
        grad_middle, grad_low, gain_two_second, grad_joined, grad_branch = feed_back(
            middle_two, gains[1, 1], two[2], two[3], kept_two, grad_kept
        )
        factors_two = [normed_two, attended_two, kept_two[0], grad_branch, None, grad_low, grad_joined, kept_two[3]]
        grad_attended = dot_nt(grad_low, two[1]).astype(bf16)
        grad_mixed = causal_attention_back(mixed, grad_attended)
        grad_normed = dot_nt(grad_mixed, two[0])
        grad_in, gain_two_first = normalize_back(inputs_two, gains[1, 0], inverse_two, grad_normed)
        grad_encoded = jnp.where(valid, 0.0, cotangent_two) + grad_middle + grad_in


        grad_out = cotangent_one + grad_encoded.astype(bf16).astype(f32)
        grad_kept = jnp.where(valid, grad_out, 0.0)
        grad_middle, grad_low, gain_one_second, grad_joined, grad_branch = feed_back(
            middle_one, gains[0, 1], one[2], one[3], kept_one, grad_kept
        )
        factors_one = [normed_one, attended_one, kept_one[0], grad_branch, None, grad_low, grad_joined, kept_one[3]]
        grad_attended = dot_nt(grad_low, one[1]).astype(bf16)
        grad_queries, grad_pairs = patch_attention_back(
            patch_row, patch_col, queries_one, byte_pairs, attention_one, grad_attended
        )
        grad_normed = dot_nt(grad_queries, one[0][:, :D])
        grad_in, gain_one_first = normalize_back(pooled, gains[0, 0], inverse_one, grad_normed)
        grad_pooled = jnp.where(valid, 0.0, grad_out) + grad_middle + grad_in
        grad_bytes = byte_grads(patch_col, (grad_pooled / counts).astype(bf16), grad_pairs, one[0])

        table_ids = requested.transpose(1, 0, 2).reshape(count_tables, -1)
        id_key = lax.sort(table_ids * positions + numbers, dimension=1)
        sorted_ids = id_key // positions
        places = (id_key % positions)[:, None, :]

        factors_two[4], factors_one[4] = grad_mixed, grad_queries
        gain_part = jnp.stack([gain_one_first, gain_one_second, gain_two_first, gain_two_second])
        return encoded, final, factors_two, factors_one, grad_pairs, grad_bytes, gain_part, sorted_ids, places

    results = lax.cond(
        first_core, both_layers, lambda one, two: both_layers(two, one), weights, other_weights
    )
    encoded, final, factors_two, factors_one, grad_pairs, grad_bytes, gain_part, sorted_ids, places = results
    sent_out = swap(jnp.where(first_core, final, encoded))
    kept_out = jnp.where(first_core, encoded, final)
    section_out = jnp.where(
        first_core, jnp.stack([kept_out, sent_out]), jnp.stack([sent_out, kept_out])
    )[None]

    gain_part = jnp.pad(gain_part.reshape(8, half_width), ((8, 0), (0, 0)))
    sums, theirs, gathered, sorted_rows = backward_sums(
        factors_two,
        factors_one,
        byte_rows,
        grad_pairs,
        grad_bytes,
        slots,
        places,
        flat_bytes[None, :],
        gain_part,
        table_rows,
    )
    hash_grad = place_rows(sorted_ids, sorted_rows, shard_rows)
    gathered = gathered.reshape(-1, half_width)
    byte_table_grad = gathered[:table_rows].astype(f32)
    first_gain = table_rows // 16 * 16 + 8
    gain_sums = gathered[first_gain : first_gain + 8].reshape(2, 2, D)
    gain_sums = (gain_sums.astype(f32) + swap(gain_sums).astype(f32)).reshape(2, 2, devices, -1)
    gains_grad = lax.dynamic_index_in_dim(gain_sums, section, 0, keepdims=True)
    gains_grad = lax.dynamic_index_in_dim(gains_grad, lax.axis_index("rows"), 2, keepdims=False)

    mine = lax.dynamic_index_in_dim(sums, section, 0, keepdims=False)
    lower = jnp.where(first_core, mine, theirs).astype(f32)
    upper = jnp.where(first_core, theirs, mine).astype(f32)
    half, half_ff = D // 2, FF // 2
    gate_up_grad = jnp.concatenate([lower[:, :FF], upper[:, :FF]], axis=1)
    down_grad = jnp.concatenate([lower[:, FF : FF + half_ff], upper[:, FF : FF + half_ff]], axis=1).T
    low_rest, high_rest = lower[:, FF + half_ff :], upper[:, FF + half_ff :]
    columns = []
    for index in range(4):
        part = slice(index * half, (index + 1) * half)
        columns.append(jnp.concatenate([low_rest[:, part], high_rest[:, part]], axis=1))
    qkv_grad = jnp.concatenate(columns[:3], axis=1)
    out_grad = columns[3]

    return (
        section_out,
        byte_table_grad,
        hash_grad,
        gains_grad,
        qkv_grad[None],
        out_grad[None],
        gate_up_grad[None],
        down_grad[None],
    )


def solution(mesh):
    return jax.shard_map(
        on_device,
        mesh=mesh,
        in_specs=(
            P("rows", None),
            P("rows", None, None),
            P("rows", None),
            P("rows"),
            P(None, "section"),
            P(None, "rows", "section"),
            P("section", None, None),
            P("section", None, None),
            P("section", None, None),
            P("section", None, None),
            P("section", None, None),
            P("section", "rows", None, None),
        ),
        out_specs=(
            P("section", "rows", None, None),
            P(None, "section"),
            P(None, "rows", "section"),
            P("section", None, "rows"),
            P("section", "rows", None),
            P("section", "rows", None),
            P("section", "rows", None),
            P("section", None, "rows"),
        ),
        check_vma=False,
    )
```

```python
import functools

import jax
import jax.numpy as jnp
from jax import lax
from jax.experimental import pallas as pl
from jax.experimental.pallas import tpu as pltpu
from jax.sharding import PartitionSpec as P

D = 1024
HEADS = 16
HEAD = 64
FF = 2816
L = 1024
MOST = 16
M = 2
P_SIZE = 256
GROUP = 512
VMEM_BYTES = 48 * 1024 * 1024
FAR_FIRST = (4, 12, 8, 5, 11, 7, 9, 6, 10, 3, 13, 2, 14, 1, 15)
SORT_TURN = 3

epsilon = 1e-05
f32 = jnp.float32
bf16 = jnp.bfloat16


def dot(left, right):
    return jnp.dot(left, right, preferred_element_type=f32)


def dot_nt(left, right):
    return lax.dot_general(left, right, (((1,), (1,)), ((), ())), preferred_element_type=f32)


def dot_tn(left, right):
    return lax.dot_general(left, right, (((0,), (0,)), ((), ())), preferred_element_type=f32)


def params(*semantics):
    return pltpu.CompilerParams(vmem_limit_bytes=VMEM_BYTES, dimension_semantics=semantics)


def as_column(row):
    shape = (row.shape[1], row.shape[1])
    same = lax.broadcasted_iota(jnp.int32, shape, 0) == lax.broadcasted_iota(jnp.int32, shape, 1)
    return jnp.sum(jnp.where(same, jnp.broadcast_to(row, shape), 0), axis=1, keepdims=True)


def gather_kernel(devices, *refs):
    requests_ref, tables_ref, slots_ref, ids_ref, bytes_ref = refs[:5]
    weights, refs = refs[5:9], refs[9:]
    out_ref, requested_ref = refs[:2]
    layers, refs = refs[2:6], refs[6:]
    held_ref, staged_ref, landed_ref, part_ref, total_ref, mine_ref, theirs_ref = refs[:7]
    load_sems, ask_send, ask_land, send_sems, land_sems, last_sems = refs[7:13]
    weight_send, weight_land = refs[13:]
    count_tables, shard_rows, half = tables_ref.shape
    each = requests_ref.shape[2]
    bits = devices.bit_length() - 1

    me = lax.axis_index("rows")
    section = lax.axis_index("section")
    partner = 1 - section
    mesh_id = pl.DeviceIdType.MESH
    places = [(me // 2**d) % 2 for d in range(bits)]

    def across(step):
        device = me
        for d in range(bits):
            if step // 2**d % 2:
                device = device + (1 - 2 * places[d]) * 2**d
        return device

    steps = [0]
    for d in range(bits):
        steps = list(range(2**d, 2 ** (d + 1))) + steps

    def load(table):
        return pltpu.make_async_copy(tables_ref.at[table], held_ref.at[table], load_sems.at[table])

    for table in range(count_tables):
        load(table).start()

    barrier = pltpu.get_barrier_semaphore()
    pl.semaphore_signal(barrier, inc=1, device_id={"section": partner}, device_id_type=mesh_id)
    for step in range(1, devices):
        pl.semaphore_signal(barrier, inc=1, device_id={"rows": across(step)}, device_id_type=mesh_id)
    pl.semaphore_wait(barrier, devices)

    def remote(source, target, send, land, **device):
        return pltpu.make_async_remote_copy(
            src_ref=source, dst_ref=target, send_sem=send, recv_sem=land, device_id=device, device_id_type=mesh_id
        )

    def ask(step):
        return remote(
            requests_ref.at[across(step)],
            requested_ref.at[me],
            ask_send.at[step - 1],
            ask_land.at[step - 1],
            rows=across(step),
        )

    def asked(step):
        return remote(
            requests_ref.at[across(step)],
            requested_ref.at[across(step)],
            ask_send.at[step - 1],
            ask_land.at[step - 1],
            rows=across(step),
        )

    for step in range(1, devices):
        ask(step).start()
    requested_ref[me] = requests_ref[me]

    def shared(index):
        return remote(
            weights[index],
            layers[index],
            weight_send.at[index],
            weight_land.at[index],
            section=partner,
        )

    tile = 512
    def own_row(index, carry):
        at = pl.ds(pl.multiple_of(index * tile, tile), tile)
        words = lax.broadcasted_iota(jnp.int32, (tile, bytes_ref.shape[0]), 1)
        word = (words == ids_ref[at, :]).astype(f32).astype(bf16)
        total_ref[at, :] = dot(word, bytes_ref[...])
        return carry

    lax.fori_loop(0, M * L // tile, own_row, 0)
    for step in range(1, devices):
        asked(step).wait_recv()

    groups = 4
    size = devices // groups

    def send(position, table):
        step = steps[position]
        slot = position * count_tables + table
        return remote(
            staged_ref.at[table, position],
            landed_ref.at[table, position],
            send_sems.at[slot],
            land_sems.at[slot],
            rows=across(step),
        )

    def find(table, group):
        positions = range(group * size, (group + 1) * size)
        ids = jnp.concatenate(
            [as_column(requested_ref[across(steps[p]), table : table + 1, :]) for p in positions], axis=0
        )
        depth = 1024
        part_ref[...] = jnp.zeros_like(part_ref)

        def body(index, carry):
            first = pl.multiple_of(index * depth, depth)
            places_in = first + lax.broadcasted_iota(jnp.int32, (size * each, depth), 1)
            chosen = (places_in == ids).astype(f32).astype(bf16)
            part_ref[...] += dot(chosen, held_ref[table, pl.ds(first, depth), :])
            return carry

        lax.fori_loop(0, shard_rows // depth, body, 0)
        for index, position in enumerate(positions):
            block = part_ref[index * each : (index + 1) * each, :].astype(bf16)
            if steps[position]:
                staged_ref[table, position] = block
                send(position, table).start()
            else:
                landed_ref[table, position] = block

    def combine(table, group):
        positions = range(group * size, (group + 1) * size)
        for position in positions:
            if steps[position]:
                send(position, table).wait_recv()
        rows = landed_ref[table, group * size : (group + 1) * size].reshape(size * each, half)
        slots = jnp.concatenate(
            [slots_ref[across(steps[p]), table : table + 1, :] for p in positions], axis=1
        )

        def body(index, carry):
            at = pl.ds(pl.multiple_of(index * tile, tile), tile)
            places_in = index * tile + lax.broadcasted_iota(jnp.int32, (tile, size * each), 0)
            chosen = (places_in == slots).astype(f32).astype(bf16)
            total_ref[at, :] += dot(chosen, rows)
            return carry

        lax.fori_loop(0, M * L // tile, body, 0)

    for index in range(len(weights)):
        shared(index).start()
    far, near = (0, 1), (2, 3)
    for table in range(count_tables):
        load(table).wait()
        for group in far:
            find(table, group)
    for table in range(count_tables):
        for group in near:
            find(table, group)
    for table in range(count_tables):
        for group in near:
            combine(table, group)
    for table in range(count_tables):
        for group in far:
            combine(table, group)

    theirs_ref[...] = total_ref[pl.ds(pl.multiple_of(partner * L, L), L), :].astype(bf16)
    mine = out_ref.at[:, pl.ds(pl.multiple_of(section * half, half), half)]
    last = remote(theirs_ref, mine, last_sems.at[0], last_sems.at[1], section=partner)
    last.start()
    mine_ref[...] = total_ref[pl.ds(pl.multiple_of(section * L, L), L), :].astype(bf16)
    own = pltpu.make_async_copy(mine_ref, mine, last_sems.at[2])
    own.start()
    for step in range(1, devices):
        ask(step).wait_send()
    for position in range(devices):
        for table in range(count_tables):
            if steps[position]:
                send(position, table).wait_send()
    for index in range(len(weights)):
        shared(index).wait()
    own.wait()
    last.wait()


def gather_rows(requests, tables, slots, ids, table, weights):
    devices, count_tables, each = requests.shape
    half = tables.shape[2]
    vmem = pl.BlockSpec(memory_space=pltpu.VMEM)
    any_space = pl.BlockSpec(memory_space=pl.ANY)
    dma = pltpu.SemaphoreType.DMA
    blocks = (count_tables, devices, each, half)
    return pl.pallas_call(
        functools.partial(gather_kernel, devices),
        in_specs=[vmem, any_space, vmem, vmem, vmem] + [any_space] * len(weights),
        out_specs=[vmem, vmem] + [any_space] * len(weights),
        out_shape=[
            jax.ShapeDtypeStruct((L, 2 * half), bf16),
            jax.ShapeDtypeStruct(requests.shape, jnp.int32),
            *[jax.ShapeDtypeStruct(weight.shape, weight.dtype) for weight in weights],
        ],
        scratch_shapes=[
            pltpu.VMEM(tables.shape, bf16),
            pltpu.VMEM(blocks, bf16),
            pltpu.VMEM(blocks, bf16),
            pltpu.VMEM((devices // 4 * each, half), f32),
            pltpu.VMEM((M * L, half), f32),
            pltpu.VMEM((L, half), bf16),
            pltpu.VMEM((L, half), bf16),
            dma((count_tables,)),
            dma((devices - 1,)),
            dma((devices - 1,)),
            dma((devices * count_tables,)),
            dma((devices * count_tables,)),
            dma((3,)),
            *[dma((len(weights),))] * 2,
        ],
        compiler_params=pltpu.CompilerParams(
            collective_id=1, has_side_effects=True, vmem_limit_bytes=56 * 1024 * 1024
        ),
        cost_estimate=pl.CostEstimate(flops=5 * 10**10, bytes_accessed=4 * 10**8, transcendentals=0),
        name="gather_rows",
    )(requests, tables, slots, ids, table, *weights)


def head_marks(heads, width):
    feature = lax.shift_right_logical(lax.broadcasted_iota(jnp.int32, (heads, width), 1), 6)
    return (feature == lax.broadcasted_iota(jnp.int32, (heads, width), 0)).astype(f32).astype(bf16)


def patch_marks(patch_row_ref, patch_col_ref):
    by_patch = (
        lax.broadcasted_iota(jnp.int32, (P_SIZE, L), 0) == patch_row_ref[...]
    ).astype(f32).astype(bf16)
    by_byte = (
        lax.broadcasted_iota(jnp.int32, (L, P_SIZE), 1) == patch_col_ref[...]
    ).astype(f32).astype(bf16)
    return by_patch, by_byte


def per_head(marks, products):
    high = products.astype(bf16)
    low = (products - high.astype(f32)).astype(bf16)
    return dot_nt(marks, high) + dot_nt(marks, low)


def neighbours(patches, heads):
    wide = jnp.broadcast_to(patches, (heads, L))
    back = [(d, pltpu.roll(wide, d, 1) == wide) for d in (1, 2, 4, 8)]
    ahead = [(L - d, pltpu.roll(wide, L - d, 1) == wide) for d in (1, 2, 4, 8)]
    return back, ahead


def scan_max(values, steps):
    for distance, same in steps:
        values = jnp.where(same, jnp.maximum(values, pltpu.roll(values, distance, 1)), values)
    return values


def scan_sum(values, steps):
    for distance, same in steps:
        values = jnp.where(same, values + pltpu.roll(values, distance, 1), values)
    return values


def patch_attention_kernel(
    patch_row_ref, patch_col_ref, query_ref, key_ref, value_ref, attention_ref, attended_ref
):
    heads, width = attention_ref.shape[0], query_ref.shape[1]
    marks = head_marks(heads, width)
    by_patch, by_byte = patch_marks(patch_row_ref, patch_col_ref)
    queries = dot(by_byte, query_ref[...])
    scores = per_head(marks, queries * key_ref[...].astype(f32)) * 0.125
    back, ahead = neighbours(patch_row_ref[...], heads)
    top = scan_max(scan_max(scores, back), ahead)
    shifted = jnp.exp(scores - top)
    total = scan_sum(shifted, back) + scan_sum(shifted, ahead) - shifted
    attention = shifted / total
    attention_ref[...] = attention
    weights = dot_tn(attention.astype(bf16), marks)
    weighted = (weights * value_ref[...].astype(f32)).astype(bf16)
    attended_ref[...] = dot(by_patch, weighted).astype(bf16)


def patch_attention(patch_row, patch_col, queries, key_value):
    groups = D // GROUP
    return pl.pallas_call(
        patch_attention_kernel,
        grid=(groups,),
        in_specs=[
            pl.BlockSpec((1, L), lambda i: (0, 0)),
            pl.BlockSpec((L, 1), lambda i: (0, 0)),
            pl.BlockSpec((P_SIZE, GROUP), lambda i: (0, i)),
            pl.BlockSpec((L, GROUP), lambda i: (0, i)),
            pl.BlockSpec((L, GROUP), lambda i: (0, i + groups)),
        ],
        out_specs=[
            pl.BlockSpec((HEADS // groups, L), lambda i: (i, 0)),
            pl.BlockSpec((P_SIZE, GROUP), lambda i: (0, i)),
        ],
        out_shape=[
            jax.ShapeDtypeStruct((HEADS, L), f32),
            jax.ShapeDtypeStruct((P_SIZE, D), bf16),
        ],
        compiler_params=params("arbitrary"),
        cost_estimate=pl.CostEstimate(flops=4 * 10**9, bytes_accessed=6 * 10**6, transcendentals=16384),
        name="patch_attention",
    )(patch_row, patch_col, queries, key_value, key_value)


def patch_attention_back_kernel(
    patch_row_ref,
    patch_col_ref,
    query_ref,
    key_ref,
    value_ref,
    attention_ref,
    grad_ref,
    grad_query_ref,
    grad_pair_ref,
):
    heads, width = attention_ref.shape[0], query_ref.shape[1]
    first = pl.multiple_of(pl.program_id(0) * width, width)
    marks = head_marks(heads, width)
    by_patch, by_byte = patch_marks(patch_row_ref, patch_col_ref)
    grads = dot(by_byte, grad_ref[...])
    attention = attention_ref[...]
    grad_attention = per_head(marks, grads * value_ref[...].astype(f32))
    weights = dot_tn(attention.astype(bf16), marks)
    grad_pair_ref[:, pl.ds(D + first, width)] = (weights * grads).astype(bf16)
    back, ahead = neighbours(patch_row_ref[...], heads)
    terms = attention * grad_attention
    total = scan_sum(terms, back) + scan_sum(terms, ahead) - terms
    grad_scores = (attention * (grad_attention - total)).astype(bf16)
    spread_scores = dot_tn(grad_scores, marks) * 0.125
    grad_pair_ref[:, pl.ds(first, width)] = (spread_scores * dot(by_byte, query_ref[...])).astype(bf16)
    weighted = (spread_scores * key_ref[...].astype(f32)).astype(bf16)
    grad_query_ref[...] = dot(by_patch, weighted).astype(bf16)


def patch_attention_back(patch_row, patch_col, queries, key_value, attention, grad_attended):
    groups = D // GROUP
    byte_block = pl.BlockSpec((L, GROUP), lambda i: (0, i))
    patch_block = pl.BlockSpec((P_SIZE, GROUP), lambda i: (0, i))
    return pl.pallas_call(
        patch_attention_back_kernel,
        grid=(groups,),
        in_specs=[
            pl.BlockSpec((1, L), lambda i: (0, 0)),
            pl.BlockSpec((L, 1), lambda i: (0, 0)),
            patch_block,
            byte_block,
            pl.BlockSpec((L, GROUP), lambda i: (0, i + groups)),
            pl.BlockSpec((HEADS // groups, L), lambda i: (i, 0)),
            patch_block,
        ],
        out_specs=[patch_block, pl.BlockSpec((L, 2 * D), lambda i: (0, 0))],
        out_shape=[
            jax.ShapeDtypeStruct((P_SIZE, D), bf16),
            jax.ShapeDtypeStruct((L, 2 * D), bf16),
        ],
        compiler_params=params("arbitrary"),
        cost_estimate=pl.CostEstimate(flops=6 * 10**9, bytes_accessed=10 * 10**6, transcendentals=0),
        name="patch_attention_back",
    )(patch_row, patch_col, queries, key_value, key_value, attention, grad_attended)


def causal_softmax(queries, keys):
    scores = dot_nt(queries, keys) * 0.125
    size = scores.shape[0]
    allowed = lax.broadcasted_iota(jnp.int32, (size, size), 0) >= lax.broadcasted_iota(
        jnp.int32, (size, size), 1
    )
    scores = jnp.where(allowed, scores, -jnp.inf)
    shifted = jnp.exp(scores - jnp.max(scores, axis=-1, keepdims=True))
    return shifted / jnp.sum(shifted, axis=-1, keepdims=True)


def pair_masks(shape):
    lane = lax.broadcasted_iota(jnp.int32, shape, 1)
    return [lane < HEAD, lane >= HEAD]


def causal_kernel(query_ref, key_ref, value_ref, out_ref):
    queries, keys, values = query_ref[...], key_ref[...], value_ref[...]
    masks = pair_masks(queries.shape)
    parts = []
    for mask in masks:
        attention = causal_softmax(jnp.where(mask, queries, 0), keys).astype(bf16)
        parts.append(dot(attention, values))
    out_ref[...] = jnp.where(masks[0], parts[0], parts[1]).astype(bf16)


def causal_attention(mixed):
    pairs = HEADS // 2
    return pl.pallas_call(
        causal_kernel,
        grid=(pairs,),
        in_specs=[
            pl.BlockSpec((P_SIZE, 2 * HEAD), lambda i: (0, i)),
            pl.BlockSpec((P_SIZE, 2 * HEAD), lambda i: (0, i + pairs)),
            pl.BlockSpec((P_SIZE, 2 * HEAD), lambda i: (0, i + 2 * pairs)),
        ],
        out_specs=pl.BlockSpec((P_SIZE, 2 * HEAD), lambda i: (0, i)),
        out_shape=jax.ShapeDtypeStruct((P_SIZE, D), bf16),
        compiler_params=params("arbitrary"),
        cost_estimate=pl.CostEstimate(flops=2 * 10**9, bytes_accessed=2 * 10**6, transcendentals=10**6),
        name="causal_attention",
    )(mixed, mixed, mixed)


def causal_back_kernel(query_ref, key_ref, value_ref, grad_ref, out_ref):
    pair = pl.program_id(0) * 2 * HEAD
    queries, keys, values, grads = query_ref[...], key_ref[...], value_ref[...], grad_ref[...]
    masks = pair_masks(queries.shape)
    results = []
    for mask in masks:
        attention = causal_softmax(jnp.where(mask, queries, 0), keys)
        grad_attention = dot_nt(jnp.where(mask, grads, 0), values)
        total = jnp.sum(attention * grad_attention, axis=-1, keepdims=True)
        grad_scores = (attention * (grad_attention - total)).astype(bf16)
        results.append(
            (
                dot(grad_scores, keys) * 0.125,
                dot_tn(grad_scores, queries) * 0.125,
                dot_tn(attention.astype(bf16), grads),
            )
        )
    for index, (first, second) in enumerate(zip(results[0], results[1])):
        columns = pl.ds(pl.multiple_of(index * D + pair, 2 * HEAD), 2 * HEAD)
        out_ref[:, columns] = jnp.where(masks[0], first, second).astype(bf16)


def causal_attention_back(mixed, grad_attended):
    pairs = HEADS // 2
    block = pl.BlockSpec((P_SIZE, 2 * HEAD), lambda i: (0, i))
    return pl.pallas_call(
        causal_back_kernel,
        grid=(pairs,),
        in_specs=[
            block,
            pl.BlockSpec((P_SIZE, 2 * HEAD), lambda i: (0, i + pairs)),
            pl.BlockSpec((P_SIZE, 2 * HEAD), lambda i: (0, i + 2 * pairs)),
            block,
        ],
        out_specs=pl.BlockSpec((P_SIZE, 3 * D), lambda i: (0, 0)),
        out_shape=jax.ShapeDtypeStruct((P_SIZE, 3 * D), bf16),
        compiler_params=params("arbitrary"),
        cost_estimate=pl.CostEstimate(flops=4 * 10**9, bytes_accessed=4 * 10**6, transcendentals=10**6),
        name="causal_attention_back",
    )(mixed, mixed, mixed, grad_attended)


def normalize(inputs, gain):
    inverse = lax.rsqrt(jnp.mean(inputs * inputs, axis=-1, keepdims=True) + epsilon)
    return (inputs * inverse * gain).astype(bf16), inverse


def normalize_back(inputs, gain, inverse, grad_normed):
    scaled = inputs * inverse
    grad_gain = jnp.sum(grad_normed * scaled, axis=0)
    grad_scaled = grad_normed * gain
    grad_inputs = inverse * (
        grad_scaled - scaled * jnp.mean(grad_scaled * scaled, axis=-1, keepdims=True)
    )
    return grad_inputs, grad_gain


def feed_kernel(
    hidden_ref, gain_ref, w_gate_ref, w_up_ref, w_down_ref, out_ref, normed_ref, gate_ref, up_ref, inner_ref
):
    @pl.when(pl.program_id(0) == 0)
    def _():
        hidden = hidden_ref[...]
        normed_ref[...] = normalize(hidden, gain_ref[...])[0]
        out_ref[...] = hidden

    gate, up = dot(normed_ref[...], w_gate_ref[...]), dot(normed_ref[...], w_up_ref[...])
    inner = (gate * jax.nn.sigmoid(gate) * up).astype(bf16)
    gate_ref[...] = gate.astype(bf16)
    up_ref[...] = up.astype(bf16)
    inner_ref[...] = inner
    out_ref[...] += dot(inner, w_down_ref[...])


def feed_specs():
    tile = FF // 2
    tiles = FF // tile
    whole = pl.BlockSpec((P_SIZE, D), lambda j: (0, 0))
    row = pl.BlockSpec((1, D), lambda j: (0, 0))
    gate = pl.BlockSpec((D, tile), lambda j: (0, j))
    up = pl.BlockSpec((D, tile), lambda j: (0, j + tiles))
    down = pl.BlockSpec((tile, D), lambda j: (j, 0))
    part = pl.BlockSpec((P_SIZE, tile), lambda j: (0, j))
    return tiles, whole, row, gate, up, down, part


def feed_forward(hidden, gain, w_gate_up, w_down):
    tiles, whole, row, gate, up, down, part = feed_specs()
    narrow = jax.ShapeDtypeStruct((P_SIZE, FF), bf16)
    out, normed, gates, ups, inner = pl.pallas_call(
        feed_kernel,
        grid=(tiles,),
        in_specs=[whole, row, gate, up, down],
        out_specs=[whole, whole, part, part, part],
        out_shape=[
            jax.ShapeDtypeStruct((P_SIZE, D), f32),
            jax.ShapeDtypeStruct((P_SIZE, D), bf16),
            narrow,
            narrow,
            narrow,
        ],
        compiler_params=params("arbitrary"),
        cost_estimate=pl.CostEstimate(flops=6 * P_SIZE * D * FF, bytes_accessed=24 * 10**6, transcendentals=P_SIZE * FF),
        name="feed_forward",
    )(hidden, gain[None, :], w_gate_up, w_gate_up, w_down)
    return out, (normed, gates, ups, inner)


def feed_back_kernel(
    grad_ref,
    hidden_ref,
    gain_ref,
    gate_ref,
    up_ref,
    w_gate_ref,
    w_up_ref,
    w_down_ref,
    out_ref,
    low_ref,
    branch_ref,
    joined_ref,
    grad_gain_ref,
    total_ref,
):
    step = pl.program_id(0)
    tile = gate_ref.shape[1]

    @pl.when(step == 0)
    def _():
        branch_ref[...] = grad_ref[...].astype(bf16)
        total_ref[...] = jnp.zeros_like(total_ref)

    grad_inner = dot_nt(branch_ref[...], w_down_ref[...])
    gate, up = gate_ref[...].astype(f32), up_ref[...].astype(f32)
    sigmoid = jax.nn.sigmoid(gate)
    grad_gate = (grad_inner * up * sigmoid * (1.0 + gate * (1.0 - sigmoid))).astype(bf16)
    grad_up = (grad_inner * gate * sigmoid).astype(bf16)
    joined_ref[:, pl.ds(pl.multiple_of(step * tile, 128), tile)] = grad_gate
    joined_ref[:, pl.ds(pl.multiple_of(FF + step * tile, 128), tile)] = grad_up
    total_ref[...] += dot_nt(grad_gate, w_gate_ref[...]) + dot_nt(grad_up, w_up_ref[...])

    @pl.when(step == pl.num_programs(0) - 1)
    def _():
        hidden = hidden_ref[...]
        inverse = lax.rsqrt(jnp.mean(hidden * hidden, axis=-1, keepdims=True) + epsilon)
        grad_in, grad_gain = normalize_back(hidden, gain_ref[...], inverse, total_ref[...])
        result = grad_ref[...] + grad_in
        out_ref[...] = result
        low_ref[...] = result.astype(bf16)
        grad_gain_ref[...] = grad_gain[None, :]


def feed_back(hidden, gain, w_gate_up, w_down, kept, grad_out):
    normed, gates, ups, inner = kept
    tiles, whole, row, gate, up, down, part = feed_specs()
    out, low, branch, joined, grad_gain = pl.pallas_call(
        feed_back_kernel,
        grid=(tiles,),
        in_specs=[whole, whole, row, part, part, gate, up, down],
        out_specs=[whole, whole, whole, pl.BlockSpec((P_SIZE, 2 * FF), lambda j: (0, 0)), row],
        out_shape=[
            jax.ShapeDtypeStruct((P_SIZE, D), f32),
            jax.ShapeDtypeStruct((P_SIZE, D), bf16),
            jax.ShapeDtypeStruct((P_SIZE, D), bf16),
            jax.ShapeDtypeStruct((P_SIZE, 2 * FF), bf16),
            jax.ShapeDtypeStruct((1, D), f32),
        ],
        scratch_shapes=[pltpu.VMEM((P_SIZE, D), f32)],
        compiler_params=params("arbitrary"),
        cost_estimate=pl.CostEstimate(flops=6 * P_SIZE * D * FF, bytes_accessed=24 * 10**6, transcendentals=P_SIZE * FF),
        name="feed_back",
    )(grad_out, hidden, gain[None, :], gates, ups, w_gate_up, w_gate_up, w_down)
    return out, low, grad_gain[0], joined, branch


def byte_grad_kernel(patch_col_ref, grad_ref, keys_ref, values_ref, w_key_ref, w_value_ref, out_ref):
    tile = out_ref.shape[0]
    owner = lax.broadcasted_iota(jnp.int32, (tile, P_SIZE), 1)
    member = (owner == patch_col_ref[...]).astype(f32).astype(bf16)
    total = dot(member, grad_ref[...]) + dot_nt(keys_ref[...], w_key_ref[...])
    out_ref[...] = (total + dot_nt(values_ref[...], w_value_ref[...])).astype(bf16)


def byte_grads(patch_col, grad_patches, grad_pairs, w_qkv):
    tile = 256
    part = lambda column: pl.BlockSpec((tile, D), lambda i: (i, column))
    weight = lambda column: pl.BlockSpec((D, D), lambda i: (0, column))
    return pl.pallas_call(
        byte_grad_kernel,
        grid=(L // tile,),
        in_specs=[
            pl.BlockSpec((tile, 1), lambda i: (i, 0)),
            pl.BlockSpec((P_SIZE, D), lambda i: (0, 0)),
            part(0),
            part(1),
            weight(1),
            weight(2),
        ],
        out_specs=pl.BlockSpec((tile, D), lambda i: (i, 0)),
        out_shape=jax.ShapeDtypeStruct((L, D), bf16),
        compiler_params=params("arbitrary"),
        cost_estimate=pl.CostEstimate(flops=5 * L * D * D, bytes_accessed=11 * 10**6, transcendentals=0),
        name="byte_grads",
    )(patch_col, grad_patches, grad_pairs, grad_pairs, w_qkv, w_qkv)


def chip_bits(devices):
    bits = devices.bit_length() - 1
    first = tuple(reversed(range(bits)))
    return bits, {"A": first, "B": (first[1], first[0]) + first[2:], "C": first[2:4] + first[:2] + first[4:]}


def at_place(ref, axis, place):
    return ref.at[(slice(None),) * axis + (place,)]


def plan_pieces():
    ff, half = FF // 2, D // 2
    pieces = []
    for layer in (1, 0):
        pieces += [
            (layer, "A", [("gate_up", 0, ff)]),
            (layer, "A", [("gate_up", ff, ff)]),
            (layer, "B", [("down", 0, ff)]),
            (layer, "B", [("query", 0, half), ("key", 0, half)]),
            (layer, "C", [("value", 0, half), ("out", 0, half)]),
        ]
    return pieces


def backward_kernel(devices, table_rows, count_tables, *refs):
    bits, orders = chip_bits(devices)
    half, ff = D // 2, FF // 2
    rows = D // devices
    table_block = table_block_rows(devices, table_rows)
    plan = plan_pieces()
    extra = len(plan)
    pieces = extra + 1
    names = [piece[1] for piece in plan] + ["C"]
    widths = [sum(width for _, _, width in piece[2]) for piece in plan] + [half]

    layers, refs = {1: refs[:8], 0: refs[8:16]}, refs[16:]
    bytes_ref, pairs_ref, grad_ref, slots_ref, places_ref, ids_ref, gains_ref = refs[:7]
    sums_ref, theirs_ref, gathered_ref, sorted_ref, arrived_ref, staged_ref = refs[7:13]
    refs = refs[13:]
    landed, refs = {1: refs[:8], 0: refs[8:16]}, refs[16:]
    bytes_landed, pairs_landed, refs = refs[0], refs[1], refs[2:]
    owns, refs = refs[:pieces], refs[pieces:]
    lands, refs = [refs[bits * i : bits * i + bits] for i in range(pieces)], refs[bits * pieces :]
    left_ref, right_ref, total_ref, send_ref, extra_ref, own_ref, table_ref, tile_ref, block_ref = refs[:9]
    swap_send, swap_land, load_sems, grad_sems, table_sem, tile_sems, block_sems, refs = *refs[9:16], refs[16:]
    send_sems, land_sems, trade_send, trade_land, spread_send, spread_land, last_sems = refs

    me = lax.axis_index("rows")
    section = lax.axis_index("section")
    partner = 1 - section
    places = [(me // 2 ** (bits - 1 - d)) % 2 for d in range(bits)]
    peers = [me + (1 - 2 * places[d]) * 2 ** (bits - 1 - d) for d in range(bits)]

    def other(step):
        return lax.rem(me + step, devices)

    barrier = pltpu.get_barrier_semaphore()
    mesh_id = pl.DeviceIdType.MESH
    pl.semaphore_signal(barrier, inc=1, device_id={"section": partner}, device_id_type=mesh_id)
    for step in range(1, devices):
        pl.semaphore_signal(barrier, inc=1, device_id={"rows": other(step)}, device_id_type=mesh_id)
    pl.semaphore_wait(barrier, devices)

    def remote(source, target, send, land, **device):
        return pltpu.make_async_remote_copy(
            src_ref=source, dst_ref=target, send_sem=send, recv_sem=land, device_id=device, device_id_type=mesh_id
        )

    def part_of(array, index, core):
        size = array.shape[1]
        if size == 3 * D:
            first = index * D + core * half
        elif size == 2 * D:
            first = index * D + core * half
        else:
            first = core * (size // 2)
            return array.at[:, pl.ds(pl.multiple_of(first, 128), size // 2)]
        return array.at[:, pl.ds(pl.multiple_of(first, 128), half)]

    swaps = {}

    def swap_of(key, source, target):
        slot = len(swaps)
        swaps[key] = remote(source, target, swap_send.at[slot], swap_land.at[slot], section=partner)
        swaps[key].start()

    def swap_layer(layer, which):
        for index in which:
            array, target = layers[layer][index], landed[layer][index]
            if index < 4:
                swap_of((layer, index, 0), array, target)
            else:
                wide = array.shape[1] // D if index == 4 else 1
                for part in range(wide):
                    there = target.at[:, pl.ds(part * half, half)] if index == 4 else target
                    swap_of((layer, index, part), part_of(array, part, partner), there)

    ready = set()

    def settled(key):
        if key not in ready:
            ready.add(key)
            swaps[key].wait_recv()

    swap_layer(1, (2, 6, 3, 7))
    own_rows = own_ref.at[pl.ds(pl.multiple_of(section * L, L), L)]
    swap_of(("grads",), grad_ref.at[:, pl.ds(pl.multiple_of(partner * half, half), half)], own_rows)
    own_copy = pltpu.make_async_copy(
        grad_ref.at[:, pl.ds(pl.multiple_of(section * half, half), half)], own_rows, grad_sems
    )
    own_copy.start()
    swap_layer(1, (0, 1, 4, 5))
    swap_layer(0, (2, 6, 3, 7, 0, 1, 4, 5))
    swap_of(("bytes",), bytes_ref, bytes_landed)
    for part in range(2):
        swap_of(
            ("pairs", part), part_of(pairs_ref, part, partner), pairs_landed.at[:, pl.ds(part * half, half)]
        )

    def jobs_of(piece):
        layer, _, segments = plan[piece]
        own, land = layers[layer], landed[layer]
        result, column = [], 0
        for kind, first, width in segments:
            if layer == 0 and kind in ("key", "value"):
                part = 0 if kind == "key" else 1
                for chunk in range(4):
                    depth = pl.ds(chunk % 2 * 512, 512)
                    if chunk < 2:
                        left, right = bytes_ref, part_of(pairs_ref, part, section)
                        keys = []
                    else:
                        left, right = bytes_landed, pairs_landed.at[:, pl.ds(part * half, half)]
                        keys = [("bytes",), ("pairs", part)]
                    copies = [("left", left.at[depth], 0, 512), ("right", right.at[depth], 0, 512)]
                    result.append((piece, column, width, chunk, 4, keys, copies))
            else:
                index, other_index, part = {
                    "gate_up": (2, 6, 0),
                    "down": (3, 7, 0),
                    "query": (0, 4, 0),
                    "key": (0, 4, 1),
                    "value": (0, 4, 2),
                    "out": (1, 5, 0),
                }[kind]
                if other_index == 4:
                    right = part_of(own[4], part, section)
                    right_landed = land[4].at[:, pl.ds(part * half, half)]
                elif kind == "gate_up":
                    start = pl.multiple_of(section * FF + first, 128)
                    right = own[6].at[:, pl.ds(start, width)]
                    right_landed = land[6].at[:, pl.ds(first, width)]
                else:
                    right, right_landed = part_of(own[other_index], 0, section), land[other_index]
                copies = [
                    ("left", own[index], 0, P_SIZE),
                    ("left", land[index], P_SIZE, P_SIZE),
                    ("right", right, 0, P_SIZE),
                    ("right", right_landed, P_SIZE, P_SIZE),
                ]
                keys = [(layer, index, 0), (layer, other_index, part)]
                result.append((piece, column, width, 0, 1, keys, copies))
            column += width
        return result

    groups = [[i for i in range(pieces) if names[i] == name] for name in "ABC"]
    order_made = []
    for rank in range(max(len(group) for group in groups)):
        order_made += [group[rank] for group in groups if rank < len(group)]
    jobs = [job for piece in order_made if piece != extra for job in jobs_of(piece)]

    def loads(number):
        piece, column, width, chunk, chunks, keys, copies = jobs[number]
        slot = number % 2
        result = []
        for index, (side, source, first, count) in enumerate(copies):
            buffer = left_ref if side == "left" else right_ref
            columns = D if side == "left" else width
            target = buffer.at[slot, pl.ds(first, count), pl.ds(0, columns)]
            result.append(pltpu.make_async_copy(source, target, load_sems.at[slot, index]))
        return result

    def start_loads(number):
        if number < len(jobs):
            for key in jobs[number][5]:
                settled(key)
            for copy in loads(number):
                copy.start()

    slots_of = {piece: index % send_ref.shape[0] for index, piece in enumerate(order_made) if piece != extra}

    def sent_part(piece):
        if piece == extra:
            return extra_ref
        return send_ref.at[slots_of[piece]].at[(slice(None),) * bits + (pl.ds(0, widths[piece]),)]

    def store(piece, device, value, column, width):
        axis = orders[names[piece]][0]
        at = [(device // 2 ** (bits - 1 - d)) % 2 for d in range(bits)]
        bit = at.pop(axis)
        at = tuple(at) + (slice(None), pl.ds(column, width))
        target = sent_part(piece)

        @pl.when(bit == places[axis])
        def _():
            owns[piece][at] = value

        @pl.when(bit != places[axis])
        def _():
            target[at] = value

    def run_job(number):
        piece, column, width, chunk, chunks, keys, copies = jobs[number]
        slot = number % 2
        for copy in loads(number):
            copy.wait()
        start_loads(number + 1)
        tile = 128

        def body(index, carry):
            at = pl.ds(pl.multiple_of(index * tile, tile), tile)
            value = dot_tn(left_ref[slot, :, at], right_ref[slot, :, pl.ds(0, width)])
            if chunk > 0:
                value = value + total_ref[at, :]
            if chunk < chunks - 1:
                total_ref[at, :] = value
            else:
                for part in range(tile // rows):
                    block = value[part * rows : (part + 1) * rows].astype(bf16)
                    store(piece, index * (tile // rows) + part, block, column, width)
            return carry

        lax.fori_loop(0, D // tile, body, 0)

    def left_of(piece, phase):
        order = orders[names[piece]]
        return [d for d in range(bits) if d not in order[:phase]]

    def kept(piece, phase):
        order = orders[names[piece]]
        ref = owns[piece]
        for step in range(1, phase):
            ref = at_place(ref, left_of(piece, step).index(order[step]), places[order[step]])
        return ref

    def send(piece, phase):
        axis = orders[names[piece]][phase]
        if phase == 0:
            source = sent_part(piece)
        else:
            source = at_place(kept(piece, phase), left_of(piece, phase).index(axis), 1 - places[axis])
        slot = piece * bits + phase
        return remote(source, lands[piece][phase], send_sems.at[slot], land_sems.at[slot], rows=peers[axis])

    made = [0, 0]
    sent = set()

    def make(piece):
        if piece == extra:
            make_extra()
        else:
            index = order_made.index(piece)
            count = send_ref.shape[0]
            earlier = [p for p in order_made[:index] if p != extra and slots_of[p] == slots_of[piece]]
            if earlier and (earlier[-1], 0) not in sent:
                sent.add((earlier[-1], 0))
                send(earlier[-1], 0).wait_send()
            while made[0] < len(jobs) and jobs[made[0]][0] == piece:
                run_job(made[0])
                made[0] += 1
        send(piece, 0).start()

    def make_extra():
        tile = table_block
        first_gain = table_rows // 16 * 16
        positions = M * L

        def body(index, carry):
            words = index * tile + lax.broadcasted_iota(jnp.int32, (tile, positions), 0)
            chosen = (words == ids_ref[...]).astype(f32).astype(bf16)
            value = dot(chosen, own_ref[...])
            row = index * tile + lax.broadcasted_iota(jnp.int32, (tile, half), 0)
            gains = jnp.concatenate([gains_ref[...]] * (tile // 16), axis=0)
            inside = (row >= first_gain) & (row < first_gain + 16)
            value = value + jnp.where(inside, gains, 0.0)
            store(extra, index, value.astype(bf16), 0, half)
            return carry

        lax.fori_loop(0, devices, body, 0)

    def add(piece, phase):
        target = kept(piece, phase + 1)
        land = lands[piece][phase]
        leads = len(target.shape) - 2
        count = 16
        groups_in = target.shape[-2] // count

        def body(index, carry):
            at = (pl.ds(pl.multiple_of(index % groups_in * count, count), count), slice(None))
            lead = index // groups_in
            at = tuple((lead // 2 ** (leads - 1 - d)) % 2 for d in range(leads)) + at
            target[at] = (target[at].astype(f32) + land[at].astype(f32)).astype(bf16)
            return carry

        lax.fori_loop(0, 2**leads * groups_in, body, 0)

    block_rows = block_ref.shape[1]
    block_slots = block_ref.shape[0]
    block_steps = [*(FAR_FIRST if devices == 16 else range(1, devices)), 0]

    def block_copy(step):
        target = staged_ref.at[step] if step else arrived_ref.at[me]
        slot = block_steps.index(step) % block_slots
        return pltpu.make_async_copy(block_ref.at[slot], target, block_sems.at[slot])

    def trade(step):
        return remote(
            staged_ref.at[step], arrived_ref.at[me], trade_send.at[step - 1], trade_land.at[step - 1], rows=other(step)
        )

    def trade_landing(step):
        back = lax.rem(me + devices - step, devices)
        return remote(
            staged_ref.at[step], arrived_ref.at[back], trade_send.at[step - 1], trade_land.at[step - 1], rows=back
        )

    own_block = block_copy(0)

    def make_blocks():
        own_copy.wait()
        settled(("grads",))
        steps = block_steps
        behind = block_slots - 1

        def pass_on(step):
            if step:
                block_copy(step).wait()
                trade(step).start()

        for index, step in enumerate(steps):
            if index >= behind:
                pass_on(steps[index - behind])
            each = block_rows // count_tables
            where = lax.broadcasted_iota(jnp.int32, (each, M * L), 1)
            for table in range(count_tables):
                slot = as_column(slots_ref[other(step), table : table + 1, :])
                chosen = (where == slot).astype(f32).astype(bf16)
                part = pl.ds(table * each, each)
                block_ref[index % block_slots, part] = dot(chosen, own_ref[...]).astype(bf16)
            block_copy(step).start()
        for step in steps[devices - behind :]:
            pass_on(step)


    def tile_copy(table, index):
        tile = tile_ref.shape[1]
        return pltpu.make_async_copy(
            tile_ref.at[index % 2],
            sorted_ref.at[table, pl.ds(pl.multiple_of(index * tile, tile), tile)],
            tile_sems.at[index % 2],
        )

    def sort_rows(table):
        if table == 0:
            own_block.wait()
            for step in range(1, devices):
                trade_landing(step).wait_recv()
        each = block_rows // count_tables
        copy = pltpu.make_async_copy(arrived_ref.at[:, pl.ds(table * each, each)], table_ref, table_sem)
        copy.start()
        copy.wait()
        tile = tile_ref.shape[1]
        for index in range(M * L // tile):
            if index >= 2:
                tile_copy(table, index - 2).wait()
            place = lax.broadcasted_iota(jnp.int32, (tile, M * L), 1)
            wanted = as_column(places_ref[table, :, index * tile : (index + 1) * tile])
            chosen = (place == wanted).astype(f32).astype(bf16)
            rows_in = table_ref[...].reshape(M * L, half)
            tile_ref[index % 2] = dot(chosen, rows_in).astype(bf16)
            tile_copy(table, index).start()
        for index in range(M * L // tile - 2, M * L // tile):
            tile_copy(table, index).wait()

    def spreads():
        return [
            remote(
                gathered_ref.at[me],
                gathered_ref.at[me],
                spread_send.at[step - 1],
                spread_land.at[step - 1],
                rows=other(step),
            )
            for step in range(1, devices)
        ]

    def spread_landing(step):
        back = lax.rem(me + devices - step, devices)
        return remote(
            gathered_ref.at[me], gathered_ref.at[back], spread_send.at[step - 1], spread_land.at[step - 1], rows=back
        )

    def finish(piece):
        if piece == extra:
            gathered_ref[me] = kept(piece, bits)[...]
            for copy in spreads():
                copy.start()
        else:
            layer = plan[piece][0]
            first = sum(widths[p] for p in range(piece) if plan[p][0] == layer)
            sums_ref[layer, :, first : first + widths[piece]] = kept(piece, bits)[...]

    start_loads(0)
    for group in groups:
        make(group[0])
    make_blocks()
    for group in groups:
        if len(group) > 1:
            make(group[1])
    rounds = max(len(group) for group in groups)
    for turn in range(rounds + bits - 1):
        for phase in range(bits):
            for group in groups:
                if not 0 <= turn - phase < len(group):
                    continue
                piece = group[turn - phase]
                send(piece, phase).wait_recv()
                if phase == 0 and turn + 2 < len(group):
                    make(group[turn + 2])
                add(piece, phase)
                if phase + 1 < bits:
                    send(piece, phase + 1).start()
                else:
                    finish(piece)
        if 0 <= turn - SORT_TURN < count_tables:
            sort_rows(turn - SORT_TURN)

    last = remote(sums_ref.at[partner], theirs_ref, last_sems.at[0], last_sems.at[1], section=partner)
    last.start()
    for piece in range(pieces):
        for phase in range(bits):
            if (piece, phase) not in sent:
                send(piece, phase).wait_send()
    for key, copy in swaps.items():
        copy.wait_send()
        settled(key)
    for step in range(1, devices):
        trade(step).wait_send()
    for copy in spreads():
        copy.wait_send()
    for step in range(1, devices):
        spread_landing(step).wait_recv()
    last.wait()


def place_kernel(starts_ref, ids_ref, rows_ref, out_ref):
    table, tile = pl.program_id(0), pl.program_id(1)
    height, window, align = out_ref.shape[1], 256, 128
    count = rows_ref.shape[1]
    at = table * (pl.num_programs(1) + 1) + tile
    first = starts_ref[at] // align * align
    places = tile * height + lax.broadcasted_iota(jnp.int32, (height, window), 0)
    lanes = lax.broadcasted_iota(jnp.int32, (height, window), 1)

    def placed(index):
        wanted = first + index * window
        begin = pl.multiple_of(jnp.minimum(wanted, count - window), align)
        part = pl.ds(begin, window)
        chosen = (places == ids_ref[0, :, part]) & (lanes >= wanted - begin)
        return dot(chosen.astype(f32).astype(bf16), rows_ref[0, part, :])

    def body(index, carry):
        out_ref[0] += placed(index)
        return carry

    out_ref[0] = placed(0)
    lax.fori_loop(1, (starts_ref[at + 1] - first + window - 1) // window, body, 0)


def place_rows(ids, rows, shard_rows):
    count_tables, count, width = rows.shape
    height = 1024
    tiles = shard_rows // height
    edges = jnp.arange(tiles + 1, dtype=jnp.int32) * height
    starts = jnp.sum((ids[:, None, :] < edges[None, :, None]).astype(jnp.int32), axis=2).reshape(-1)
    return pl.pallas_call(
        place_kernel,
        grid_spec=pltpu.PrefetchScalarGridSpec(
            num_scalar_prefetch=1,
            grid=(count_tables, tiles),
            in_specs=[
                pl.BlockSpec((1, 1, count), lambda i, j, starts: (i, 0, 0)),
                pl.BlockSpec((1, count, width), lambda i, j, starts: (i, 0, 0)),
            ],
            out_specs=pl.BlockSpec((1, height, width), lambda i, j, starts: (i, j, 0)),
        ),
        out_shape=jax.ShapeDtypeStruct((count_tables, shard_rows, width), f32),
        compiler_params=params("arbitrary", "arbitrary"),
        cost_estimate=pl.CostEstimate(flops=10**10, bytes_accessed=6 * 10**7, transcendentals=0),
        name="place_rows",
    )(starts, ids[:, None, :], rows)


def table_block_rows(devices, table_rows):
    return -(-(table_rows + 12) // (16 * devices)) * 16


def backward_sums(layer_two, layer_one, byte_rows, grad_pairs, grad_bytes, slots, places, ids, gains, table_rows):
    devices = lax.axis_size("rows")
    bits, orders = chip_bits(devices)
    rows = D // devices
    plan = plan_pieces()
    table_block = table_block_rows(devices, table_rows)
    half, ff = D // 2, FF // 2
    count_tables, each = slots.shape[1:]
    block_rows = count_tables * each
    widths = [sum(width for _, _, width in piece[2]) for piece in plan]
    shapes = [(rows, width) for width in widths] + [(table_block, half)]
    owns, lands = [], []
    for shape in shapes:
        owns.append(pltpu.VMEM((2,) * (bits - 1) + shape, bf16))
        lands += [pltpu.VMEM((2,) * (bits - 1 - phase) + shape, bf16) for phase in range(bits)]
    total = sum(widths) // 2
    landed = []
    for layer in (layer_two, layer_one):
        for index, array in enumerate(layer):
            shape = array.shape if index < 4 else (array.shape[0], array.shape[1] // 2)
            landed.append(jax.ShapeDtypeStruct(shape, bf16))
    landed += [
        jax.ShapeDtypeStruct(byte_rows.shape, bf16),
        jax.ShapeDtypeStruct((grad_pairs.shape[0], grad_pairs.shape[1] // 2), bf16),
    ]
    swaps = 2 * 7 + 3 + 1 + 4
    copies = len(shapes) * bits
    any_space = pl.BlockSpec(memory_space=pl.ANY)
    vmem = pl.BlockSpec(memory_space=pltpu.VMEM)
    blocks = jax.ShapeDtypeStruct((devices, block_rows, half), bf16)
    dma = pltpu.SemaphoreType.DMA
    results = pl.pallas_call(
        functools.partial(backward_kernel, devices, table_rows, count_tables),
        in_specs=[any_space] * 19 + [vmem] * 4,
        out_specs=[vmem, any_space, vmem] + [any_space] * (3 + len(landed)),
        out_shape=[
            jax.ShapeDtypeStruct((2, rows, total), bf16),
            jax.ShapeDtypeStruct((rows, total), bf16),
            jax.ShapeDtypeStruct((devices, table_block, half), bf16),
            jax.ShapeDtypeStruct((count_tables, M * L, half), bf16),
            blocks,
            blocks,
            *landed,
        ],
        scratch_shapes=[
            *owns,
            *lands,
            pltpu.VMEM((2, 2 * P_SIZE, D), bf16),
            pltpu.VMEM((2, 2 * P_SIZE, ff), bf16),
            pltpu.VMEM((D, half), f32),
            pltpu.VMEM((4,) + (2,) * (bits - 1) + (rows, ff), bf16),
            pltpu.VMEM((2,) * (bits - 1) + (table_block, half), bf16),
            pltpu.VMEM((M * L, half), bf16),
            pltpu.VMEM((devices, each, half), bf16),
            pltpu.VMEM((2, 256, half), bf16),
            pltpu.VMEM((3, block_rows, half), bf16),
            dma((swaps,)),
            dma((swaps,)),
            dma((2, 4)),
            dma,
            dma,
            dma((2,)),
            dma((3,)),
            dma((copies,)),
            dma((copies,)),
            dma((devices - 1,)),
            dma((devices - 1,)),
            dma((devices - 1,)),
            dma((devices - 1,)),
            dma((2,)),
        ],
        compiler_params=pltpu.CompilerParams(
            collective_id=0, has_side_effects=True, vmem_limit_bytes=60 * 1024 * 1024
        ),
        cost_estimate=pl.CostEstimate(flops=5 * 10**10, bytes_accessed=6 * 10**8, transcendentals=0),
        name="backward_sums",
    )(*layer_two, *layer_one, byte_rows, grad_pairs, grad_bytes, slots, places, ids, gains)
    return results[:4]


def swap(array):
    return lax.ppermute(array, "section", [(0, 1), (1, 0)])


def on_device(
    byte_ids,
    hash_ids,
    patch_lengths,
    row_lengths,
    byte_table,
    hash_tables,
    norm_gains,
    w_qkv,
    w_out,
    w_gate_up,
    w_down,
    cotangent,
):
    section = lax.axis_index("section")
    first_core = section == 0
    devices = lax.axis_size("rows")
    count_tables, shard_rows, half_width = hash_tables.shape
    positions = M * L

    def both(array):
        return lax.all_gather(array, "section", axis=0, tiled=True)

    flat_ids = hash_ids.reshape(positions, count_tables).T
    owners = flat_ids // shard_rows
    order_key = owners * positions + jnp.arange(positions, dtype=jnp.int32)[None, :]
    order_key, grouped = lax.sort((order_key, flat_ids % shard_rows), dimension=1, num_keys=1)

    def by_owner(array):
        return array.reshape(count_tables, devices, -1).transpose(1, 0, 2)

    byte_of_slot = order_key % positions
    numbers = jnp.arange(positions, dtype=jnp.int32)[None, :]
    flat_bytes = byte_ids.reshape(positions)
    table_rows = byte_table.shape[0]
    padded = jnp.pad(byte_table, ((0, -table_rows % 128), (0, 0)))
    slots = by_owner(byte_of_slot)
    weights = [w_qkv[0], w_out[0], w_gate_up[0], w_down[0]]
    byte_rows, requested, *other_weights = gather_rows(
        by_owner(grouped), hash_tables, slots, flat_bytes[:, None], padded, weights
    )
    gains = both(norm_gains).astype(f32)

    lengths = lax.dynamic_index_in_dim(patch_lengths, section, 0, keepdims=False)
    row_length = lax.dynamic_index_in_dim(row_lengths, section, 0, keepdims=False)
    starts = jnp.cumsum(lengths) - lengths
    byte_positions = jnp.arange(L, dtype=jnp.int32)
    byte_patch = jnp.sum((starts[:, None] <= byte_positions[None, :]).astype(jnp.int32), axis=0) - 1
    patch_row, patch_col = byte_patch[None, :], byte_patch[:, None]
    patches = jnp.arange(P_SIZE, dtype=jnp.int32)
    member = (patches[:, None] == patch_row).astype(bf16)
    counts = lengths.astype(f32)[:, None]
    valid = (patches < row_length)[:, None]

    own_cotangent = lax.dynamic_index_in_dim(cotangent[0], section, 0, keepdims=False)
    sent_cotangent = swap(lax.dynamic_index_in_dim(cotangent[0], 1 - section, 0, keepdims=False))
    cotangent_one = jnp.where(first_core, own_cotangent, sent_cotangent).astype(f32)
    cotangent_two = jnp.where(first_core, sent_cotangent, own_cotangent).astype(f32)

    def both_layers(one, two):
        pooled = dot(member, byte_rows) / counts
        normed_one, inverse_one = normalize(pooled, gains[0, 0])
        queries_one = dot(normed_one, one[0][:, :D]).astype(bf16)
        byte_pairs = dot(byte_rows, one[0][:, D:]).astype(bf16)
        attention_one, attended_one = patch_attention(patch_row, patch_col, queries_one, byte_pairs)
        middle_one = pooled + dot(attended_one, one[1])
        result_one, kept_one = feed_forward(middle_one, gains[0, 1], one[2], one[3])
        encoded = jnp.where(valid, result_one, pooled).astype(bf16)

        inputs_two = encoded.astype(f32)
        normed_two, inverse_two = normalize(inputs_two, gains[1, 0])
        mixed = dot(normed_two, two[0]).astype(bf16)
        attended_two = causal_attention(mixed)
        middle_two = inputs_two + dot(attended_two, two[1])
        result_two, kept_two = feed_forward(middle_two, gains[1, 1], two[2], two[3])
        final = jnp.where(valid, result_two, inputs_two).astype(bf16)
        grad_kept = jnp.where(valid, cotangent_two, 0.0)
        grad_middle, grad_low, gain_two_second, grad_joined, grad_branch = feed_back(
            middle_two, gains[1, 1], two[2], two[3], kept_two, grad_kept
        )
        factors_two = [normed_two, attended_two, kept_two[0], grad_branch, None, grad_low, grad_joined, kept_two[3]]
        grad_attended = dot_nt(grad_low, two[1]).astype(bf16)
        grad_mixed = causal_attention_back(mixed, grad_attended)
        grad_normed = dot_nt(grad_mixed, two[0])
        grad_in, gain_two_first = normalize_back(inputs_two, gains[1, 0], inverse_two, grad_normed)
        grad_encoded = jnp.where(valid, 0.0, cotangent_two) + grad_middle + grad_in


        grad_out = cotangent_one + grad_encoded.astype(bf16).astype(f32)
        grad_kept = jnp.where(valid, grad_out, 0.0)
        grad_middle, grad_low, gain_one_second, grad_joined, grad_branch = feed_back(
            middle_one, gains[0, 1], one[2], one[3], kept_one, grad_kept
        )
        factors_one = [normed_one, attended_one, kept_one[0], grad_branch, None, grad_low, grad_joined, kept_one[3]]
        grad_attended = dot_nt(grad_low, one[1]).astype(bf16)
        grad_queries, grad_pairs = patch_attention_back(
            patch_row, patch_col, queries_one, byte_pairs, attention_one, grad_attended
        )
        grad_normed = dot_nt(grad_queries, one[0][:, :D])
        grad_in, gain_one_first = normalize_back(pooled, gains[0, 0], inverse_one, grad_normed)
        grad_pooled = jnp.where(valid, 0.0, grad_out) + grad_middle + grad_in
        grad_bytes = byte_grads(patch_col, (grad_pooled / counts).astype(bf16), grad_pairs, one[0])

        table_ids = requested.transpose(1, 0, 2).reshape(count_tables, -1)
        id_key = lax.sort(table_ids * positions + numbers, dimension=1)
        sorted_ids = id_key // positions
        places = (id_key % positions)[:, None, :]

        factors_two[4], factors_one[4] = grad_mixed, grad_queries
        gain_part = jnp.stack([gain_one_first, gain_one_second, gain_two_first, gain_two_second])
        return encoded, final, factors_two, factors_one, grad_pairs, grad_bytes, gain_part, sorted_ids, places

    results = lax.cond(
        first_core, both_layers, lambda one, two: both_layers(two, one), weights, other_weights
    )
    encoded, final, factors_two, factors_one, grad_pairs, grad_bytes, gain_part, sorted_ids, places = results
    sent_out = swap(jnp.where(first_core, final, encoded))
    kept_out = jnp.where(first_core, encoded, final)
    section_out = jnp.where(
        first_core, jnp.stack([kept_out, sent_out]), jnp.stack([sent_out, kept_out])
    )[None]

    gain_part = jnp.pad(gain_part.reshape(8, half_width), ((8, 0), (0, 0)))
    sums, theirs, gathered, sorted_rows = backward_sums(
        factors_two,
        factors_one,
        byte_rows,
        grad_pairs,
        grad_bytes,
        slots,
        places,
        flat_bytes[None, :],
        gain_part,
        table_rows,
    )
    hash_grad = place_rows(sorted_ids, sorted_rows, shard_rows)
    gathered = gathered.reshape(-1, half_width)
    byte_table_grad = gathered[:table_rows].astype(f32)
    first_gain = table_rows // 16 * 16 + 8
    gain_sums = gathered[first_gain : first_gain + 8].reshape(2, 2, D)
    gain_sums = (gain_sums.astype(f32) + swap(gain_sums).astype(f32)).reshape(2, 2, devices, -1)
    gains_grad = lax.dynamic_index_in_dim(gain_sums, section, 0, keepdims=True)
    gains_grad = lax.dynamic_index_in_dim(gains_grad, lax.axis_index("rows"), 2, keepdims=False)

    mine = lax.dynamic_index_in_dim(sums, section, 0, keepdims=False)
    lower = jnp.where(first_core, mine, theirs).astype(f32)
    upper = jnp.where(first_core, theirs, mine).astype(f32)
    half, half_ff = D // 2, FF // 2
    gate_up_grad = jnp.concatenate([lower[:, :FF], upper[:, :FF]], axis=1)
    down_grad = jnp.concatenate([lower[:, FF : FF + half_ff], upper[:, FF : FF + half_ff]], axis=1).T
    low_rest, high_rest = lower[:, FF + half_ff :], upper[:, FF + half_ff :]
    columns = []
    for index in range(4):
        part = slice(index * half, (index + 1) * half)
        columns.append(jnp.concatenate([low_rest[:, part], high_rest[:, part]], axis=1))
    qkv_grad = jnp.concatenate(columns[:3], axis=1)
    out_grad = columns[3]

    return (
        section_out,
        byte_table_grad,
        hash_grad,
        gains_grad,
        qkv_grad[None],
        out_grad[None],
        gate_up_grad[None],
        down_grad[None],
    )


def solution(mesh):
    return jax.shard_map(
        on_device,
        mesh=mesh,
        in_specs=(
            P("rows", None),
            P("rows", None, None),
            P("rows", None),
            P("rows"),
            P(None, "section"),
            P(None, "rows", "section"),
            P("section", None, None),
            P("section", None, None),
            P("section", None, None),
            P("section", None, None),
            P("section", None, None),
            P("section", "rows", None, None),
        ),
        out_specs=(
            P("section", "rows", None, None),
            P(None, "section"),
            P(None, "rows", "section"),
            P("section", None, "rows"),
            P("section", "rows", None),
            P("section", "rows", None),
            P("section", "rows", None),
            P("section", None, "rows"),
        ),
        check_vma=False,
    )
```

```python
import functools

import jax
import jax.numpy as jnp
from jax import lax
from jax.experimental import pallas as pl
from jax.experimental.pallas import tpu as pltpu
from jax.sharding import PartitionSpec as P

D = 1024
HEADS = 16
HEAD = 64
FF = 2816
L = 1024
MOST = 16
M = 2
P_SIZE = 256
GROUP = 512
VMEM_BYTES = 48 * 1024 * 1024
FAR_FIRST = (4, 12, 8, 5, 11, 7, 9, 6, 10, 3, 13, 2, 14, 1, 15)
SORT_TURN = 3

epsilon = 1e-05
f32 = jnp.float32
bf16 = jnp.bfloat16


def dot(left, right):
    return jnp.dot(left, right, preferred_element_type=f32)


def dot_nt(left, right):
    return lax.dot_general(left, right, (((1,), (1,)), ((), ())), preferred_element_type=f32)


def dot_tn(left, right):
    return lax.dot_general(left, right, (((0,), (0,)), ((), ())), preferred_element_type=f32)


def params(*semantics):
    return pltpu.CompilerParams(vmem_limit_bytes=VMEM_BYTES, dimension_semantics=semantics)


def as_column(row):
    shape = (row.shape[1], row.shape[1])
    same = lax.broadcasted_iota(jnp.int32, shape, 0) == lax.broadcasted_iota(jnp.int32, shape, 1)
    return jnp.sum(jnp.where(same, jnp.broadcast_to(row, shape), 0), axis=1, keepdims=True)


def gather_kernel(devices, *refs):
    requests_ref, tables_ref, slots_ref, ids_ref, bytes_ref = refs[:5]
    weights, refs = refs[5:9], refs[9:]
    out_ref, requested_ref = refs[:2]
    layers, refs = refs[2:6], refs[6:]
    held_ref, staged_ref, landed_ref, part_ref, total_ref, mine_ref, theirs_ref = refs[:7]
    load_sems, ask_send, ask_land, send_sems, land_sems, last_sems = refs[7:13]
    weight_send, weight_land = refs[13:]
    count_tables, shard_rows, half = tables_ref.shape
    each = requests_ref.shape[2]
    bits = devices.bit_length() - 1

    me = lax.axis_index("rows")
    section = lax.axis_index("section")
    partner = 1 - section
    mesh_id = pl.DeviceIdType.MESH
    places = [(me // 2**d) % 2 for d in range(bits)]

    def across(step):
        device = me
        for d in range(bits):
            if step // 2**d % 2:
                device = device + (1 - 2 * places[d]) * 2**d
        return device

    steps = [0]
    for d in range(bits):
        steps = list(range(2**d, 2 ** (d + 1))) + steps

    def load(table):
        return pltpu.make_async_copy(tables_ref.at[table], held_ref.at[table], load_sems.at[table])

    for table in range(count_tables):
        load(table).start()

    barrier = pltpu.get_barrier_semaphore()
    pl.semaphore_signal(barrier, inc=1, device_id={"section": partner}, device_id_type=mesh_id)
    for step in range(1, devices):
        pl.semaphore_signal(barrier, inc=1, device_id={"rows": across(step)}, device_id_type=mesh_id)
    pl.semaphore_wait(barrier, devices)

    def remote(source, target, send, land, **device):
        return pltpu.make_async_remote_copy(
            src_ref=source, dst_ref=target, send_sem=send, recv_sem=land, device_id=device, device_id_type=mesh_id
        )

    def ask(step):
        return remote(
            requests_ref.at[across(step)],
            requested_ref.at[me],
            ask_send.at[step - 1],
            ask_land.at[step - 1],
            rows=across(step),
        )

    def asked(step):
        return remote(
            requests_ref.at[across(step)],
            requested_ref.at[across(step)],
            ask_send.at[step - 1],
            ask_land.at[step - 1],
            rows=across(step),
        )

    for step in range(1, devices):
        ask(step).start()
    requested_ref[me] = requests_ref[me]

    def shared(index):
        return remote(
            weights[index],
            layers[index],
            weight_send.at[index],
            weight_land.at[index],
            section=partner,
        )

    tile = 512
    def own_row(index, carry):
        at = pl.ds(pl.multiple_of(index * tile, tile), tile)
        words = lax.broadcasted_iota(jnp.int32, (tile, bytes_ref.shape[0]), 1)
        word = (words == ids_ref[at, :]).astype(f32).astype(bf16)
        total_ref[at, :] = dot(word, bytes_ref[...])
        return carry

    lax.fori_loop(0, M * L // tile, own_row, 0)
    for step in range(1, devices):
        asked(step).wait_recv()

    groups = 4
    size = devices // groups

    def send(position, table):
        step = steps[position]
        slot = position * count_tables + table
        return remote(
            staged_ref.at[table, position],
            landed_ref.at[table, position],
            send_sems.at[slot],
            land_sems.at[slot],
            rows=across(step),
        )

    def find(table, group):
        positions = range(group * size, (group + 1) * size)
        ids = jnp.concatenate(
            [as_column(requested_ref[across(steps[p]), table : table + 1, :]) for p in positions], axis=0
        )
        depth = 1024
        part_ref[...] = jnp.zeros_like(part_ref)

        def body(index, carry):
            first = pl.multiple_of(index * depth, depth)
            places_in = first + lax.broadcasted_iota(jnp.int32, (size * each, depth), 1)
            chosen = (places_in == ids).astype(f32).astype(bf16)
            part_ref[...] += dot(chosen, held_ref[table, pl.ds(first, depth), :])
            return carry

        lax.fori_loop(0, shard_rows // depth, body, 0)
        for index, position in enumerate(positions):
            block = part_ref[index * each : (index + 1) * each, :].astype(bf16)
            if steps[position]:
                staged_ref[table, position] = block
                send(position, table).start()
            else:
                landed_ref[table, position] = block

    def combine(table, group):
        positions = range(group * size, (group + 1) * size)
        for position in positions:
            if steps[position]:
                send(position, table).wait_recv()
        rows = landed_ref[table, group * size : (group + 1) * size].reshape(size * each, half)
        slots = jnp.concatenate(
            [slots_ref[across(steps[p]), table : table + 1, :] for p in positions], axis=1
        )

        def body(index, carry):
            at = pl.ds(pl.multiple_of(index * tile, tile), tile)
            places_in = index * tile + lax.broadcasted_iota(jnp.int32, (tile, size * each), 0)
            chosen = (places_in == slots).astype(f32).astype(bf16)
            total_ref[at, :] += dot(chosen, rows)
            return carry

        lax.fori_loop(0, M * L // tile, body, 0)

    for index in range(len(weights)):
        shared(index).start()
    far, near = (0, 1), (2, 3)
    for table in range(count_tables):
        load(table).wait()
        for group in far:
            find(table, group)
    for table in range(count_tables):
        for group in near:
            find(table, group)
    for table in range(count_tables):
        for group in near:
            combine(table, group)
    for table in range(count_tables):
        for group in far:
            combine(table, group)

    theirs_ref[...] = total_ref[pl.ds(pl.multiple_of(partner * L, L), L), :].astype(bf16)
    mine = out_ref.at[:, pl.ds(pl.multiple_of(section * half, half), half)]
    last = remote(theirs_ref, mine, last_sems.at[0], last_sems.at[1], section=partner)
    last.start()
    mine_ref[...] = total_ref[pl.ds(pl.multiple_of(section * L, L), L), :].astype(bf16)
    own = pltpu.make_async_copy(mine_ref, mine, last_sems.at[2])
    own.start()
    for step in range(1, devices):
        ask(step).wait_send()
    for position in range(devices):
        for table in range(count_tables):
            if steps[position]:
                send(position, table).wait_send()
    for index in range(len(weights)):
        shared(index).wait()
    own.wait()
    last.wait()


def gather_rows(requests, tables, slots, ids, table, weights):
    devices, count_tables, each = requests.shape
    half = tables.shape[2]
    vmem = pl.BlockSpec(memory_space=pltpu.VMEM)
    any_space = pl.BlockSpec(memory_space=pl.ANY)
    dma = pltpu.SemaphoreType.DMA
    blocks = (count_tables, devices, each, half)
    return pl.pallas_call(
        functools.partial(gather_kernel, devices),
        in_specs=[vmem, any_space, vmem, vmem, vmem] + [any_space] * len(weights),
        out_specs=[vmem, vmem] + [any_space] * len(weights),
        out_shape=[
            jax.ShapeDtypeStruct((L, 2 * half), bf16),
            jax.ShapeDtypeStruct(requests.shape, jnp.int32),
            *[jax.ShapeDtypeStruct(weight.shape, weight.dtype) for weight in weights],
        ],
        scratch_shapes=[
            pltpu.VMEM(tables.shape, bf16),
            pltpu.VMEM(blocks, bf16),
            pltpu.VMEM(blocks, bf16),
            pltpu.VMEM((devices // 4 * each, half), f32),
            pltpu.VMEM((M * L, half), f32),
            pltpu.VMEM((L, half), bf16),
            pltpu.VMEM((L, half), bf16),
            dma((count_tables,)),
            dma((devices - 1,)),
            dma((devices - 1,)),
            dma((devices * count_tables,)),
            dma((devices * count_tables,)),
            dma((3,)),
            *[dma((len(weights),))] * 2,
        ],
        compiler_params=pltpu.CompilerParams(
            collective_id=1, has_side_effects=True, vmem_limit_bytes=56 * 1024 * 1024
        ),
        cost_estimate=pl.CostEstimate(flops=5 * 10**10, bytes_accessed=4 * 10**8, transcendentals=0),
        name="gather_rows",
    )(requests, tables, slots, ids, table, *weights)


def head_marks(heads, width):
    feature = lax.shift_right_logical(lax.broadcasted_iota(jnp.int32, (heads, width), 1), 6)
    return (feature == lax.broadcasted_iota(jnp.int32, (heads, width), 0)).astype(f32).astype(bf16)


def patch_marks(patch_row_ref, patch_col_ref):
    by_patch = (
        lax.broadcasted_iota(jnp.int32, (P_SIZE, L), 0) == patch_row_ref[...]
    ).astype(f32).astype(bf16)
    by_byte = (
        lax.broadcasted_iota(jnp.int32, (L, P_SIZE), 1) == patch_col_ref[...]
    ).astype(f32).astype(bf16)
    return by_patch, by_byte


def per_head(marks, products):
    high = products.astype(bf16)
    low = (products - high.astype(f32)).astype(bf16)
    return dot_nt(marks, high) + dot_nt(marks, low)


def neighbours(patches, heads):
    wide = jnp.broadcast_to(patches, (heads, L))
    back = [(d, pltpu.roll(wide, d, 1) == wide) for d in (1, 2, 4, 8)]
    ahead = [(L - d, pltpu.roll(wide, L - d, 1) == wide) for d in (1, 2, 4, 8)]
    return back, ahead


def scan_max(values, steps):
    for distance, same in steps:
        values = jnp.where(same, jnp.maximum(values, pltpu.roll(values, distance, 1)), values)
    return values


def scan_sum(values, steps):
    for distance, same in steps:
        values = jnp.where(same, values + pltpu.roll(values, distance, 1), values)
    return values


def patch_attention_kernel(
    patch_row_ref, patch_col_ref, query_ref, key_ref, value_ref, attention_ref, attended_ref
):
    heads, width = attention_ref.shape[0], query_ref.shape[1]
    marks = head_marks(heads, width)
    by_patch, by_byte = patch_marks(patch_row_ref, patch_col_ref)
    queries = dot(by_byte, query_ref[...])
    scores = per_head(marks, queries * key_ref[...].astype(f32)) * 0.125
    back, ahead = neighbours(patch_row_ref[...], heads)
    top = scan_max(scan_max(scores, back), ahead)
    shifted = jnp.exp(scores - top)
    total = scan_sum(shifted, back) + scan_sum(shifted, ahead) - shifted
    attention = shifted / total
    attention_ref[...] = attention
    weights = dot_tn(attention.astype(bf16), marks)
    weighted = (weights * value_ref[...].astype(f32)).astype(bf16)
    attended_ref[...] = dot(by_patch, weighted).astype(bf16)


def patch_attention(patch_row, patch_col, queries, key_value):
    groups = D // GROUP
    return pl.pallas_call(
        patch_attention_kernel,
        grid=(groups,),
        in_specs=[
            pl.BlockSpec((1, L), lambda i: (0, 0)),
            pl.BlockSpec((L, 1), lambda i: (0, 0)),
            pl.BlockSpec((P_SIZE, GROUP), lambda i: (0, i)),
            pl.BlockSpec((L, GROUP), lambda i: (0, i)),
            pl.BlockSpec((L, GROUP), lambda i: (0, i + groups)),
        ],
        out_specs=[
            pl.BlockSpec((HEADS // groups, L), lambda i: (i, 0)),
            pl.BlockSpec((P_SIZE, GROUP), lambda i: (0, i)),
        ],
        out_shape=[
            jax.ShapeDtypeStruct((HEADS, L), f32),
            jax.ShapeDtypeStruct((P_SIZE, D), bf16),
        ],
        compiler_params=params("arbitrary"),
        cost_estimate=pl.CostEstimate(flops=4 * 10**9, bytes_accessed=6 * 10**6, transcendentals=16384),
        name="patch_attention",
    )(patch_row, patch_col, queries, key_value, key_value)


def patch_attention_back_kernel(
    patch_row_ref,
    patch_col_ref,
    query_ref,
    key_ref,
    value_ref,
    attention_ref,
    grad_ref,
    grad_query_ref,
    grad_pair_ref,
):
    heads, width = attention_ref.shape[0], query_ref.shape[1]
    first = pl.multiple_of(pl.program_id(0) * width, width)
    marks = head_marks(heads, width)
    by_patch, by_byte = patch_marks(patch_row_ref, patch_col_ref)
    grads = dot(by_byte, grad_ref[...])
    attention = attention_ref[...]
    grad_attention = per_head(marks, grads * value_ref[...].astype(f32))
    weights = dot_tn(attention.astype(bf16), marks)
    grad_pair_ref[:, pl.ds(D + first, width)] = (weights * grads).astype(bf16)
    back, ahead = neighbours(patch_row_ref[...], heads)
    terms = attention * grad_attention
    total = scan_sum(terms, back) + scan_sum(terms, ahead) - terms
    grad_scores = (attention * (grad_attention - total)).astype(bf16)
    spread_scores = dot_tn(grad_scores, marks) * 0.125
    grad_pair_ref[:, pl.ds(first, width)] = (spread_scores * dot(by_byte, query_ref[...])).astype(bf16)
    weighted = (spread_scores * key_ref[...].astype(f32)).astype(bf16)
    grad_query_ref[...] = dot(by_patch, weighted).astype(bf16)


def patch_attention_back(patch_row, patch_col, queries, key_value, attention, grad_attended):
    groups = D // GROUP
    byte_block = pl.BlockSpec((L, GROUP), lambda i: (0, i))
    patch_block = pl.BlockSpec((P_SIZE, GROUP), lambda i: (0, i))
    return pl.pallas_call(
        patch_attention_back_kernel,
        grid=(groups,),
        in_specs=[
            pl.BlockSpec((1, L), lambda i: (0, 0)),
            pl.BlockSpec((L, 1), lambda i: (0, 0)),
            patch_block,
            byte_block,
            pl.BlockSpec((L, GROUP), lambda i: (0, i + groups)),
            pl.BlockSpec((HEADS // groups, L), lambda i: (i, 0)),
            patch_block,
        ],
        out_specs=[patch_block, pl.BlockSpec((L, 2 * D), lambda i: (0, 0))],
        out_shape=[
            jax.ShapeDtypeStruct((P_SIZE, D), bf16),
            jax.ShapeDtypeStruct((L, 2 * D), bf16),
        ],
        compiler_params=params("arbitrary"),
        cost_estimate=pl.CostEstimate(flops=6 * 10**9, bytes_accessed=10 * 10**6, transcendentals=0),
        name="patch_attention_back",
    )(patch_row, patch_col, queries, key_value, key_value, attention, grad_attended)


def causal_softmax(queries, keys):
    scores = dot_nt(queries, keys) * 0.125
    size = scores.shape[0]
    allowed = lax.broadcasted_iota(jnp.int32, (size, size), 0) >= lax.broadcasted_iota(
        jnp.int32, (size, size), 1
    )
    scores = jnp.where(allowed, scores, -jnp.inf)
    shifted = jnp.exp(scores - jnp.max(scores, axis=-1, keepdims=True))
    return shifted / jnp.sum(shifted, axis=-1, keepdims=True)


def pair_masks(shape):
    lane = lax.broadcasted_iota(jnp.int32, shape, 1)
    return [lane < HEAD, lane >= HEAD]


def causal_kernel(query_ref, key_ref, value_ref, out_ref):
    queries, keys, values = query_ref[...], key_ref[...], value_ref[...]
    masks = pair_masks(queries.shape)
    parts = []
    for mask in masks:
        attention = causal_softmax(jnp.where(mask, queries, 0), keys).astype(bf16)
        parts.append(dot(attention, values))
    out_ref[...] = jnp.where(masks[0], parts[0], parts[1]).astype(bf16)


def causal_attention(mixed):
    pairs = HEADS // 2
    return pl.pallas_call(
        causal_kernel,
        grid=(pairs,),
        in_specs=[
            pl.BlockSpec((P_SIZE, 2 * HEAD), lambda i: (0, i)),
            pl.BlockSpec((P_SIZE, 2 * HEAD), lambda i: (0, i + pairs)),
            pl.BlockSpec((P_SIZE, 2 * HEAD), lambda i: (0, i + 2 * pairs)),
        ],
        out_specs=pl.BlockSpec((P_SIZE, 2 * HEAD), lambda i: (0, i)),
        out_shape=jax.ShapeDtypeStruct((P_SIZE, D), bf16),
        compiler_params=params("arbitrary"),
        cost_estimate=pl.CostEstimate(flops=2 * 10**9, bytes_accessed=2 * 10**6, transcendentals=10**6),
        name="causal_attention",
    )(mixed, mixed, mixed)


def causal_back_kernel(query_ref, key_ref, value_ref, grad_ref, out_ref):
    pair = pl.program_id(0) * 2 * HEAD
    queries, keys, values, grads = query_ref[...], key_ref[...], value_ref[...], grad_ref[...]
    masks = pair_masks(queries.shape)
    results = []
    for mask in masks:
        attention = causal_softmax(jnp.where(mask, queries, 0), keys)
        grad_attention = dot_nt(jnp.where(mask, grads, 0), values)
        total = jnp.sum(attention * grad_attention, axis=-1, keepdims=True)
        grad_scores = (attention * (grad_attention - total)).astype(bf16)
        results.append(
            (
                dot(grad_scores, keys) * 0.125,
                dot_tn(grad_scores, queries) * 0.125,
                dot_tn(attention.astype(bf16), grads),
            )
        )
    for index, (first, second) in enumerate(zip(results[0], results[1])):
        columns = pl.ds(pl.multiple_of(index * D + pair, 2 * HEAD), 2 * HEAD)
        out_ref[:, columns] = jnp.where(masks[0], first, second).astype(bf16)


def causal_attention_back(mixed, grad_attended):
    pairs = HEADS // 2
    block = pl.BlockSpec((P_SIZE, 2 * HEAD), lambda i: (0, i))
    return pl.pallas_call(
        causal_back_kernel,
        grid=(pairs,),
        in_specs=[
            block,
            pl.BlockSpec((P_SIZE, 2 * HEAD), lambda i: (0, i + pairs)),
            pl.BlockSpec((P_SIZE, 2 * HEAD), lambda i: (0, i + 2 * pairs)),
            block,
        ],
        out_specs=pl.BlockSpec((P_SIZE, 3 * D), lambda i: (0, 0)),
        out_shape=jax.ShapeDtypeStruct((P_SIZE, 3 * D), bf16),
        compiler_params=params("arbitrary"),
        cost_estimate=pl.CostEstimate(flops=4 * 10**9, bytes_accessed=4 * 10**6, transcendentals=10**6),
        name="causal_attention_back",
    )(mixed, mixed, mixed, grad_attended)


def normalize(inputs, gain):
    inverse = lax.rsqrt(jnp.mean(inputs * inputs, axis=-1, keepdims=True) + epsilon)
    return (inputs * inverse * gain).astype(bf16), inverse


def normalize_back(inputs, gain, inverse, grad_normed):
    scaled = inputs * inverse
    grad_gain = jnp.sum(grad_normed * scaled, axis=0)
    grad_scaled = grad_normed * gain
    grad_inputs = inverse * (
        grad_scaled - scaled * jnp.mean(grad_scaled * scaled, axis=-1, keepdims=True)
    )
    return grad_inputs, grad_gain


def feed_kernel(
    hidden_ref, gain_ref, w_gate_ref, w_up_ref, w_down_ref, out_ref, normed_ref, gate_ref, up_ref, inner_ref
):
    @pl.when(pl.program_id(0) == 0)
    def _():
        hidden = hidden_ref[...]
        normed_ref[...] = normalize(hidden, gain_ref[...])[0]
        out_ref[...] = hidden

    gate, up = dot(normed_ref[...], w_gate_ref[...]), dot(normed_ref[...], w_up_ref[...])
    inner = (gate * jax.nn.sigmoid(gate) * up).astype(bf16)
    gate_ref[...] = gate.astype(bf16)
    up_ref[...] = up.astype(bf16)
    inner_ref[...] = inner
    out_ref[...] += dot(inner, w_down_ref[...])


def feed_specs():
    tile = FF // 2
    tiles = FF // tile
    whole = pl.BlockSpec((P_SIZE, D), lambda j: (0, 0))
    row = pl.BlockSpec((1, D), lambda j: (0, 0))
    gate = pl.BlockSpec((D, tile), lambda j: (0, j))
    up = pl.BlockSpec((D, tile), lambda j: (0, j + tiles))
    down = pl.BlockSpec((tile, D), lambda j: (j, 0))
    part = pl.BlockSpec((P_SIZE, tile), lambda j: (0, j))
    return tiles, whole, row, gate, up, down, part


def feed_forward(hidden, gain, w_gate_up, w_down):
    tiles, whole, row, gate, up, down, part = feed_specs()
    narrow = jax.ShapeDtypeStruct((P_SIZE, FF), bf16)
    out, normed, gates, ups, inner = pl.pallas_call(
        feed_kernel,
        grid=(tiles,),
        in_specs=[whole, row, gate, up, down],
        out_specs=[whole, whole, part, part, part],
        out_shape=[
            jax.ShapeDtypeStruct((P_SIZE, D), f32),
            jax.ShapeDtypeStruct((P_SIZE, D), bf16),
            narrow,
            narrow,
            narrow,
        ],
        compiler_params=params("arbitrary"),
        cost_estimate=pl.CostEstimate(flops=6 * P_SIZE * D * FF, bytes_accessed=24 * 10**6, transcendentals=P_SIZE * FF),
        name="feed_forward",
    )(hidden, gain[None, :], w_gate_up, w_gate_up, w_down)
    return out, (normed, gates, ups, inner)


def feed_back_kernel(
    grad_ref,
    hidden_ref,
    gain_ref,
    gate_ref,
    up_ref,
    w_gate_ref,
    w_up_ref,
    w_down_ref,
    out_ref,
    low_ref,
    branch_ref,
    joined_ref,
    grad_gain_ref,
    total_ref,
):
    step = pl.program_id(0)
    tile = gate_ref.shape[1]

    @pl.when(step == 0)
    def _():
        branch_ref[...] = grad_ref[...].astype(bf16)
        total_ref[...] = jnp.zeros_like(total_ref)

    grad_inner = dot_nt(branch_ref[...], w_down_ref[...])
    gate, up = gate_ref[...].astype(f32), up_ref[...].astype(f32)
    sigmoid = jax.nn.sigmoid(gate)
    grad_gate = (grad_inner * up * sigmoid * (1.0 + gate * (1.0 - sigmoid))).astype(bf16)
    grad_up = (grad_inner * gate * sigmoid).astype(bf16)
    joined_ref[:, pl.ds(pl.multiple_of(step * tile, 128), tile)] = grad_gate
    joined_ref[:, pl.ds(pl.multiple_of(FF + step * tile, 128), tile)] = grad_up
    total_ref[...] += dot_nt(grad_gate, w_gate_ref[...]) + dot_nt(grad_up, w_up_ref[...])

    @pl.when(step == pl.num_programs(0) - 1)
    def _():
        hidden = hidden_ref[...]
        inverse = lax.rsqrt(jnp.mean(hidden * hidden, axis=-1, keepdims=True) + epsilon)
        grad_in, grad_gain = normalize_back(hidden, gain_ref[...], inverse, total_ref[...])
        result = grad_ref[...] + grad_in
        out_ref[...] = result
        low_ref[...] = result.astype(bf16)
        grad_gain_ref[...] = grad_gain[None, :]


def feed_back(hidden, gain, w_gate_up, w_down, kept, grad_out):
    normed, gates, ups, inner = kept
    tiles, whole, row, gate, up, down, part = feed_specs()
    out, low, branch, joined, grad_gain = pl.pallas_call(
        feed_back_kernel,
        grid=(tiles,),
        in_specs=[whole, whole, row, part, part, gate, up, down],
        out_specs=[whole, whole, whole, pl.BlockSpec((P_SIZE, 2 * FF), lambda j: (0, 0)), row],
        out_shape=[
            jax.ShapeDtypeStruct((P_SIZE, D), f32),
            jax.ShapeDtypeStruct((P_SIZE, D), bf16),
            jax.ShapeDtypeStruct((P_SIZE, D), bf16),
            jax.ShapeDtypeStruct((P_SIZE, 2 * FF), bf16),
            jax.ShapeDtypeStruct((1, D), f32),
        ],
        scratch_shapes=[pltpu.VMEM((P_SIZE, D), f32)],
        compiler_params=params("arbitrary"),
        cost_estimate=pl.CostEstimate(flops=6 * P_SIZE * D * FF, bytes_accessed=24 * 10**6, transcendentals=P_SIZE * FF),
        name="feed_back",
    )(grad_out, hidden, gain[None, :], gates, ups, w_gate_up, w_gate_up, w_down)
    return out, low, grad_gain[0], joined, branch


def byte_grad_kernel(patch_col_ref, grad_ref, keys_ref, values_ref, w_key_ref, w_value_ref, out_ref):
    tile = out_ref.shape[0]
    owner = lax.broadcasted_iota(jnp.int32, (tile, P_SIZE), 1)
    member = (owner == patch_col_ref[...]).astype(f32).astype(bf16)
    total = dot(member, grad_ref[...]) + dot_nt(keys_ref[...], w_key_ref[...])
    out_ref[...] = (total + dot_nt(values_ref[...], w_value_ref[...])).astype(bf16)


def byte_grads(patch_col, grad_patches, grad_pairs, w_qkv):
    tile = 256
    part = lambda column: pl.BlockSpec((tile, D), lambda i: (i, column))
    weight = lambda column: pl.BlockSpec((D, D), lambda i: (0, column))
    return pl.pallas_call(
        byte_grad_kernel,
        grid=(L // tile,),
        in_specs=[
            pl.BlockSpec((tile, 1), lambda i: (i, 0)),
            pl.BlockSpec((P_SIZE, D), lambda i: (0, 0)),
            part(0),
            part(1),
            weight(1),
            weight(2),
        ],
        out_specs=pl.BlockSpec((tile, D), lambda i: (i, 0)),
        out_shape=jax.ShapeDtypeStruct((L, D), bf16),
        compiler_params=params("arbitrary"),
        cost_estimate=pl.CostEstimate(flops=5 * L * D * D, bytes_accessed=11 * 10**6, transcendentals=0),
        name="byte_grads",
    )(patch_col, grad_patches, grad_pairs, grad_pairs, w_qkv, w_qkv)


def chip_bits(devices):
    bits = devices.bit_length() - 1
    first = tuple(reversed(range(bits)))
    return bits, {"A": first, "B": (first[1], first[0]) + first[2:], "C": first[2:4] + first[:2] + first[4:]}


def at_place(ref, axis, place):
    return ref.at[(slice(None),) * axis + (place,)]


def plan_pieces():
    ff, half = FF // 2, D // 2
    pieces = []
    for layer in (1, 0):
        pieces += [
            (layer, "A", [("gate_up", 0, ff)]),
            (layer, "A", [("gate_up", ff, ff)]),
            (layer, "B", [("down", 0, ff)]),
            (layer, "B", [("query", 0, half), ("key", 0, half)]),
            (layer, "C", [("value", 0, half), ("out", 0, half)]),
        ]
    return pieces


def backward_kernel(devices, table_rows, count_tables, *refs):
    bits, orders = chip_bits(devices)
    half, ff = D // 2, FF // 2
    rows = D // devices
    table_block = table_block_rows(devices, table_rows)
    plan = plan_pieces()
    extra = len(plan)
    pieces = extra + 1
    names = [piece[1] for piece in plan] + ["C"]
    widths = [sum(width for _, _, width in piece[2]) for piece in plan] + [half]

    layers, refs = {1: refs[:8], 0: refs[8:16]}, refs[16:]
    bytes_ref, pairs_ref, grad_ref, slots_ref, places_ref, ids_ref, gains_ref = refs[:7]
    sums_ref, theirs_ref, gathered_ref, sorted_ref, arrived_ref, staged_ref = refs[7:13]
    refs = refs[13:]
    landed, refs = {1: refs[:8], 0: refs[8:16]}, refs[16:]
    bytes_landed, pairs_landed, refs = refs[0], refs[1], refs[2:]
    owns, refs = refs[:pieces], refs[pieces:]
    lands, refs = [refs[bits * i : bits * i + bits] for i in range(pieces)], refs[bits * pieces :]
    left_ref, right_ref, total_ref, send_ref, extra_ref, own_ref, table_ref, tile_ref, block_ref = refs[:9]
    swap_send, swap_land, load_sems, grad_sems, table_sem, tile_sems, block_sems, refs = *refs[9:16], refs[16:]
    send_sems, land_sems, trade_send, trade_land, spread_send, spread_land, last_sems = refs

    me = lax.axis_index("rows")
    section = lax.axis_index("section")
    partner = 1 - section
    places = [(me // 2 ** (bits - 1 - d)) % 2 for d in range(bits)]
    peers = [me + (1 - 2 * places[d]) * 2 ** (bits - 1 - d) for d in range(bits)]

    def other(step):
        return lax.rem(me + step, devices)

    barrier = pltpu.get_barrier_semaphore()
    mesh_id = pl.DeviceIdType.MESH
    pl.semaphore_signal(barrier, inc=1, device_id={"section": partner}, device_id_type=mesh_id)
    for step in range(1, devices):
        pl.semaphore_signal(barrier, inc=1, device_id={"rows": other(step)}, device_id_type=mesh_id)
    pl.semaphore_wait(barrier, devices)

    def remote(source, target, send, land, **device):
        return pltpu.make_async_remote_copy(
            src_ref=source, dst_ref=target, send_sem=send, recv_sem=land, device_id=device, device_id_type=mesh_id
        )

    def part_of(array, index, core):
        size = array.shape[1]
        if size == 3 * D:
            first = index * D + core * half
        elif size == 2 * D:
            first = index * D + core * half
        else:
            first = core * (size // 2)
            return array.at[:, pl.ds(pl.multiple_of(first, 128), size // 2)]
        return array.at[:, pl.ds(pl.multiple_of(first, 128), half)]

    swaps = {}

    def swap_of(key, source, target):
        slot = len(swaps)
        swaps[key] = remote(source, target, swap_send.at[slot], swap_land.at[slot], section=partner)
        swaps[key].start()

    def swap_layer(layer, which):
        for index in which:
            array, target = layers[layer][index], landed[layer][index]
            if index < 4:
                swap_of((layer, index, 0), array, target)
            else:
                wide = array.shape[1] // D if index == 4 else 1
                for part in range(wide):
                    there = target.at[:, pl.ds(part * half, half)] if index == 4 else target
                    swap_of((layer, index, part), part_of(array, part, partner), there)

    ready = set()

    def settled(key):
        if key not in ready:
            ready.add(key)
            swaps[key].wait_recv()

    swap_layer(1, (2, 6, 3, 7))
    own_rows = own_ref.at[pl.ds(pl.multiple_of(section * L, L), L)]
    swap_of(("grads",), grad_ref.at[:, pl.ds(pl.multiple_of(partner * half, half), half)], own_rows)
    own_copy = pltpu.make_async_copy(
        grad_ref.at[:, pl.ds(pl.multiple_of(section * half, half), half)], own_rows, grad_sems
    )
    own_copy.start()
    swap_layer(1, (0, 1, 4, 5))
    swap_layer(0, (2, 6, 3, 7, 0, 1, 4, 5))
    swap_of(("bytes",), bytes_ref, bytes_landed)
    for part in range(2):
        swap_of(
            ("pairs", part), part_of(pairs_ref, part, partner), pairs_landed.at[:, pl.ds(part * half, half)]
        )

    def jobs_of(piece):
        layer, _, segments = plan[piece]
        own, land = layers[layer], landed[layer]
        result, column = [], 0
        for kind, first, width in segments:
            if layer == 0 and kind in ("key", "value"):
                part = 0 if kind == "key" else 1
                for chunk in range(4):
                    depth = pl.ds(chunk % 2 * 512, 512)
                    if chunk < 2:
                        left, right = bytes_ref, part_of(pairs_ref, part, section)
                        keys = []
                    else:
                        left, right = bytes_landed, pairs_landed.at[:, pl.ds(part * half, half)]
                        keys = [("bytes",), ("pairs", part)]
                    copies = [("left", left.at[depth], 0, 512), ("right", right.at[depth], 0, 512)]
                    result.append((piece, column, width, chunk, 4, keys, copies))
            else:
                index, other_index, part = {
                    "gate_up": (2, 6, 0),
                    "down": (3, 7, 0),
                    "query": (0, 4, 0),
                    "key": (0, 4, 1),
                    "value": (0, 4, 2),
                    "out": (1, 5, 0),
                }[kind]
                if other_index == 4:
                    right = part_of(own[4], part, section)
                    right_landed = land[4].at[:, pl.ds(part * half, half)]
                elif kind == "gate_up":
                    start = pl.multiple_of(section * FF + first, 128)
                    right = own[6].at[:, pl.ds(start, width)]
                    right_landed = land[6].at[:, pl.ds(first, width)]
                else:
                    right, right_landed = part_of(own[other_index], 0, section), land[other_index]
                copies = [
                    ("left", own[index], 0, P_SIZE),
                    ("left", land[index], P_SIZE, P_SIZE),
                    ("right", right, 0, P_SIZE),
                    ("right", right_landed, P_SIZE, P_SIZE),
                ]
                keys = [(layer, index, 0), (layer, other_index, part)]
                result.append((piece, column, width, 0, 1, keys, copies))
            column += width
        return result

    groups = [[i for i in range(pieces) if names[i] == name] for name in "ABC"]
    order_made = []
    for rank in range(max(len(group) for group in groups)):
        order_made += [group[rank] for group in groups if rank < len(group)]
    jobs = [job for piece in order_made if piece != extra for job in jobs_of(piece)]

    def loads(number):
        piece, column, width, chunk, chunks, keys, copies = jobs[number]
        slot = number % 2
        result = []
        for index, (side, source, first, count) in enumerate(copies):
            buffer = left_ref if side == "left" else right_ref
            columns = D if side == "left" else width
            target = buffer.at[slot, pl.ds(first, count), pl.ds(0, columns)]
            result.append(pltpu.make_async_copy(source, target, load_sems.at[slot, index]))
        return result

    def start_loads(number):
        if number < len(jobs):
            for key in jobs[number][5]:
                settled(key)
            for copy in loads(number):
                copy.start()

    slots_of = {piece: index % send_ref.shape[0] for index, piece in enumerate(order_made) if piece != extra}

    def sent_part(piece):
        if piece == extra:
            return extra_ref
        return send_ref.at[slots_of[piece]].at[(slice(None),) * bits + (pl.ds(0, widths[piece]),)]

    def store(piece, device, value, column, width):
        axis = orders[names[piece]][0]
        at = [(device // 2 ** (bits - 1 - d)) % 2 for d in range(bits)]
        bit = at.pop(axis)
        at = tuple(at) + (slice(None), pl.ds(column, width))
        target = sent_part(piece)

        @pl.when(bit == places[axis])
        def _():
            owns[piece][at] = value

        @pl.when(bit != places[axis])
        def _():
            target[at] = value

    def run_job(number):
        piece, column, width, chunk, chunks, keys, copies = jobs[number]
        slot = number % 2
        for copy in loads(number):
            copy.wait()
        start_loads(number + 1)
        tile = 128

        def body(index, carry):
            at = pl.ds(pl.multiple_of(index * tile, tile), tile)
            value = dot_tn(left_ref[slot, :, at], right_ref[slot, :, pl.ds(0, width)])
            if chunk > 0:
                value = value + total_ref[at, :]
            if chunk < chunks - 1:
                total_ref[at, :] = value
            else:
                for part in range(tile // rows):
                    block = value[part * rows : (part + 1) * rows].astype(bf16)
                    store(piece, index * (tile // rows) + part, block, column, width)
            return carry

        lax.fori_loop(0, D // tile, body, 0)

    def left_of(piece, phase):
        order = orders[names[piece]]
        return [d for d in range(bits) if d not in order[:phase]]

    def kept(piece, phase):
        order = orders[names[piece]]
        ref = owns[piece]
        for step in range(1, phase):
            ref = at_place(ref, left_of(piece, step).index(order[step]), places[order[step]])
        return ref

    def send(piece, phase):
        axis = orders[names[piece]][phase]
        if phase == 0:
            source = sent_part(piece)
        else:
            source = at_place(kept(piece, phase), left_of(piece, phase).index(axis), 1 - places[axis])
        slot = piece * bits + phase
        return remote(source, lands[piece][phase], send_sems.at[slot], land_sems.at[slot], rows=peers[axis])

    made = [0, 0]
    sent = set()

    def make(piece):
        if piece == extra:
            make_extra()
        else:
            index = order_made.index(piece)
            count = send_ref.shape[0]
            earlier = [p for p in order_made[:index] if p != extra and slots_of[p] == slots_of[piece]]
            if earlier and (earlier[-1], 0) not in sent:
                sent.add((earlier[-1], 0))
                send(earlier[-1], 0).wait_send()
            while made[0] < len(jobs) and jobs[made[0]][0] == piece:
                run_job(made[0])
                made[0] += 1
        send(piece, 0).start()

    def make_extra():
        tile = table_block
        first_gain = table_rows // 16 * 16
        positions = M * L

        def body(index, carry):
            words = index * tile + lax.broadcasted_iota(jnp.int32, (tile, positions), 0)
            chosen = (words == ids_ref[...]).astype(f32).astype(bf16)
            value = dot(chosen, own_ref[...])
            row = index * tile + lax.broadcasted_iota(jnp.int32, (tile, half), 0)
            gains = jnp.concatenate([gains_ref[...]] * (tile // 16), axis=0)
            inside = (row >= first_gain) & (row < first_gain + 16)
            value = value + jnp.where(inside, gains, 0.0)
            store(extra, index, value.astype(bf16), 0, half)
            return carry

        lax.fori_loop(0, devices, body, 0)

    def add(piece, phase):
        target = kept(piece, phase + 1)
        land = lands[piece][phase]
        leads = len(target.shape) - 2
        count = 16
        groups_in = target.shape[-2] // count

        def body(index, carry):
            at = (pl.ds(pl.multiple_of(index % groups_in * count, count), count), slice(None))
            lead = index // groups_in
            at = tuple((lead // 2 ** (leads - 1 - d)) % 2 for d in range(leads)) + at
            target[at] = (target[at].astype(f32) + land[at].astype(f32)).astype(bf16)
            return carry

        lax.fori_loop(0, 2**leads * groups_in, body, 0)

    block_rows = block_ref.shape[1]
    block_slots = block_ref.shape[0]
    block_steps = [*(FAR_FIRST if devices == 16 else range(1, devices)), 0]

    def block_copy(step):
        target = staged_ref.at[step] if step else arrived_ref.at[me]
        slot = block_steps.index(step) % block_slots
        return pltpu.make_async_copy(block_ref.at[slot], target, block_sems.at[slot])

    def trade(step):
        return remote(
            staged_ref.at[step], arrived_ref.at[me], trade_send.at[step - 1], trade_land.at[step - 1], rows=other(step)
        )

    def trade_landing(step):
        back = lax.rem(me + devices - step, devices)
        return remote(
            staged_ref.at[step], arrived_ref.at[back], trade_send.at[step - 1], trade_land.at[step - 1], rows=back
        )

    own_block = block_copy(0)

    def make_blocks():
        own_copy.wait()
        settled(("grads",))
        steps = block_steps
        behind = block_slots - 1

        def pass_on(step):
            if step:
                block_copy(step).wait()
                trade(step).start()

        for index, step in enumerate(steps):
            if index >= behind:
                pass_on(steps[index - behind])
            each = block_rows // count_tables
            where = lax.broadcasted_iota(jnp.int32, (each, M * L), 1)
            for table in range(count_tables):
                slot = as_column(slots_ref[other(step), table : table + 1, :])
                chosen = (where == slot).astype(f32).astype(bf16)
                part = pl.ds(table * each, each)
                block_ref[index % block_slots, part] = dot(chosen, own_ref[...]).astype(bf16)
            block_copy(step).start()
        for step in steps[devices - behind :]:
            pass_on(step)


    def tile_copy(table, index):
        tile = tile_ref.shape[1]
        return pltpu.make_async_copy(
            tile_ref.at[index % 2],
            sorted_ref.at[table, pl.ds(pl.multiple_of(index * tile, tile), tile)],
            tile_sems.at[index % 2],
        )

    def sort_rows(table):
        if table == 0:
            own_block.wait()
            for step in range(1, devices):
                trade_landing(step).wait_recv()
        each = block_rows // count_tables
        copy = pltpu.make_async_copy(arrived_ref.at[:, pl.ds(table * each, each)], table_ref, table_sem)
        copy.start()
        copy.wait()
        tile = tile_ref.shape[1]
        for index in range(M * L // tile):
            if index >= 2:
                tile_copy(table, index - 2).wait()
            place = lax.broadcasted_iota(jnp.int32, (tile, M * L), 1)
            wanted = as_column(places_ref[table, :, index * tile : (index + 1) * tile])
            chosen = (place == wanted).astype(f32).astype(bf16)
            rows_in = table_ref[...].reshape(M * L, half)
            tile_ref[index % 2] = dot(chosen, rows_in).astype(bf16)
            tile_copy(table, index).start()
        for index in range(M * L // tile - 2, M * L // tile):
            tile_copy(table, index).wait()

    def spreads():
        return [
            remote(
                gathered_ref.at[me],
                gathered_ref.at[me],
                spread_send.at[step - 1],
                spread_land.at[step - 1],
                rows=other(step),
            )
            for step in range(1, devices)
        ]

    def spread_landing(step):
        back = lax.rem(me + devices - step, devices)
        return remote(
            gathered_ref.at[me], gathered_ref.at[back], spread_send.at[step - 1], spread_land.at[step - 1], rows=back
        )

    def finish(piece):
        if piece == extra:
            gathered_ref[me] = kept(piece, bits)[...]
            for copy in spreads():
                copy.start()
        else:
            layer = plan[piece][0]
            first = sum(widths[p] for p in range(piece) if plan[p][0] == layer)
            sums_ref[layer, :, first : first + widths[piece]] = kept(piece, bits)[...]

    start_loads(0)
    for group in groups:
        make(group[0])
    make_blocks()
    for group in groups:
        if len(group) > 1:
            make(group[1])
    rounds = max(len(group) for group in groups)
    for turn in range(rounds + bits - 1):
        for phase in range(bits):
            for group in groups:
                if not 0 <= turn - phase < len(group):
                    continue
                piece = group[turn - phase]
                send(piece, phase).wait_recv()
                if phase == 0 and turn + 2 < len(group):
                    make(group[turn + 2])
                add(piece, phase)
                if phase + 1 < bits:
                    send(piece, phase + 1).start()
                else:
                    finish(piece)
        if 0 <= turn - SORT_TURN < count_tables:
            sort_rows(turn - SORT_TURN)

    last = remote(sums_ref.at[partner], theirs_ref, last_sems.at[0], last_sems.at[1], section=partner)
    last.start()
    for piece in range(pieces):
        for phase in range(bits):
            if (piece, phase) not in sent:
                send(piece, phase).wait_send()
    for key, copy in swaps.items():
        copy.wait_send()
        settled(key)
    for step in range(1, devices):
        trade(step).wait_send()
    for copy in spreads():
        copy.wait_send()
    for step in range(1, devices):
        spread_landing(step).wait_recv()
    last.wait()


def place_kernel(starts_ref, ids_ref, rows_ref, out_ref):
    table, tile = pl.program_id(0), pl.program_id(1)
    height, window, align = out_ref.shape[1], 256, 128
    count = rows_ref.shape[1]
    at = table * (pl.num_programs(1) + 1) + tile
    first = starts_ref[at] // align * align
    places = tile * height + lax.broadcasted_iota(jnp.int32, (height, window), 0)
    lanes = lax.broadcasted_iota(jnp.int32, (height, window), 1)

    def placed(index):
        wanted = first + index * window
        begin = pl.multiple_of(jnp.minimum(wanted, count - window), align)
        part = pl.ds(begin, window)
        chosen = (places == ids_ref[0, :, part]) & (lanes >= wanted - begin)
        return dot(chosen.astype(f32).astype(bf16), rows_ref[0, part, :])

    def body(index, carry):
        out_ref[0] += placed(index)
        return carry

    out_ref[0] = placed(0)
    lax.fori_loop(1, (starts_ref[at + 1] - first + window - 1) // window, body, 0)


def place_rows(ids, rows, shard_rows):
    count_tables, count, width = rows.shape
    height = 1024
    tiles = shard_rows // height
    edges = jnp.arange(tiles + 1, dtype=jnp.int32) * height
    starts = jnp.sum((ids[:, None, :] < edges[None, :, None]).astype(jnp.int32), axis=2).reshape(-1)
    return pl.pallas_call(
        place_kernel,
        grid_spec=pltpu.PrefetchScalarGridSpec(
            num_scalar_prefetch=1,
            grid=(count_tables, tiles),
            in_specs=[
                pl.BlockSpec((1, 1, count), lambda i, j, starts: (i, 0, 0)),
                pl.BlockSpec((1, count, width), lambda i, j, starts: (i, 0, 0)),
            ],
            out_specs=pl.BlockSpec((1, height, width), lambda i, j, starts: (i, j, 0)),
        ),
        out_shape=jax.ShapeDtypeStruct((count_tables, shard_rows, width), f32),
        compiler_params=params("arbitrary", "arbitrary"),
        cost_estimate=pl.CostEstimate(flops=10**10, bytes_accessed=6 * 10**7, transcendentals=0),
        name="place_rows",
    )(starts, ids[:, None, :], rows)


def join_kernel(section_ref, sums_ref, theirs_ref, gate_up_ref, down_ref, qkv_ref, out_ref):
    section = section_ref[0]
    mine, theirs = sums_ref[section].astype(f32), theirs_ref[...].astype(f32)
    lower, upper = jnp.where(section == 0, mine, theirs), jnp.where(section == 0, theirs, mine)
    half, half_ff, rest = D // 2, FF // 2, FF + FF // 2
    for core, part in enumerate((lower, upper)):
        gate_up_ref[:, core * FF : (core + 1) * FF] = part[:, :FF]
        down_ref[:, core * half_ff : (core + 1) * half_ff] = part[:, FF:rest]
        for index in range(3):
            first = index * D + core * half
            qkv_ref[:, first : first + half] = part[:, rest + index * half : rest + (index + 1) * half]
        out_ref[:, core * half : (core + 1) * half] = part[:, rest + 3 * half :]


def join_sums(section, sums, theirs):
    rows = theirs.shape[0]
    vmem = pl.BlockSpec(memory_space=pltpu.VMEM)
    return pl.pallas_call(
        join_kernel,
        in_specs=[pl.BlockSpec(memory_space=pltpu.SMEM), vmem, vmem],
        out_specs=[vmem] * 4,
        out_shape=[jax.ShapeDtypeStruct((rows, width), f32) for width in (2 * FF, FF, 3 * D, D)],
        compiler_params=pltpu.CompilerParams(vmem_limit_bytes=VMEM_BYTES),
        cost_estimate=pl.CostEstimate(flops=10**6, bytes_accessed=8 * 10**6, transcendentals=0),
        name="join_sums",
    )(section.reshape(1).astype(jnp.int32), sums, theirs)


def table_block_rows(devices, table_rows):
    return -(-(table_rows + 12) // (16 * devices)) * 16


def backward_sums(layer_two, layer_one, byte_rows, grad_pairs, grad_bytes, slots, places, ids, gains, table_rows):
    devices = lax.axis_size("rows")
    bits, orders = chip_bits(devices)
    rows = D // devices
    plan = plan_pieces()
    table_block = table_block_rows(devices, table_rows)
    half, ff = D // 2, FF // 2
    count_tables, each = slots.shape[1:]
    block_rows = count_tables * each
    widths = [sum(width for _, _, width in piece[2]) for piece in plan]
    shapes = [(rows, width) for width in widths] + [(table_block, half)]
    owns, lands = [], []
    for shape in shapes:
        owns.append(pltpu.VMEM((2,) * (bits - 1) + shape, bf16))
        lands += [pltpu.VMEM((2,) * (bits - 1 - phase) + shape, bf16) for phase in range(bits)]
    total = sum(widths) // 2
    landed = []
    for layer in (layer_two, layer_one):
        for index, array in enumerate(layer):
            shape = array.shape if index < 4 else (array.shape[0], array.shape[1] // 2)
            landed.append(jax.ShapeDtypeStruct(shape, bf16))
    landed += [
        jax.ShapeDtypeStruct(byte_rows.shape, bf16),
        jax.ShapeDtypeStruct((grad_pairs.shape[0], grad_pairs.shape[1] // 2), bf16),
    ]
    swaps = 2 * 7 + 3 + 1 + 4
    copies = len(shapes) * bits
    any_space = pl.BlockSpec(memory_space=pl.ANY)
    vmem = pl.BlockSpec(memory_space=pltpu.VMEM)
    blocks = jax.ShapeDtypeStruct((devices, block_rows, half), bf16)
    dma = pltpu.SemaphoreType.DMA
    results = pl.pallas_call(
        functools.partial(backward_kernel, devices, table_rows, count_tables),
        in_specs=[any_space] * 19 + [vmem] * 4,
        out_specs=[vmem, any_space, vmem] + [any_space] * (3 + len(landed)),
        out_shape=[
            jax.ShapeDtypeStruct((2, rows, total), bf16),
            jax.ShapeDtypeStruct((rows, total), bf16),
            jax.ShapeDtypeStruct((devices, table_block, half), bf16),
            jax.ShapeDtypeStruct((count_tables, M * L, half), bf16),
            blocks,
            blocks,
            *landed,
        ],
        scratch_shapes=[
            *owns,
            *lands,
            pltpu.VMEM((2, 2 * P_SIZE, D), bf16),
            pltpu.VMEM((2, 2 * P_SIZE, ff), bf16),
            pltpu.VMEM((D, half), f32),
            pltpu.VMEM((4,) + (2,) * (bits - 1) + (rows, ff), bf16),
            pltpu.VMEM((2,) * (bits - 1) + (table_block, half), bf16),
            pltpu.VMEM((M * L, half), bf16),
            pltpu.VMEM((devices, each, half), bf16),
            pltpu.VMEM((2, 256, half), bf16),
            pltpu.VMEM((3, block_rows, half), bf16),
            dma((swaps,)),
            dma((swaps,)),
            dma((2, 4)),
            dma,
            dma,
            dma((2,)),
            dma((3,)),
            dma((copies,)),
            dma((copies,)),
            dma((devices - 1,)),
            dma((devices - 1,)),
            dma((devices - 1,)),
            dma((devices - 1,)),
            dma((2,)),
        ],
        compiler_params=pltpu.CompilerParams(
            collective_id=0, has_side_effects=True, vmem_limit_bytes=60 * 1024 * 1024
        ),
        cost_estimate=pl.CostEstimate(flops=5 * 10**10, bytes_accessed=6 * 10**8, transcendentals=0),
        name="backward_sums",
    )(*layer_two, *layer_one, byte_rows, grad_pairs, grad_bytes, slots, places, ids, gains)
    return results[:4]


def swap(array):
    return lax.ppermute(array, "section", [(0, 1), (1, 0)])


def on_device(
    byte_ids,
    hash_ids,
    patch_lengths,
    row_lengths,
    byte_table,
    hash_tables,
    norm_gains,
    w_qkv,
    w_out,
    w_gate_up,
    w_down,
    cotangent,
):
    section = lax.axis_index("section")
    first_core = section == 0
    devices = lax.axis_size("rows")
    count_tables, shard_rows, half_width = hash_tables.shape
    positions = M * L

    def both(array):
        return lax.all_gather(array, "section", axis=0, tiled=True)

    flat_ids = hash_ids.reshape(positions, count_tables).T
    owners = flat_ids // shard_rows
    order_key = owners * positions + jnp.arange(positions, dtype=jnp.int32)[None, :]
    order_key, grouped = lax.sort((order_key, flat_ids % shard_rows), dimension=1, num_keys=1)

    def by_owner(array):
        return array.reshape(count_tables, devices, -1).transpose(1, 0, 2)

    byte_of_slot = order_key % positions
    numbers = jnp.arange(positions, dtype=jnp.int32)[None, :]
    flat_bytes = byte_ids.reshape(positions)
    table_rows = byte_table.shape[0]
    padded = jnp.pad(byte_table, ((0, -table_rows % 128), (0, 0)))
    slots = by_owner(byte_of_slot)
    weights = [w_qkv[0], w_out[0], w_gate_up[0], w_down[0]]
    byte_rows, requested, *other_weights = gather_rows(
        by_owner(grouped), hash_tables, slots, flat_bytes[:, None], padded, weights
    )
    gains = both(norm_gains).astype(f32)

    lengths = lax.dynamic_index_in_dim(patch_lengths, section, 0, keepdims=False)
    row_length = lax.dynamic_index_in_dim(row_lengths, section, 0, keepdims=False)
    starts = jnp.cumsum(lengths) - lengths
    byte_positions = jnp.arange(L, dtype=jnp.int32)
    byte_patch = jnp.sum((starts[:, None] <= byte_positions[None, :]).astype(jnp.int32), axis=0) - 1
    patch_row, patch_col = byte_patch[None, :], byte_patch[:, None]
    patches = jnp.arange(P_SIZE, dtype=jnp.int32)
    member = (patches[:, None] == patch_row).astype(bf16)
    counts = lengths.astype(f32)[:, None]
    valid = (patches < row_length)[:, None]

    own_cotangent = lax.dynamic_index_in_dim(cotangent[0], section, 0, keepdims=False)
    sent_cotangent = swap(lax.dynamic_index_in_dim(cotangent[0], 1 - section, 0, keepdims=False))
    cotangent_one = jnp.where(first_core, own_cotangent, sent_cotangent).astype(f32)
    cotangent_two = jnp.where(first_core, sent_cotangent, own_cotangent).astype(f32)

    def both_layers(one, two):
        pooled = dot(member, byte_rows) / counts
        normed_one, inverse_one = normalize(pooled, gains[0, 0])
        queries_one = dot(normed_one, one[0][:, :D]).astype(bf16)
        byte_pairs = dot(byte_rows, one[0][:, D:]).astype(bf16)
        attention_one, attended_one = patch_attention(patch_row, patch_col, queries_one, byte_pairs)
        middle_one = pooled + dot(attended_one, one[1])
        result_one, kept_one = feed_forward(middle_one, gains[0, 1], one[2], one[3])
        encoded = jnp.where(valid, result_one, pooled).astype(bf16)

        inputs_two = encoded.astype(f32)
        normed_two, inverse_two = normalize(inputs_two, gains[1, 0])
        mixed = dot(normed_two, two[0]).astype(bf16)
        attended_two = causal_attention(mixed)
        middle_two = inputs_two + dot(attended_two, two[1])
        result_two, kept_two = feed_forward(middle_two, gains[1, 1], two[2], two[3])
        final = jnp.where(valid, result_two, inputs_two).astype(bf16)
        grad_kept = jnp.where(valid, cotangent_two, 0.0)
        grad_middle, grad_low, gain_two_second, grad_joined, grad_branch = feed_back(
            middle_two, gains[1, 1], two[2], two[3], kept_two, grad_kept
        )
        factors_two = [normed_two, attended_two, kept_two[0], grad_branch, None, grad_low, grad_joined, kept_two[3]]
        grad_attended = dot_nt(grad_low, two[1]).astype(bf16)
        grad_mixed = causal_attention_back(mixed, grad_attended)
        grad_normed = dot_nt(grad_mixed, two[0])
        grad_in, gain_two_first = normalize_back(inputs_two, gains[1, 0], inverse_two, grad_normed)
        grad_encoded = jnp.where(valid, 0.0, cotangent_two) + grad_middle + grad_in


        grad_out = cotangent_one + grad_encoded.astype(bf16).astype(f32)
        grad_kept = jnp.where(valid, grad_out, 0.0)
        grad_middle, grad_low, gain_one_second, grad_joined, grad_branch = feed_back(
            middle_one, gains[0, 1], one[2], one[3], kept_one, grad_kept
        )
        factors_one = [normed_one, attended_one, kept_one[0], grad_branch, None, grad_low, grad_joined, kept_one[3]]
        grad_attended = dot_nt(grad_low, one[1]).astype(bf16)
        grad_queries, grad_pairs = patch_attention_back(
            patch_row, patch_col, queries_one, byte_pairs, attention_one, grad_attended
        )
        grad_normed = dot_nt(grad_queries, one[0][:, :D])
        grad_in, gain_one_first = normalize_back(pooled, gains[0, 0], inverse_one, grad_normed)
        grad_pooled = jnp.where(valid, 0.0, grad_out) + grad_middle + grad_in
        grad_bytes = byte_grads(patch_col, (grad_pooled / counts).astype(bf16), grad_pairs, one[0])

        table_ids = requested.transpose(1, 0, 2).reshape(count_tables, -1)
        id_key = lax.sort(table_ids * positions + numbers, dimension=1)
        sorted_ids = id_key // positions
        places = (id_key % positions)[:, None, :]

        factors_two[4], factors_one[4] = grad_mixed, grad_queries
        gain_part = jnp.stack([gain_one_first, gain_one_second, gain_two_first, gain_two_second])
        return encoded, final, factors_two, factors_one, grad_pairs, grad_bytes, gain_part, sorted_ids, places

    results = lax.cond(
        first_core, both_layers, lambda one, two: both_layers(two, one), weights, other_weights
    )
    encoded, final, factors_two, factors_one, grad_pairs, grad_bytes, gain_part, sorted_ids, places = results
    sent_out = swap(jnp.where(first_core, final, encoded))
    kept_out = jnp.where(first_core, encoded, final)
    section_out = jnp.where(
        first_core, jnp.stack([kept_out, sent_out]), jnp.stack([sent_out, kept_out])
    )[None]

    gain_part = jnp.pad(gain_part.reshape(8, half_width), ((8, 0), (0, 0)))
    sums, theirs, gathered, sorted_rows = backward_sums(
        factors_two,
        factors_one,
        byte_rows,
        grad_pairs,
        grad_bytes,
        slots,
        places,
        flat_bytes[None, :],
        gain_part,
        table_rows,
    )
    hash_grad = place_rows(sorted_ids, sorted_rows, shard_rows)
    gathered = gathered.reshape(-1, half_width)
    byte_table_grad = gathered[:table_rows].astype(f32)
    first_gain = table_rows // 16 * 16 + 8
    gain_sums = gathered[first_gain : first_gain + 8].reshape(2, 2, D)
    gain_sums = (gain_sums.astype(f32) + swap(gain_sums).astype(f32)).reshape(2, 2, devices, -1)
    gains_grad = lax.dynamic_index_in_dim(gain_sums, section, 0, keepdims=True)
    gains_grad = lax.dynamic_index_in_dim(gains_grad, lax.axis_index("rows"), 2, keepdims=False)

    gate_up_grad, down_grad, qkv_grad, out_grad = join_sums(section, sums, theirs)
    down_grad = down_grad.T

    return (
        section_out,
        byte_table_grad,
        hash_grad,
        gains_grad,
        qkv_grad[None],
        out_grad[None],
        gate_up_grad[None],
        down_grad[None],
    )


def solution(mesh):
    return jax.shard_map(
        on_device,
        mesh=mesh,
        in_specs=(
            P("rows", None),
            P("rows", None, None),
            P("rows", None),
            P("rows"),
            P(None, "section"),
            P(None, "rows", "section"),
            P("section", None, None),
            P("section", None, None),
            P("section", None, None),
            P("section", None, None),
            P("section", None, None),
            P("section", "rows", None, None),
        ),
        out_specs=(
            P("section", "rows", None, None),
            P(None, "section"),
            P(None, "rows", "section"),
            P("section", None, "rows"),
            P("section", "rows", None),
            P("section", "rows", None),
            P("section", "rows", None),
            P("section", None, "rows"),
        ),
        check_vma=False,
    )
```
